32 devices in a mesh: clip: 16 (over z, y, core), frame: 2 (over x).
Axes of the slice: x: 2, y: 2, z: 4, core: 2. Of those that a mesh axis runs over, the one named last changes fastest.
Arguments:
- tokens: bfloat16 [32, 16, 196, 768], P('clip', 'frame'), may hold values from -6 to 6
- cotangent: bfloat16 [32, 16, 196, 768], P('clip', 'frame'), may hold values from -6 to 6
- space_gain: bfloat16 [768], P(('clip', 'frame')), may hold values from 0.099609375 to 1.8984375
- time_gain: bfloat16 [768], P(('clip', 'frame')), may hold values from 0.099609375 to 1.8984375
- feed_gain: bfloat16 [768], P(('clip', 'frame')), may hold values from 0.099609375 to 1.8984375
- space_proj: bfloat16 [768, 2304], P(('clip', 'frame')), may hold values from -0.21875 to 0.21875
- space_out: bfloat16 [768, 768], P(('clip', 'frame')), may hold values from -0.625 to 0.625
- time_proj: bfloat16 [768, 2304], P(('clip', 'frame')), may hold values from -0.21875 to 0.21875
- time_out: bfloat16 [768, 768], P(('clip', 'frame')), may hold values from -0.4375 to 0.4375
- up_proj: bfloat16 [768, 3072], P(('clip', 'frame')), may hold values from -0.21875 to 0.21875
- down_proj: bfloat16 [3072, 768], P(('clip', 'frame')), may hold values from -0.15625 to 0.15625
Outputs:
- mixed: bfloat16 [32, 16, 196, 768], P('clip', 'frame')
- grad_tokens: float32 [32, 16, 196, 768], P('clip', 'frame')
- grad_space_gain: float32 [768], P(('clip', 'frame'))
- grad_time_gain: float32 [768], P(('clip', 'frame'))
- grad_feed_gain: float32 [768], P(('clip', 'frame'))
- grad_space_proj: float32 [768, 2304], P(('clip', 'frame'))
- grad_space_out: float32 [768, 768], P(('clip', 'frame'))
- grad_time_proj: float32 [768, 2304], P(('clip', 'frame'))
- grad_time_out: float32 [768, 768], P(('clip', 'frame'))
- grad_up_proj: float32 [768, 3072], P(('clip', 'frame'))
- grad_down_proj: float32 [3072, 768], P(('clip', 'frame'))
The draws below stay inside these ranges and needn't reach their ends.
All inputs are finite; a program needn't handle non-finite values.
Results may differ from the reference program's by a relative error of at most 0.024.
Values may be sent and summed in bfloat16 or wider, within the bound.
No kernel may reach another device: no remote copies, remote signals or barrier semaphores. Data moves between devices by JAX's collectives and lax.ppermute only.
A program may use at most 512 MiB of HBM per device.

```python
import jax
import jax.numpy as jnp
from jax import lax

D = 768
HEADS = 12
HEAD = 64
FF = 3072
FRAMES = 16
PLACES = 196
CLIPS = 32


def strengthened(entries, own_key, source, target, blocks, factor):
    owner, partner = [(jnp.arange(entries.shape[axis_at]) // (entries.shape[axis_at] // blocks)).reshape([-1 if axis == axis_at else 1 for axis in range(entries.ndim)]) for axis_at in (source, target)]
    chosen = jax.random.permutation(own_key, blocks)[partner]
    strong = (owner == chosen) | (owner == (partner + blocks // 2) % blocks)
    return jnp.where(strong, factor * entries, entries)


def steps_of(own_key, extent, cuts, low, top_value):
    def one(dim, blocks):
        steps = jax.random.uniform(jax.random.fold_in(jax.random.fold_in(own_key, 6), dim), (blocks,), jnp.float32, low / len(cuts), top_value / len(cuts))
        return jnp.repeat(jnp.exp(steps), extent[dim] // blocks).reshape((-1,) + (1,) * (len(extent) - dim - 1))

    level = one(*cuts[0])
    for cut in cuts[1:]:
        level = level * one(*cut)
    return level


def bell_draw(rng, shape, scale, reach, cuts=(), kind=jnp.bfloat16):
    loudness = steps_of(rng, shape, cuts, -0.22, 0.18) if cuts else 1.0
    entries = jax.random.normal(rng, shape, jnp.float32) * scale * loudness
    return jnp.minimum(jnp.maximum(entries, -reach), reach).astype(kind)


def noise_with(own_key, shape, width, bound, cuts, heavy, dtype=jnp.bfloat16):
    values = width * jax.random.normal(own_key, shape, jnp.float32)
    if cuts:
        values = values * steps_of(own_key, shape, cuts, -0.22, 0.18)
    return jnp.clip(strengthened(values, jax.random.fold_in(own_key, 3), *heavy), -bound, bound).astype(dtype)


def setup_inputs(seed: int = 0) -> dict:
    seeds = jax.random.split(jax.random.key(seed), 12)
    return {
        "tokens": bell_draw(seeds[0], (CLIPS, FRAMES, PLACES, D), 1.0, 6.0, ((0, 16), (1, 2))),
        "cotangent": noise_with(seeds[1], (CLIPS, FRAMES, PLACES, D), 1.0, 6.0, ((0, 16), (1, 2)), (0, 3, 16, 2.0)),
        "space_gain": jnp.clip(1.0 + 0.18 * jax.random.normal(seeds[2], (D,), jnp.float32), 0.099609375, 1.8984375).astype(jnp.bfloat16),
        "time_gain": jnp.clip(1.0 + 0.18 * jax.random.normal(seeds[3], (D,), jnp.float32), 0.099609375, 1.8984375).astype(jnp.bfloat16),
        "feed_gain": jnp.clip(1.0 + 0.18 * jax.random.normal(seeds[4], (D,), jnp.float32), 0.099609375, 1.8984375).astype(jnp.bfloat16),
        "space_proj": bell_draw(seeds[5], (D, 3 * D), D ** -0.5, 0.21875, ((0, 32),)),
        "space_out": bell_draw(seeds[6], (D, D), (D // 8) ** -0.5, 0.625, ((0, 32),)),
        "time_proj": bell_draw(seeds[7], (D, 3 * D), D ** -0.5, 0.21875, ((0, 32),)),
        "time_out": bell_draw(seeds[8], (D, D), (D // 4) ** -0.5, 0.4375, ((0, 32),)),
        "up_proj": bell_draw(seeds[9], (D, FF), D ** -0.5, 0.21875, ((0, 32),)),
        "down_proj": bell_draw(seeds[10], (FF, D), (FF // 2) ** -0.5, 0.15625, ((0, 32),)),
    }


epsilon = 1e-06

@jax.custom_vjp
def low(v):
    return lax.optimization_barrier(v.astype(jnp.bfloat16)).astype(jnp.float32)

@jax.custom_vjp
def low_back(v):
    return v

def low_keep(v):
    return (low(v), None)

def low_pass(kept, grad):
    return (grad,)

def back_keep(v):
    return (v, None)

def back_low(kept, grad):
    return (low(grad),)
low.defvjp(low_keep, low_pass)
low_back.defvjp(back_keep, back_low)

def norm_rows(values, gain):
    centred = values - lax.optimization_barrier(jnp.mean(values, axis=-1, keepdims=True))
    return centred * lax.rsqrt(lax.optimization_barrier(jnp.mean(centred * centred, axis=-1, keepdims=True)) + epsilon) * gain

def attend(queries, key_block, value_block):
    scores = jnp.einsum('blhe,bmhe->bhlm', queries, key_block, precision=lax.Precision.HIGHEST) * HEAD ** (-0.5)
    scores = low_back(scores)
    chances = low(jax.nn.softmax(scores, axis=-1))
    return jnp.einsum('bhlm,bmhe->blhe', chances, value_block, precision=lax.Precision.HIGHEST)

def project(values, matrix):
    return jnp.einsum('fpd,de->fpe', values, matrix, precision=lax.Precision.HIGHEST)

def layer(sample, params):
    space_gain, time_gain, feed_gain, space_proj, space_out, time_proj, time_out, up_proj, down_proj = params
    frames, places, model_width = sample.shape
    in_space = low(norm_rows(sample, space_gain))
    qkv_space = low_back(low(project(in_space, space_proj)))
    parted = qkv_space.reshape(frames, places, 3, HEADS, HEAD)
    attended = attend(parted[:, :, 0], parted[:, :, 1], parted[:, :, 2])
    out_space = low_back(low(attended.reshape(frames, places, model_width)))
    after_space = sample + low_back(project(out_space, space_out))
    in_time = low(norm_rows(after_space, time_gain))
    qkv_time = low_back(low(project(in_time, time_proj)))
    parted = qkv_time.reshape(frames, places, 3, HEADS, HEAD).transpose(1, 0, 2, 3, 4)
    attended = attend(parted[:, :, 0], parted[:, :, 1], parted[:, :, 2])
    out_time = low_back(low(attended.transpose(1, 0, 2, 3).reshape(frames, places, model_width)))
    after_time = after_space + low_back(project(out_time, time_out))
    in_feed = low(norm_rows(after_time, feed_gain))
    hidden = low_back(project(in_feed, up_proj))
    active = low(jax.nn.gelu(hidden))
    return after_time + low_back(project(active, down_proj))

def reference(tokens, cotangent, space_gain, time_gain, feed_gain, space_proj, space_out, time_proj, time_out, up_proj, down_proj):
    params = tuple((item.astype(jnp.float32) for item in (space_gain, time_gain, feed_gain, space_proj, space_out, time_proj, time_out, up_proj, down_proj)))

    def whole(inputs, weights):

        def per_clip(sample):
            return layer(sample, weights)
        return lax.map(jax.checkpoint(per_clip), inputs)
    result, pull = jax.vjp(whole, tokens.astype(jnp.float32), params)
    grad_tokens, grads = pull(cotangent.astype(jnp.float32))
    g_space_gain, g_time_gain, g_feed_gain, g_space_proj, g_space_out, g_time_proj, g_time_out, g_up_proj, g_down_proj = grads
    return (result.astype(jnp.bfloat16), grad_tokens, g_space_gain, g_time_gain, g_feed_gain, g_space_proj, g_space_out, g_time_proj, g_time_out, g_up_proj, g_down_proj)
```

```python
import functools
import math

import jax
import jax.numpy as jnp
from jax import lax
from jax.experimental import pallas as pl
from jax.experimental.pallas import tpu as pltpu
from jax.sharding import PartitionSpec as P

HEADS = 12
HEAD = 64
PAIRS = HEADS // 2
LANES = 2 * HEAD
epsilon = 1e-06
LOW = jnp.bfloat16
WIDE = jnp.float32
NN = (((1,), (0,)), ((), ()))
NT = (((1,), (1,)), ((), ()))
TN = (((0,), (0,)), ((), ()))
SCALE = HEAD ** (-0.5)
POWER = SCALE * math.log2(math.e)
NEVER = -1e30
GROUP = 8
STEP = 2 * GROUP
LIMIT = 60 << 20


def dot(first, second, numbers=NN):
    return lax.dot_general(first, second, numbers, preferred_element_type=WIDE)


def norm_rows(values, gain):
    centred = values - jnp.mean(values, axis=-1, keepdims=True)
    inverse = lax.rsqrt(jnp.mean(centred * centred, axis=-1, keepdims=True) + epsilon)
    normed = centred * inverse
    return normed * gain, normed, inverse


def norm_back(gradient, normed, inverse, gain):
    scaled = gradient * gain
    return inverse * (
        scaled
        - jnp.mean(scaled, axis=-1, keepdims=True)
        - normed * jnp.mean(scaled * normed, axis=-1, keepdims=True)
    )


def fold_rows(values):
    rows, width = values.shape
    return jnp.sum(values.reshape(rows // 8, 8, width), axis=0)


def split_heads(values):
    first = lax.broadcasted_iota(jnp.int32, values.shape, 1) < HEAD
    zero = jnp.zeros_like(values)
    return jnp.where(first, values, zero), jnp.where(first, zero, values)


def join_heads(first, second):
    keep = lax.broadcasted_iota(jnp.int32, first.shape, 1) < HEAD
    return jnp.where(keep, first, second)


def stack_heads(values):
    return jnp.concatenate(split_heads(values), axis=0)


def pair(ref, rows, part, index):
    start = (part * PAIRS + index) * LANES
    return ref[rows, start : start + LANES]


def load_padded(x_ref, pad_ref):
    frames, places, width = x_ref.shape

    @pl.when(pl.program_id(0) == 0)
    def _():
        pad_ref[...] = jnp.zeros_like(pad_ref)

    for frame in range(frames):
        pad_ref[frame, 0:places] = x_ref[frame].astype(WIDE)
    return pad_ref[...].reshape(frames * pad_ref.shape[1], width)


def space_forward_kernel(
    places, x_ref, gain_ref, proj_ref, out_ref, in_ref, qkv_ref, o_ref, after_ref, pad_ref
):
    frames, padded, width = pad_ref.shape
    values = load_padded(x_ref, pad_ref)
    normed = norm_rows(values, gain_ref[...])[0].astype(LOW)
    in_ref[...] = normed.reshape(frames, padded, width)
    qkv_ref[...] = dot(normed, proj_ref[...]).astype(LOW).reshape(frames, padded, 3 * width)
    real = lax.broadcasted_iota(jnp.int32, (padded, padded), 1) < places

    def one_frame(frame, carry):
        for index in range(PAIRS):
            queries = qkv_ref[frame, :, index * LANES : (index + 1) * LANES]
            start = width + index * LANES
            keys = split_heads(qkv_ref[frame, :, start : start + LANES])
            start = 2 * width + index * LANES
            value_block = qkv_ref[frame, :, start : start + LANES]
            outs = []
            for head in range(2):
                scores = jnp.where(real, dot(queries, keys[head], NT), NEVER)
                powers = jnp.exp2((scores - jnp.max(scores, axis=1, keepdims=True)) * POWER)
                chances = powers * (1.0 / jnp.sum(powers, axis=1, keepdims=True))
                outs.append(dot(chances.astype(LOW), value_block))
            o_ref[frame, :, index * LANES : (index + 1) * LANES] = join_heads(*outs).astype(LOW)
        return carry

    lax.fori_loop(0, frames, one_frame, 0)
    after = values + dot(o_ref[...].reshape(frames * padded, width), out_ref[...])
    after = after.reshape(frames, padded // GROUP, GROUP, width)
    for frame in range(frames):
        after_ref[:, frame] = after[frame]


def middle_kernel(
    places,
    ao_ref,
    ar_ref,
    go_ref,
    gr_ref,
    tgain_ref,
    fgain_ref,
    tproj_ref,
    tout_ref,
    up_ref,
    down_ref,
    qkv_ref,
    int_ref,
    ot_ref,
    inf_ref,
    act_ref,
    gh_ref,
    gb_ref,
    mo_ref,
    mr_ref,
    gt_ref,
    gain_ref,
):
    half = ao_ref.shape[1]
    frames = half + ar_ref.shape[1]
    width = ao_ref.shape[3]
    rows = 2 * frames * GROUP
    block = frames * GROUP
    values = jnp.concatenate([ao_ref[...], ar_ref[...]], axis=1).reshape(rows, width)
    in_time = norm_rows(values, tgain_ref[...])[0].astype(LOW)
    int_ref[...] = in_time
    qkv_ref[...] = dot(in_time, tproj_ref[...]).astype(LOW)
    across = lax.broadcasted_iota(jnp.int32, (block, block), 0)
    down = lax.broadcasted_iota(jnp.int32, (block, block), 1)
    bias = jnp.where(((across ^ down) & (GROUP - 1)) == 0, 0.0, NEVER)
    for group in range(2):
        own = slice(group * block, (group + 1) * block)
        for index in range(PAIRS):
            queries = pair(qkv_ref, own, 0, index)
            keys = stack_heads(pair(qkv_ref, own, 1, index))
            value_block = stack_heads(pair(qkv_ref, own, 2, index))
            both = dot(queries, keys, NT)
            chances = []
            for head in range(2):
                scores = both[:, head * block : (head + 1) * block] + bias
                powers = jnp.exp2((scores - jnp.max(scores, axis=1, keepdims=True)) * POWER)
                total = jnp.sum(powers, axis=1, keepdims=True)
                chances.append((powers * (1.0 / total)).astype(LOW))
            result = dot(jnp.concatenate(chances, axis=1), value_block)
            ot_ref[own, index * LANES : (index + 1) * LANES] = result.astype(LOW)
    values = values + dot(ot_ref[...], tout_ref[...])
    feed_gain = fgain_ref[...]
    in_feed, normed, inverse = norm_rows(values, feed_gain)
    in_feed = in_feed.astype(LOW)
    inf_ref[...] = in_feed
    place = pl.program_id(0) * STEP + lax.broadcasted_iota(jnp.int32, (STEP, width), 0)
    lows, highs = [], []
    for ref in (go_ref, gr_ref):
        for frame in range(half):
            tile = jnp.where(place < places, ref[frame].astype(WIDE), 0.0)
            lows.append(tile[:GROUP])
            highs.append(tile[GROUP:])
    gradient = jnp.concatenate(lows + highs, axis=0)
    grad_low = gradient.astype(LOW)
    gb_ref[...] = grad_low
    hidden_width = up_ref.shape[1]
    piece = 512
    root = math.sqrt(2.0 / math.pi)
    for start in range(0, hidden_width, piece):
        cut = slice(start, start + piece)
        hidden = dot(in_feed, up_ref[:, cut])
        back = dot(grad_low, down_ref[cut, :], NT)
        square = hidden * hidden
        slope = jnp.tanh(hidden * (root + (root * 0.044715) * square))
        plus = 0.5 * slope + 0.5
        act_ref[:, cut] = (hidden * plus).astype(LOW)
        inner = hidden * (0.5 * root + (1.5 * root * 0.044715) * square)
        gh_ref[:, cut] = (back * (plus + inner * (1.0 - slope * slope))).astype(LOW)
    mixed = values + dot(act_ref[...], down_ref[...])
    for frame in range(frames):
        low = mixed[frame * GROUP : (frame + 1) * GROUP]
        high = mixed[block + frame * GROUP : block + (frame + 1) * GROUP]
        tile = jnp.concatenate([low, high], axis=0).astype(LOW)
        if frame < half:
            mo_ref[frame] = tile
        else:
            mr_ref[frame - half] = tile
    back = dot(gh_ref[...], up_ref[...], NT)
    gt_ref[...] = gradient + norm_back(back, normed, inverse, feed_gain)

    @pl.when(pl.program_id(0) == 0)
    def _():
        gain_ref[...] = jnp.zeros_like(gain_ref)

    gain_ref[...] += fold_rows(back * normed)


def time_backward_kernel(
    qkv_ref,
    gt_ref,
    ao_ref,
    ar_ref,
    tgain_ref,
    tout_ref,
    tproj_ref,
    gq_ref,
    tb_ref,
    gso_ref,
    gsr_ref,
    gain_ref,
    d_ref,
):
    half = ao_ref.shape[1]
    frames = half + ar_ref.shape[1]
    width = ao_ref.shape[3]
    rows = 2 * frames * GROUP
    block = frames * GROUP
    tb = gt_ref[...].astype(LOW)
    tb_ref[...] = tb
    d_ref[...] = dot(tb, tout_ref[...], NT).astype(LOW)
    across = lax.broadcasted_iota(jnp.int32, (block, block), 0)
    down = lax.broadcasted_iota(jnp.int32, (block, block), 1)
    bias = jnp.where(((across ^ down) & (GROUP - 1)) == 0, 0.0, NEVER)
    for group in range(2):
        own = slice(group * block, (group + 1) * block)
        for index in range(PAIRS):
            queries = pair(qkv_ref, own, 0, index)
            keys = stack_heads(pair(qkv_ref, own, 1, index))
            value_block = stack_heads(pair(qkv_ref, own, 2, index))
            grad = pair(d_ref, own, 0, index)
            both = dot(keys, queries, NT)
            grad_both = dot(value_block, grad, NT)
            chances, grads = [], []
            for head in range(2):
                cut = slice(head * block, (head + 1) * block)
                scores = both[cut] + bias
                powers = jnp.exp2((scores - jnp.max(scores, axis=0, keepdims=True)) * POWER)
                share = powers * (1.0 / jnp.sum(powers, axis=0, keepdims=True))
                grad_share = grad_both[cut]
                mean = jnp.sum(share * grad_share, axis=0, keepdims=True)
                chances.append(share.astype(LOW))
                grads.append((share * (grad_share - mean)).astype(LOW))
            dv = dot(jnp.concatenate(chances, axis=1), stack_heads(grad))
            dk = dot(jnp.concatenate(grads, axis=1), stack_heads(queries)) * SCALE
            dq = dot(jnp.concatenate(grads, axis=0), keys, TN) * SCALE
            for part, item in enumerate((dq, dk, dv)):
                start = (part * PAIRS + index) * LANES
                gq_ref[own, start : start + LANES] = item.astype(LOW)
    values = jnp.concatenate([ao_ref[...], ar_ref[...]], axis=1).reshape(rows, width)
    gain = tgain_ref[...]
    _, normed, inverse = norm_rows(values, gain)
    back = dot(gq_ref[...], tproj_ref[...], NT)
    result = gt_ref[...] + norm_back(back, normed, inverse, gain)
    for frame in range(frames):
        low = result[frame * GROUP : (frame + 1) * GROUP]
        high = result[block + frame * GROUP : block + (frame + 1) * GROUP]
        tile = jnp.concatenate([low, high], axis=0)
        if frame < half:
            gso_ref[frame] = tile
        else:
            gsr_ref[frame - half] = tile

    @pl.when(pl.program_id(0) == 0)
    def _():
        gain_ref[...] = jnp.zeros_like(gain_ref)

    gain_ref[...] += fold_rows(back * normed)


def space_backward_kernel(
    places,
    x_ref,
    gs_ref,
    qkv_ref,
    gain_row_ref,
    out_ref,
    proj_ref,
    gq_ref,
    sb_ref,
    gx_ref,
    gain_ref,
    pad_ref,
    d_ref,
):
    frames, padded, width = pad_ref.shape
    values = load_padded(x_ref, pad_ref)
    grad_space = gs_ref[...].reshape(frames * padded, width)
    sb = grad_space.astype(LOW)
    sb_ref[...] = sb.reshape(frames, padded, width)
    d_ref[...] = dot(sb, out_ref[...], NT).astype(LOW).reshape(frames, padded, width)
    real = lax.broadcasted_iota(jnp.int32, (padded, padded), 0) < places

    def one_frame(frame, carry):
        for index in range(PAIRS):
            queries = qkv_ref[frame, :, index * LANES : (index + 1) * LANES]
            start = width + index * LANES
            key_block = qkv_ref[frame, :, start : start + LANES]
            start = 2 * width + index * LANES
            value_block = qkv_ref[frame, :, start : start + LANES]
            grad = d_ref[frame, :, index * LANES : (index + 1) * LANES]
            keys = split_heads(key_block)
            vals = split_heads(value_block)
            outs = []
            for head in range(2):
                scores = jnp.where(real, dot(keys[head], queries, NT), NEVER)
                powers = jnp.exp2((scores - jnp.max(scores, axis=0, keepdims=True)) * POWER)
                share = powers * (1.0 / jnp.sum(powers, axis=0, keepdims=True))
                grad_share = dot(vals[head], grad, NT)
                mean = jnp.sum(share * grad_share, axis=0, keepdims=True)
                ds = (share * (grad_share - mean)).astype(LOW)
                outs.append(
                    (
                        dot(ds, key_block, TN) * SCALE,
                        dot(ds, queries) * SCALE,
                        dot(share.astype(LOW), grad),
                    )
                )
            for part in range(3):
                start = part * width + index * LANES
                gq_ref[frame, :, start : start + LANES] = join_heads(
                    outs[0][part], outs[1][part]
                ).astype(LOW)
        return carry

    lax.fori_loop(0, frames, one_frame, 0)
    gain = gain_row_ref[...]
    _, normed, inverse = norm_rows(values, gain)
    back = dot(gq_ref[...].reshape(frames * padded, 3 * width), proj_ref[...], NT)
    result = grad_space + norm_back(back, normed, inverse, gain)
    result = result.reshape(frames, padded, width)
    for frame in range(frames):
        gx_ref[frame] = result[frame, 0:places].astype(gx_ref.dtype)

    @pl.when(pl.program_id(0) == 0)
    def _():
        gain_ref[...] = jnp.zeros_like(gain_ref)

    gain_ref[...] += fold_rows(back * normed)


def whole(shape):
    return pl.BlockSpec(
        shape, lambda *_: (0,) * len(shape), pipeline_mode=pl.Buffered(buffer_count=1)
    )


def params():
    return pltpu.CompilerParams(vmem_limit_bytes=LIMIT)


def cost(flops, *arrays):
    size = sum(math.prod(item.shape) * jnp.dtype(item.dtype).itemsize for item in arrays)
    return pl.CostEstimate(flops=int(flops), bytes_accessed=int(size), transcendentals=0)


def padded_places(places):
    return -(-places // STEP) * STEP


def by_frame(count, *tail):
    return pl.BlockSpec((count,) + tail, lambda step: (step,) + (0,) * len(tail))


def space_forward(x, gain, proj, out):
    frames, places, width = x.shape
    padded = padded_places(places)
    groups = padded // GROUP
    rows = frames * padded
    outs = (
        jax.ShapeDtypeStruct((frames, padded, width), LOW),
        jax.ShapeDtypeStruct((frames, padded, 3 * width), LOW),
        jax.ShapeDtypeStruct((frames, padded, width), LOW),
        jax.ShapeDtypeStruct((groups, frames, GROUP, width), WIDE),
    )
    flops = 2 * rows * width * 4 * width + 8 * rows * padded * width
    return pl.pallas_call(
        functools.partial(space_forward_kernel, places),
        grid=(frames // 2,),
        in_specs=[by_frame(2, places, width), whole(gain.shape), whole(proj.shape), whole(out.shape)],
        out_specs=[
            by_frame(2, padded, width),
            by_frame(2, padded, 3 * width),
            by_frame(2, padded, width),
            pl.BlockSpec((groups, 2, GROUP, width), lambda step: (0, step, 0, 0)),
        ],
        out_shape=outs,
        scratch_shapes=[pltpu.VMEM((2, padded, width), WIDE)],
        compiler_params=params(),
        cost_estimate=cost(flops, x, proj, out, *outs),
        name="space_forward",
    )(x, gain, proj, out)


def middle(after_own, after_rest, g_own, g_rest, tgain, fgain, tproj, tout, up, down):
    groups, half, _, width = after_own.shape
    places = g_own.shape[1]
    frames = 2 * half
    rows = groups * frames * GROUP
    block = 2 * frames * GROUP
    hidden = up.shape[1]
    padded = groups * GROUP
    outs = (
        jax.ShapeDtypeStruct((rows, 3 * width), LOW),
        jax.ShapeDtypeStruct((rows, width), LOW),
        jax.ShapeDtypeStruct((rows, width), LOW),
        jax.ShapeDtypeStruct((rows, width), LOW),
        jax.ShapeDtypeStruct((rows, hidden), LOW),
        jax.ShapeDtypeStruct((rows, hidden), LOW),
        jax.ShapeDtypeStruct((rows, width), LOW),
        jax.ShapeDtypeStruct((half, places, width), LOW),
        jax.ShapeDtypeStruct((half, places, width), LOW),
        jax.ShapeDtypeStruct((rows, width), WIDE),
        jax.ShapeDtypeStruct((8, width), WIDE),
    )
    by_row = lambda size: pl.BlockSpec((block, size), lambda step: (step, 0))
    by_group = pl.BlockSpec((2, half, GROUP, width), lambda step: (step, 0, 0, 0))
    by_place = pl.BlockSpec((half, STEP, width), lambda step: (0, step, 0))
    flops = 2 * rows * width * (4 * width + 4 * hidden) + 8 * rows * frames * GROUP * width
    return pl.pallas_call(
        functools.partial(middle_kernel, places),
        grid=(groups // 2,),
        in_specs=[by_group, by_group, by_place, by_place]
        + [whole(item.shape) for item in (tgain, fgain, tproj, tout, up, down)],
        out_specs=[
            by_row(3 * width),
            by_row(width),
            by_row(width),
            by_row(width),
            by_row(hidden),
            by_row(hidden),
            by_row(width),
            by_place,
            by_place,
            by_row(width),
            pl.BlockSpec((8, width), lambda step: (0, 0)),
        ],
        out_shape=outs,
        compiler_params=params(),
        cost_estimate=cost(flops, after_own, after_rest, g_own, g_rest, *outs),
        name="middle",
    )(after_own, after_rest, g_own, g_rest, tgain, fgain, tproj, tout, up, down)


def time_backward(qkv, g_time, after_own, after_rest, tgain, tout, tproj):
    groups, half, _, width = after_own.shape
    frames = 2 * half
    rows = groups * frames * GROUP
    block = 2 * frames * GROUP
    padded = groups * GROUP
    outs = (
        jax.ShapeDtypeStruct((rows, 3 * width), LOW),
        jax.ShapeDtypeStruct((rows, width), LOW),
        jax.ShapeDtypeStruct((half, padded, width), WIDE),
        jax.ShapeDtypeStruct((half, padded, width), WIDE),
        jax.ShapeDtypeStruct((8, width), WIDE),
    )
    by_row = lambda size: pl.BlockSpec((block, size), lambda step: (step, 0))
    by_group = pl.BlockSpec((2, half, GROUP, width), lambda step: (step, 0, 0, 0))
    by_place = pl.BlockSpec((half, STEP, width), lambda step: (0, step, 0))
    flops = 2 * rows * width * 4 * width + 20 * rows * frames * GROUP * width
    return pl.pallas_call(
        time_backward_kernel,
        grid=(groups // 2,),
        in_specs=[by_row(3 * width), by_row(width), by_group, by_group]
        + [whole(item.shape) for item in (tgain, tout, tproj)],
        out_specs=[
            by_row(3 * width),
            by_row(width),
            by_place,
            by_place,
            pl.BlockSpec((8, width), lambda step: (0, 0)),
        ],
        out_shape=outs,
        scratch_shapes=[pltpu.VMEM((block, width), LOW)],
        compiler_params=params(),
        cost_estimate=cost(flops, qkv, g_time, after_own, after_rest, *outs),
        name="time_backward",
    )(qkv, g_time, after_own, after_rest, tgain, tout, tproj)


def space_backward(x, g_space, qkv, gain, out, proj, kind):
    frames, places, width = x.shape
    padded = padded_places(places)
    rows = frames * padded
    outs = (
        jax.ShapeDtypeStruct((frames, padded, 3 * width), LOW),
        jax.ShapeDtypeStruct((frames, padded, width), LOW),
        jax.ShapeDtypeStruct((frames, places, width), kind),
        jax.ShapeDtypeStruct((8, width), WIDE),
    )
    flops = 2 * rows * width * 4 * width + 20 * rows * padded * width
    return pl.pallas_call(
        functools.partial(space_backward_kernel, places),
        grid=(frames // 2,),
        in_specs=[
            by_frame(2, places, width),
            by_frame(2, padded, width),
            by_frame(2, padded, 3 * width),
            whole(gain.shape),
            whole(out.shape),
            whole(proj.shape),
        ],
        out_specs=[
            by_frame(2, padded, 3 * width),
            by_frame(2, padded, width),
            by_frame(2, places, width),
            pl.BlockSpec((8, width), lambda step: (0, 0)),
        ],
        out_shape=outs,
        scratch_shapes=[
            pltpu.VMEM((2, padded, width), WIDE),
            pltpu.VMEM((2, padded, width), LOW),
        ],
        compiler_params=params(),
        cost_estimate=cost(flops, x, g_space, qkv, *outs),
        name="space_backward",
    )(x, g_space, qkv, gain, out, proj)


def weight_gradient(values, gradient):
    rows = math.prod(values.shape[:-1])
    return dot(
        values.reshape(rows, values.shape[-1]), gradient.reshape(rows, gradient.shape[-1]), TN
    ).astype(LOW)


MICRO = 2


def norm_forward(values, gain):
    centred = values - jnp.mean(values, axis=-1, keepdims=True)
    inverse = lax.rsqrt(jnp.mean(centred * centred, axis=-1, keepdims=True) + epsilon)
    normed = centred * inverse
    return (normed * gain, normed, inverse)


def norm_backward(gradient, normed, inverse, gain):
    gain_grad = jnp.sum(gradient * normed, axis=(0, 1, 2))
    scaled = gradient * gain
    centred_grad = (
        scaled
        - jnp.mean(scaled, axis=-1, keepdims=True)
        - normed * jnp.mean(scaled * normed, axis=-1, keepdims=True)
    )
    return (inverse * centred_grad, gain_grad)


def to_places(blocks):
    clip_count, frames, places, model_width = blocks.shape
    return blocks.transpose(0, 2, 1, 3).reshape(clip_count * places, frames, HEADS, HEAD)


def from_places(attended, clip_count, places):
    frames = attended.shape[1]
    return attended.reshape(clip_count, places, frames, HEADS * HEAD).transpose(0, 2, 1, 3)


def attend_forward(queries, key_block, value_block):
    factor = HEAD ** (-0.5)
    scores = (
        jnp.einsum("blhe,bmhe->bhlm", queries, key_block, preferred_element_type=jnp.float32)
        * factor
    )
    highest = jnp.max(scores, axis=-1, keepdims=True)
    powers = jnp.exp(scores - highest)
    row_total = jnp.sum(powers, axis=-1, keepdims=True)
    chances = (powers / row_total).astype(jnp.bfloat16)
    result = jnp.einsum("bhlm,bmhe->blhe", chances, value_block, preferred_element_type=jnp.float32)
    return (result, highest + jnp.log(row_total))


def attend_backward(queries, key_block, value_block, logsum, grad_out):
    factor = HEAD ** (-0.5)
    scores = (
        jnp.einsum("blhe,bmhe->bhlm", queries, key_block, preferred_element_type=jnp.float32)
        * factor
    )
    chances = jnp.exp(scores - logsum)
    grad_chances = jnp.einsum(
        "blhe,bmhe->bhlm", grad_out, value_block, preferred_element_type=jnp.float32
    )
    grad_scores = (
        chances * (grad_chances - jnp.sum(chances * grad_chances, axis=-1, keepdims=True))
    ).astype(jnp.bfloat16)
    grad_queries = (
        jnp.einsum("bhlm,bmhe->blhe", grad_scores, key_block, preferred_element_type=jnp.float32)
        * factor
    )
    grad_keys = (
        jnp.einsum("bhlm,blhe->bmhe", grad_scores, queries, preferred_element_type=jnp.float32)
        * factor
    )
    grad_values = jnp.einsum(
        "bhlm,blhe->bmhe",
        chances.astype(jnp.bfloat16),
        grad_out,
        preferred_element_type=jnp.float32,
    )
    return (grad_queries, grad_keys, grad_values)


def project(values, matrix):
    return jnp.einsum("cfpd,de->cfpe", values, matrix, preferred_element_type=jnp.float32)


def project_back(gradient, matrix):
    return jnp.einsum("cfpe,de->cfpd", gradient, matrix, preferred_element_type=jnp.float32)


def outer_sum(values, gradient):
    return jnp.einsum("cfpd,cfpe->de", values, gradient, preferred_element_type=jnp.float32)


def forward(sample, gathered):
    (
        space_gain,
        time_gain,
        feed_gain,
        space_proj,
        space_out,
        time_proj,
        time_out,
        up_proj,
        down_proj,
    ) = gathered
    clip_count, frames, places, model_width = sample.shape
    normed_space = norm_forward(sample, space_gain.astype(jnp.float32))
    in_space = normed_space[0].astype(jnp.bfloat16)
    qkv_space = project(in_space, space_proj).astype(jnp.bfloat16)
    parted = qkv_space.reshape(clip_count * frames, places, 3, HEADS, HEAD)
    attended, logsum_space = attend_forward(parted[:, :, 0], parted[:, :, 1], parted[:, :, 2])
    out_space = attended.reshape(clip_count, frames, places, model_width).astype(jnp.bfloat16)
    after_space = sample + project(out_space, space_out)
    normed_time = norm_forward(after_space, time_gain.astype(jnp.float32))
    in_time = normed_time[0].astype(jnp.bfloat16)
    qkv_time = project(in_time, time_proj).astype(jnp.bfloat16)
    kv_whole = lax.all_gather(qkv_time[..., model_width:], "frame", axis=1, tiled=True)
    attended, logsum_time = attend_forward(
        to_places(qkv_time[..., :model_width]),
        to_places(kv_whole[..., :model_width]),
        to_places(kv_whole[..., model_width:]),
    )
    out_time = from_places(attended, clip_count, places).astype(jnp.bfloat16)
    after_time = after_space + project(out_time, time_out)
    normed_feed = norm_forward(after_time, feed_gain.astype(jnp.float32))
    in_feed = normed_feed[0].astype(jnp.bfloat16)
    hidden = project(in_feed, up_proj)
    active = jax.nn.gelu(hidden).astype(jnp.bfloat16)
    result = after_time + project(active, down_proj)
    saved = (
        normed_space,
        in_space,
        qkv_space,
        logsum_space,
        out_space,
        normed_time,
        in_time,
        qkv_time,
        kv_whole,
        logsum_time,
        out_time,
        normed_feed,
        in_feed,
        hidden,
        active,
    )
    return (result, saved)


def backward(gradient, saved, gathered):
    (
        space_gain,
        time_gain,
        feed_gain,
        space_proj,
        space_out,
        time_proj,
        time_out,
        up_proj,
        down_proj,
    ) = gathered
    (
        normed_space,
        in_space,
        qkv_space,
        logsum_space,
        out_space,
        normed_time,
        in_time,
        qkv_time,
        time_side,
        logsum_time,
        out_time,
        normed_feed,
        in_feed,
        hidden,
        active,
    ) = saved
    clip_count, frames, places, model_width = gradient.shape
    grad_low = gradient.astype(jnp.bfloat16)
    grad_down = outer_sum(active, grad_low)
    grad_active = project_back(grad_low, down_proj)
    gelu_value, gelu_pull = jax.vjp(jax.nn.gelu, hidden)
    grad_hidden = gelu_pull(grad_active)[0].astype(jnp.bfloat16)
    grad_up = outer_sum(in_feed, grad_hidden)
    back_feed, grad_feed_gain = norm_backward(
        project_back(grad_hidden, up_proj),
        normed_feed[1],
        normed_feed[2],
        feed_gain.astype(jnp.float32),
    )
    grad_time = gradient + back_feed
    time_low = grad_time.astype(jnp.bfloat16)
    grad_tout = outer_sum(out_time, time_low)
    grad_out_time = project_back(time_low, time_out).astype(jnp.bfloat16)
    grad_queries, grad_keys, grad_values = attend_backward(
        to_places(qkv_time[..., :model_width]),
        to_places(time_side[..., :model_width]),
        to_places(time_side[..., model_width:]),
        logsum_time,
        to_places(grad_out_time),
    )
    grad_kv = jnp.concatenate(
        (from_places(grad_keys, clip_count, places), from_places(grad_values, clip_count, places)),
        axis=-1,
    )
    grad_kv_own = lax.psum_scatter(
        grad_kv.astype(jnp.bfloat16), "frame", scatter_dimension=1, tiled=True
    ).astype(jnp.float32)
    grad_qkv_time = jnp.concatenate(
        (from_places(grad_queries, clip_count, places), grad_kv_own), axis=-1
    ).astype(jnp.bfloat16)
    grad_tproj = outer_sum(in_time, grad_qkv_time)
    back_time, grad_time_gain = norm_backward(
        project_back(grad_qkv_time, time_proj),
        normed_time[1],
        normed_time[2],
        time_gain.astype(jnp.float32),
    )
    grad_space = grad_time + back_time
    space_low = grad_space.astype(jnp.bfloat16)
    grad_sout = outer_sum(out_space, space_low)
    grad_out_space = project_back(space_low, space_out).astype(jnp.bfloat16)
    parted = qkv_space.reshape(clip_count * frames, places, 3, HEADS, HEAD)
    grad_queries, grad_keys, grad_values = attend_backward(
        parted[:, :, 0],
        parted[:, :, 1],
        parted[:, :, 2],
        logsum_space,
        grad_out_space.reshape(clip_count * frames, places, HEADS, HEAD),
    )
    grad_qkv_space = (
        jnp.stack((grad_queries, grad_keys, grad_values), axis=2)
        .reshape(clip_count, frames, places, 3 * model_width)
        .astype(jnp.bfloat16)
    )
    grad_sproj = outer_sum(in_space, grad_qkv_space)
    back_space, grad_space_gain = norm_backward(
        project_back(grad_qkv_space, space_proj),
        normed_space[1],
        normed_space[2],
        space_gain.astype(jnp.float32),
    )
    grad_input = grad_space + back_space
    return (
        grad_input,
        (
            grad_space_gain,
            grad_time_gain,
            grad_feed_gain,
            grad_sproj,
            grad_sout,
            grad_tproj,
            grad_tout,
            grad_up,
            grad_down,
        ),
    )


def general(
    tokens,
    cotangent,
    space_gain,
    time_gain,
    feed_gain,
    space_proj,
    space_out,
    time_proj,
    time_out,
    up_proj,
    down_proj,
):
    owned = (
        space_gain,
        time_gain,
        feed_gain,
        space_proj,
        space_out,
        time_proj,
        time_out,
        up_proj,
        down_proj,
    )
    devices_all = lax.axis_size(("clip", "frame"))
    per_micro = tokens.shape[0] // MICRO
    totals = tuple(
        (
            jnp.zeros((piece.shape[0] * devices_all,) + piece.shape[1:], jnp.float32)
            for piece in owned
        )
    )
    gathered = (
        lax.all_gather(space_gain, ("clip", "frame"), axis=0, tiled=True),
        lax.all_gather(time_gain, ("clip", "frame"), axis=0, tiled=True),
        lax.all_gather(feed_gain, ("clip", "frame"), axis=0, tiled=True),
        lax.all_gather(space_proj, ("clip", "frame"), axis=0, tiled=True),
        lax.all_gather(space_out, ("clip", "frame"), axis=0, tiled=True),
        lax.all_gather(time_proj, ("clip", "frame"), axis=0, tiled=True),
        lax.all_gather(time_out, ("clip", "frame"), axis=0, tiled=True),
        lax.all_gather(up_proj, ("clip", "frame"), axis=0, tiled=True),
        lax.all_gather(down_proj, ("clip", "frame"), axis=0, tiled=True),
    )
    mixed_parts = []
    grad_parts = []
    for micro_index in range(MICRO):
        sample = tokens[micro_index * per_micro : (micro_index + 1) * per_micro].astype(jnp.float32)
        result, saved = forward(sample, gathered)
        mixed_parts.append(result.astype(jnp.bfloat16))
        gradient = cotangent[micro_index * per_micro : (micro_index + 1) * per_micro].astype(
            jnp.float32
        )
        grad_input, grads = backward(gradient, saved, gathered)
        grad_parts.append(grad_input)
        totals = tuple((first + second for first, second in zip(totals, grads)))
    flat = tuple((item.reshape(-1) for item in totals))
    owners = (
        lax.psum_scatter(flat[0], ("clip", "frame"), scatter_dimension=0, tiled=True),
        lax.psum_scatter(flat[1], ("clip", "frame"), scatter_dimension=0, tiled=True),
        lax.psum_scatter(flat[2], ("clip", "frame"), scatter_dimension=0, tiled=True),
        lax.psum_scatter(flat[3], ("clip", "frame"), scatter_dimension=0, tiled=True),
        lax.psum_scatter(flat[4], ("clip", "frame"), scatter_dimension=0, tiled=True),
        lax.psum_scatter(flat[5], ("clip", "frame"), scatter_dimension=0, tiled=True),
        lax.psum_scatter(flat[6], ("clip", "frame"), scatter_dimension=0, tiled=True),
        lax.psum_scatter(flat[7], ("clip", "frame"), scatter_dimension=0, tiled=True),
        lax.psum_scatter(flat[8], ("clip", "frame"), scatter_dimension=0, tiled=True),
    )
    shaped = tuple((piece.reshape(mine.shape) for piece, mine in zip(owners, owned)))
    mixed = jnp.concatenate(mixed_parts, axis=0)
    grad_tokens = jnp.concatenate(grad_parts, axis=0)
    return (
        mixed,
        grad_tokens,
        shaped[0],
        shaped[1],
        shaped[2],
        shaped[3],
        shaped[4],
        shaped[5],
        shaped[6],
        shaped[7],
        shaped[8],
    )


def swap_axis(values, axis):
    size = lax.axis_size(axis)
    return lax.ppermute(values, axis, [(index, size - 1 - index) for index in range(size)])


def own_first(mine, other, place):
    return jnp.where(
        place == 0, jnp.stack([mine, other], axis=0), jnp.stack([other, mine], axis=0)
    )


def gain_row(values):
    return values.astype(WIDE).reshape(1, -1)


def clip_local(
    tokens,
    cotangent,
    space_gain,
    time_gain,
    feed_gain,
    space_proj,
    space_out,
    time_proj,
    time_out,
    up_proj,
    down_proj,
):
    axes = ("clip", "frame")
    place = lax.axis_index("frame")
    width = tokens.shape[-1]
    collect = lambda item: lax.all_gather(item, axes, axis=0, tiled=True)

    gains = jnp.stack([space_gain, time_gain, feed_gain], axis=1)
    gains = jnp.pad(gains, ((0, 0), (0, LANES - 3)))
    space = collect(jnp.concatenate([space_proj, space_out, gains], axis=1))
    time = collect(jnp.concatenate([time_proj, time_out], axis=1))
    up = collect(up_proj)
    down = collect(down_proj)
    rest = swap_axis(lax.dynamic_index_in_dim(tokens, 1 - place, 0, keepdims=False), "frame")
    g_rest = swap_axis(lax.dynamic_index_in_dim(cotangent, 1 - place, 0, keepdims=False), "frame")
    own = lax.dynamic_index_in_dim(tokens, place, 0, keepdims=False)
    g_own = lax.dynamic_index_in_dim(cotangent, place, 0, keepdims=False)

    proj_width = 3 * width
    table = space[:, 4 * width : 4 * width + 3].astype(WIDE).T
    sgain, tgain, fgain = (table[index : index + 1] for index in range(3))
    w_sproj, w_sout = space[:, :proj_width], space[:, proj_width : 4 * width]
    w_tproj, w_tout = time[:, :proj_width], time[:, proj_width:]

    in_o, qkv_o, o_o, after_o = space_forward(own, sgain, w_sproj, w_sout)
    in_r, qkv_r, o_r, after_r = space_forward(rest, sgain, w_sproj, w_sout)
    qkv_t, in_t, o_t, in_f, act, gh, gb, mixed_o, mixed_r, g_time, gain_f = middle(
        after_o, after_r, g_own, g_rest, tgain, fgain, w_tproj, w_tout, up, down
    )
    mixed_other = swap_axis(mixed_r, "frame")
    scatter = lambda item: lax.psum_scatter(item, axes, scatter_dimension=0, tiled=True)
    d_down = scatter(weight_gradient(act, gb)).astype(WIDE)
    d_up = scatter(weight_gradient(in_f, gh)).astype(WIDE)
    gq_t, tb, gs_o, gs_r, gain_t = time_backward(
        qkv_t, g_time, after_o, after_r, tgain, w_tout, w_tproj
    )
    d_time = scatter(
        jnp.concatenate([weight_gradient(in_t, gq_t), weight_gradient(o_t, tb)], axis=1)
    ).astype(WIDE)
    gq_r, sb_r, gx_r, gain_sr = space_backward(rest, gs_r, qkv_r, sgain, w_sout, w_sproj, LOW)
    grad_other = swap_axis(gx_r, "frame")
    gq_o, sb_o, gx_o, gain_so = space_backward(own, gs_o, qkv_o, sgain, w_sout, w_sproj, WIDE)
    gain_grads = jnp.stack(
        [jnp.sum(item, axis=0) for item in (gain_so + gain_sr, gain_t, gain_f)], axis=1
    )
    gain_grads = jnp.pad(gain_grads, ((0, 0), (0, LANES - 3))).astype(LOW)
    d_space = scatter(
        jnp.concatenate(
            [
                weight_gradient(
                    jnp.concatenate([in_o, in_r]), jnp.concatenate([gq_o, gq_r])
                ),
                weight_gradient(jnp.concatenate([o_o, o_r]), jnp.concatenate([sb_o, sb_r])),
                gain_grads,
            ],
            axis=1,
        )
    ).astype(WIDE)
    mixed = own_first(mixed_o, mixed_other, place)
    grad_tokens = own_first(gx_o, grad_other.astype(WIDE), place)
    return (
        mixed,
        grad_tokens,
        d_space[:, 4 * width],
        d_space[:, 4 * width + 1],
        d_space[:, 4 * width + 2],
        d_space[:, :proj_width],
        d_space[:, proj_width : 4 * width],
        d_time[:, :proj_width],
        d_time[:, proj_width:],
        d_up,
        d_down,
    )


def shards(tokens, *others):
    frames = lax.axis_size("frame")
    local = frames == 2 and tokens.shape[0] == 2 and tokens.shape[1] == GROUP
    return (clip_local if local else general)(tokens, *others)


def solution(mesh):
    in_specs = (
        P("clip", "frame", None, None),
        P("clip", "frame", None, None),
        P(("clip", "frame")),
        P(("clip", "frame")),
        P(("clip", "frame")),
        P(("clip", "frame"), None),
        P(("clip", "frame"), None),
        P(("clip", "frame"), None),
        P(("clip", "frame"), None),
        P(("clip", "frame"), None),
        P(("clip", "frame"), None),
    )
    out_specs = (
        P("clip", "frame", None, None),
        P("clip", "frame", None, None),
        P(("clip", "frame")),
        P(("clip", "frame")),
        P(("clip", "frame")),
        P(("clip", "frame"), None),
        P(("clip", "frame"), None),
        P(("clip", "frame"), None),
        P(("clip", "frame"), None),
        P(("clip", "frame"), None),
        P(("clip", "frame"), None),
    )
    return jax.shard_map(shards, mesh=mesh, in_specs=in_specs, out_specs=out_specs, check_vma=False)
```

```python
import functools
import math

import jax
import jax.numpy as jnp
from jax import lax
from jax.experimental import pallas as pl
from jax.experimental.pallas import tpu as pltpu
from jax.sharding import PartitionSpec as P

HEADS = 12
HEAD = 64
PAIRS = HEADS // 2
LANES = 2 * HEAD
epsilon = 1e-06
LOW = jnp.bfloat16
WIDE = jnp.float32
NN = (((1,), (0,)), ((), ()))
NT = (((1,), (1,)), ((), ()))
TN = (((0,), (0,)), ((), ()))
SCALE = HEAD ** (-0.5)
POWER = SCALE * math.log2(math.e)
NEVER = -1e30
GROUP = 8
STEP = 2 * GROUP
LIMIT = 60 << 20
SHRINK = 6


def dot(first, second, numbers=NN):
    return lax.dot_general(first, second, numbers, preferred_element_type=WIDE)


def norm_rows(values, gain):
    centred = values - jnp.mean(values, axis=-1, keepdims=True)
    inverse = lax.rsqrt(jnp.mean(centred * centred, axis=-1, keepdims=True) + epsilon)
    normed = centred * inverse
    return normed * gain, normed, inverse


def norm_back(gradient, normed, inverse, gain):
    scaled = gradient * gain
    return inverse * (
        scaled
        - jnp.mean(scaled, axis=-1, keepdims=True)
        - normed * jnp.mean(scaled * normed, axis=-1, keepdims=True)
    )


def fold_rows(values):
    rows, width = values.shape
    return jnp.sum(values.reshape(rows // 8, 8, width), axis=0)


def split_heads(values):
    first = lax.broadcasted_iota(jnp.int32, values.shape, 1) < HEAD
    zero = jnp.zeros_like(values)
    return jnp.where(first, values, zero), jnp.where(first, zero, values)


def join_heads(first, second):
    keep = lax.broadcasted_iota(jnp.int32, first.shape, 1) < HEAD
    return jnp.where(keep, first, second)


def stack_heads(values):
    return jnp.concatenate(split_heads(values), axis=0)


def pair(ref, rows, part, index):
    start = (part * PAIRS + index) * LANES
    return ref[rows, start : start + LANES]


def load_padded(x_ref, pad_ref):
    frames, places, width = x_ref.shape

    @pl.when(pl.program_id(0) == 0)
    def _():
        pad_ref[...] = jnp.zeros_like(pad_ref)

    for frame in range(frames):
        pad_ref[frame, 0:places] = x_ref[frame].astype(WIDE)
    return pad_ref[...].reshape(frames * pad_ref.shape[1], width)


def space_forward_kernel(
    places, x_ref, gain_ref, qk_ref, v_ref, out_ref, in_ref, qkv_ref, o_ref, after_ref, pad_ref
):
    frames, padded, width = pad_ref.shape
    values = load_padded(x_ref, pad_ref)
    normed = norm_rows(values, gain_ref[...])[0].astype(LOW)
    in_ref[...] = normed.reshape(frames, padded, width)
    for start, ref in ((0, qk_ref), (2 * width, v_ref)):
        part = dot(normed, ref[...]).astype(LOW)
        qkv_ref[:, :, start : start + part.shape[1]] = part.reshape(frames, padded, -1)
    real = lax.broadcasted_iota(jnp.int32, (padded, padded), 1) < places

    def one_frame(frame, carry):
        for index in range(PAIRS):
            queries = qkv_ref[frame, :, index * LANES : (index + 1) * LANES]
            start = width + index * LANES
            keys = split_heads(qkv_ref[frame, :, start : start + LANES])
            start = 2 * width + index * LANES
            value_block = qkv_ref[frame, :, start : start + LANES]
            outs = []
            for head in range(2):
                scores = jnp.where(real, dot(queries, keys[head], NT), NEVER)
                powers = jnp.exp2((scores - jnp.max(scores, axis=1, keepdims=True)) * POWER)
                chances = powers * (1.0 / jnp.sum(powers, axis=1, keepdims=True))
                outs.append(dot(chances.astype(LOW), value_block))
            o_ref[frame, :, index * LANES : (index + 1) * LANES] = join_heads(*outs).astype(LOW)
        return carry

    lax.fori_loop(0, frames, one_frame, 0)
    after = values + dot(o_ref[...].reshape(frames * padded, width), out_ref[...])
    after = after.reshape(frames, padded // GROUP, GROUP, width)
    for frame in range(frames):
        after_ref[:, frame] = after[frame]


def middle_kernel(
    places,
    place_ref,
    ao_ref,
    ar_ref,
    go_ref,
    gr_ref,
    tgain_ref,
    fgain_ref,
    tproj_ref,
    tout_ref,
    up_ref,
    down_ref,
    qkv_ref,
    int_ref,
    ot_ref,
    inf_ref,
    act_ref,
    gh_ref,
    gb_ref,
    mo_ref,
    mr_ref,
    gt_ref,
    gain_ref,
):
    half = ao_ref.shape[1]
    frames = half + ar_ref.shape[1]
    width = ao_ref.shape[3]
    rows = 2 * frames * GROUP
    block = frames * GROUP
    values = jnp.concatenate([ao_ref[...], ar_ref[...]], axis=1).reshape(rows, width)
    in_time = norm_rows(values, tgain_ref[...])[0].astype(LOW)
    int_ref[...] = in_time
    qkv_ref[...] = dot(in_time, tproj_ref[...]).astype(LOW)
    across = lax.broadcasted_iota(jnp.int32, (block, block), 0)
    down = lax.broadcasted_iota(jnp.int32, (block, block), 1)
    bias = jnp.where(((across ^ down) & (GROUP - 1)) == 0, 0.0, NEVER)
    for group in range(2):
        own = slice(group * block, (group + 1) * block)
        for index in range(PAIRS):
            queries = pair(qkv_ref, own, 0, index)
            keys = stack_heads(pair(qkv_ref, own, 1, index))
            value_block = stack_heads(pair(qkv_ref, own, 2, index))
            both = dot(queries, keys, NT)
            chances = []
            for head in range(2):
                scores = both[:, head * block : (head + 1) * block] + bias
                powers = jnp.exp2((scores - jnp.max(scores, axis=1, keepdims=True)) * POWER)
                total = jnp.sum(powers, axis=1, keepdims=True)
                chances.append((powers * (1.0 / total)).astype(LOW))
            result = dot(jnp.concatenate(chances, axis=1), value_block)
            ot_ref[own, index * LANES : (index + 1) * LANES] = result.astype(LOW)
    values = values + dot(ot_ref[...], tout_ref[...])
    feed_gain = fgain_ref[...]
    in_feed, normed, inverse = norm_rows(values, feed_gain)
    in_feed = in_feed.astype(LOW)
    inf_ref[...] = in_feed
    place = pl.program_id(0) * STEP + lax.broadcasted_iota(jnp.int32, (STEP, width), 0)
    lows, highs = [], []
    for ref in (go_ref, gr_ref):
        for frame in range(half):
            tile = jnp.where(place < places, ref[frame].astype(WIDE), 0.0)
            lows.append(tile[:GROUP])
            highs.append(tile[GROUP:])
    gradient = jnp.concatenate(lows + highs, axis=0)
    grad_low = gradient.astype(LOW)
    gb_ref[...] = grad_low
    hidden_width = up_ref.shape[1]
    piece = width
    root = math.sqrt(2.0 / math.pi)
    for start in range(0, hidden_width, piece):
        cut = slice(start, start + piece)
        hidden = dot(in_feed, up_ref[:, cut])
        back = dot(grad_low, down_ref[:, cut], NT)
        square = hidden * hidden
        slope = jnp.tanh(hidden * (root + (root * 0.044715) * square))
        plus = 0.5 * slope + 0.5
        act_ref[:, cut] = (hidden * plus).astype(LOW)
        inner = hidden * (0.5 * root + (1.5 * root * 0.044715) * square)
        gh_ref[:, cut] = (back * (plus + inner * (1.0 - slope * slope))).astype(LOW)
    mixed = values
    for start in range(0, hidden_width, piece):
        cut = slice(start, start + piece)
        mixed = mixed + dot(act_ref[:, cut], down_ref[:, cut])
    mixed = mixed.reshape(2, frames, GROUP, width)
    for group in range(2):
        cut = slice(group * GROUP, (group + 1) * GROUP)
        mo_ref[0, cut] = jnp.swapaxes(mixed[group, :half], 0, 1).astype(LOW)
        mr_ref[cut] = jnp.swapaxes(mixed[group, half:], 0, 1).astype(LOW)
    back = dot(gh_ref[...], up_ref[...], NT)
    gt_ref[...] = gradient + norm_back(back, normed, inverse, feed_gain)

    @pl.when(pl.program_id(0) == 0)
    def _():
        gain_ref[...] = jnp.zeros_like(gain_ref)

    gain_ref[...] += fold_rows(back * normed)


def time_backward_kernel(
    qkv_ref,
    gt_ref,
    ao_ref,
    ar_ref,
    tgain_ref,
    tout_ref,
    tproj_ref,
    gq_ref,
    tb_ref,
    gso_ref,
    gsr_ref,
    gain_ref,
    d_ref,
):
    half = ao_ref.shape[1]
    frames = half + ar_ref.shape[1]
    width = ao_ref.shape[3]
    rows = 2 * frames * GROUP
    block = frames * GROUP
    tb = gt_ref[...].astype(LOW)
    tb_ref[...] = tb
    d_ref[...] = dot(tb, tout_ref[...], NT).astype(LOW)
    across = lax.broadcasted_iota(jnp.int32, (block, block), 0)
    down = lax.broadcasted_iota(jnp.int32, (block, block), 1)
    bias = jnp.where(((across ^ down) & (GROUP - 1)) == 0, 0.0, NEVER)
    for group in range(2):
        own = slice(group * block, (group + 1) * block)
        for index in range(PAIRS):
            queries = pair(qkv_ref, own, 0, index)
            keys = stack_heads(pair(qkv_ref, own, 1, index))
            value_block = stack_heads(pair(qkv_ref, own, 2, index))
            grad = pair(d_ref, own, 0, index)
            both = dot(keys, queries, NT)
            grad_both = dot(value_block, grad, NT)
            chances, grads = [], []
            for head in range(2):
                cut = slice(head * block, (head + 1) * block)
                scores = both[cut] + bias
                powers = jnp.exp2((scores - jnp.max(scores, axis=0, keepdims=True)) * POWER)
                share = powers * (1.0 / jnp.sum(powers, axis=0, keepdims=True))
                grad_share = grad_both[cut]
                mean = jnp.sum(share * grad_share, axis=0, keepdims=True)
                chances.append(share.astype(LOW))
                grads.append((share * (grad_share - mean)).astype(LOW))
            dv = dot(jnp.concatenate(chances, axis=1), stack_heads(grad))
            dk = dot(jnp.concatenate(grads, axis=1), stack_heads(queries)) * SCALE
            dq = dot(jnp.concatenate(grads, axis=0), keys, TN) * SCALE
            for part, item in enumerate((dq, dk, dv)):
                start = (part * PAIRS + index) * LANES
                gq_ref[own, start : start + LANES] = item.astype(LOW)
    values = jnp.concatenate([ao_ref[...], ar_ref[...]], axis=1).reshape(rows, width)
    gain = tgain_ref[...]
    _, normed, inverse = norm_rows(values, gain)
    back = dot(gq_ref[...], tproj_ref[...], NT)
    result = gt_ref[...] + norm_back(back, normed, inverse, gain)
    for frame in range(frames):
        low = result[frame * GROUP : (frame + 1) * GROUP]
        high = result[block + frame * GROUP : block + (frame + 1) * GROUP]
        tile = jnp.concatenate([low, high], axis=0)
        if frame < half:
            gso_ref[frame] = tile
        else:
            gsr_ref[frame - half] = tile

    @pl.when(pl.program_id(0) == 0)
    def _():
        gain_ref[...] = jnp.zeros_like(gain_ref)

    gain_ref[...] += fold_rows(back * normed)


def space_backward_kernel(
    places,
    place_ref,
    x_ref,
    gs_ref,
    qkv_ref,
    gain_row_ref,
    out_ref,
    qk_ref,
    v_ref,
    gq_ref,
    sb_ref,
    gx_ref,
    gain_ref,
    pad_ref,
    d_ref,
    order_ref,
):
    frames, padded, width = pad_ref.shape
    stride = order_ref.shape[1] // padded
    values = load_padded(x_ref, pad_ref)
    grad_space = gs_ref[...].reshape(frames * padded, width)
    sb = grad_space.astype(LOW)
    sb_ref[...] = sb.reshape(frames, padded, width)
    d_ref[...] = dot(sb, out_ref[...], NT).astype(LOW).reshape(frames, padded, width)
    real = lax.broadcasted_iota(jnp.int32, (padded, padded), 0) < places

    def one_frame(frame, carry):
        for index in range(PAIRS):
            queries = qkv_ref[frame, :, index * LANES : (index + 1) * LANES]
            start = width + index * LANES
            key_block = qkv_ref[frame, :, start : start + LANES]
            start = 2 * width + index * LANES
            value_block = qkv_ref[frame, :, start : start + LANES]
            grad = d_ref[frame, :, index * LANES : (index + 1) * LANES]
            keys = split_heads(key_block)
            vals = split_heads(value_block)
            outs = []
            for head in range(2):
                scores = jnp.where(real, dot(keys[head], queries, NT), NEVER)
                powers = jnp.exp2((scores - jnp.max(scores, axis=0, keepdims=True)) * POWER)
                share = powers * (1.0 / jnp.sum(powers, axis=0, keepdims=True))
                grad_share = dot(vals[head], grad, NT)
                mean = jnp.sum(share * grad_share, axis=0, keepdims=True)
                ds = (share * (grad_share - mean)).astype(LOW)
                outs.append(
                    (
                        dot(ds, key_block, TN) * SCALE,
                        dot(ds, queries) * SCALE,
                        dot(share.astype(LOW), grad),
                    )
                )
            for part in range(3):
                start = part * width + index * LANES
                gq_ref[frame, :, start : start + LANES] = join_heads(
                    outs[0][part], outs[1][part]
                ).astype(LOW)
        return carry

    lax.fori_loop(0, frames, one_frame, 0)
    gain = gain_row_ref[...]
    _, normed, inverse = norm_rows(values, gain)
    back = dot(gq_ref[:, :, : 2 * width].reshape(frames * padded, 2 * width), qk_ref[...], NT)
    back = back + dot(gq_ref[:, :, 2 * width :].reshape(frames * padded, width), v_ref[...], NT)
    result = grad_space + norm_back(back, normed, inverse, gain)
    result = result.reshape(frames, padded, width)
    for frame in range(frames):
        rows = pl.ds(pl.program_id(0) * frames + frame, padded, stride=stride)
        for lane in range(width // LANES):
            order_ref[lane, rows, :] = result[frame, :, lane * LANES : (lane + 1) * LANES]

    @pl.when(pl.program_id(0) == pl.num_programs(0) - 1)
    def _():
        for lane in range(width // LANES):
            tile = order_ref[lane, 0 : places * stride].astype(gx_ref.dtype)
            tile = tile.reshape(places, stride, LANES)
            if len(gx_ref.shape) == 4:
                gx_ref[0, :, :, lane * LANES : (lane + 1) * LANES] = tile
            else:
                gx_ref[:, :, lane * LANES : (lane + 1) * LANES] = tile

    @pl.when(pl.program_id(0) == 0)
    def _():
        gain_ref[...] = jnp.zeros_like(gain_ref)

    gain_ref[...] += fold_rows(back * normed)


def whole(shape):
    return pl.BlockSpec(
        shape, lambda *_: (0,) * len(shape), pipeline_mode=pl.Buffered(buffer_count=1)
    )


def columns(array, width, index):
    return pl.BlockSpec(
        (array.shape[0], width),
        lambda *_: (0, index),
        pipeline_mode=pl.Buffered(buffer_count=1),
    )


def params():
    return pltpu.CompilerParams(vmem_limit_bytes=LIMIT)


def cost(flops, *arrays):
    size = sum(math.prod(item.shape) * jnp.dtype(item.dtype).itemsize for item in arrays)
    return pl.CostEstimate(
        flops=int(flops) // SHRINK, bytes_accessed=int(size) // SHRINK, transcendentals=0
    )


def padded_places(places):
    return -(-places // STEP) * STEP


def by_frame(count, *tail):
    return pl.BlockSpec((count,) + tail, lambda step, *_: (step,) + (0,) * len(tail))


def space_forward(x, gain, first, second):
    frames, places, width = x.shape
    padded = padded_places(places)
    groups = padded // GROUP
    rows = frames * padded
    outs = (
        jax.ShapeDtypeStruct((frames, padded, width), LOW),
        jax.ShapeDtypeStruct((frames, padded, 3 * width), LOW),
        jax.ShapeDtypeStruct((frames, padded, width), LOW),
        jax.ShapeDtypeStruct((groups, frames, GROUP, width), WIDE),
    )
    flops = 2 * rows * width * 4 * width + 8 * rows * padded * width
    return pl.pallas_call(
        functools.partial(space_forward_kernel, places),
        grid=(frames // 2,),
        in_specs=[
            by_frame(2, places, width),
            whole(gain.shape),
            whole(first.shape),
            columns(second, width, 0),
            columns(second, width, 1),
        ],
        out_specs=[
            by_frame(2, padded, width),
            by_frame(2, padded, 3 * width),
            by_frame(2, padded, width),
            pl.BlockSpec((groups, 2, GROUP, width), lambda step: (0, step, 0, 0)),
        ],
        out_shape=outs,
        scratch_shapes=[pltpu.VMEM((2, padded, width), WIDE)],
        compiler_params=params(),
        cost_estimate=cost(flops, x, first, second, *outs),
        name="space_forward",
    )(x, gain, first, second, second)


def middle(place, after_own, after_rest, g_own, g_rest, tgain, fgain, packed):
    groups, half, _, width = after_own.shape
    places = g_own.shape[1]
    frames = 2 * half
    rows = groups * frames * GROUP
    block = 2 * frames * GROUP
    hidden = (packed.shape[1] - 4 * width) // 2
    padded = groups * GROUP
    outs = (
        jax.ShapeDtypeStruct((rows, 3 * width), LOW),
        jax.ShapeDtypeStruct((rows, width), LOW),
        jax.ShapeDtypeStruct((rows, width), LOW),
        jax.ShapeDtypeStruct((rows, width), LOW),
        jax.ShapeDtypeStruct((rows, hidden), LOW),
        jax.ShapeDtypeStruct((rows, hidden), LOW),
        jax.ShapeDtypeStruct((rows, width), LOW),
        jax.ShapeDtypeStruct((2, places, half, width), LOW),
        jax.ShapeDtypeStruct((places, half, width), LOW),
        jax.ShapeDtypeStruct((rows, width), WIDE),
        jax.ShapeDtypeStruct((8, width), WIDE),
    )
    by_row = lambda size: pl.BlockSpec((block, size), lambda step, place: (step, 0))
    by_group = pl.BlockSpec((2, half, GROUP, width), lambda step, place: (step, 0, 0, 0))
    by_place = pl.BlockSpec((half, STEP, width), lambda step, place: (0, step, 0))
    flops = 2 * rows * width * (4 * width + 4 * hidden) + 8 * rows * frames * GROUP * width
    return pl.pallas_call(
        functools.partial(middle_kernel, places),
        grid_spec=pltpu.PrefetchScalarGridSpec(
            num_scalar_prefetch=1,
            grid=(groups // 2,),
            in_specs=[by_group, by_group, by_place, by_place]
            + [
                whole(tgain.shape),
                whole(fgain.shape),
                columns(packed, 3 * width, 0),
                columns(packed, width, 3),
                columns(packed, hidden, 1),
                columns(packed, hidden, 2),
            ],
            out_specs=[
                by_row(3 * width),
                by_row(width),
                by_row(width),
                by_row(width),
                by_row(hidden),
                by_row(hidden),
                by_row(width),
                pl.BlockSpec((1, STEP, half, width), lambda step, place: (place[0], step, 0, 0)),
                pl.BlockSpec((STEP, half, width), lambda step, place: (step, 0, 0)),
                by_row(width),
                pl.BlockSpec((8, width), lambda step, place: (0, 0)),
            ],
        ),
        out_shape=outs,
        compiler_params=params(),
        cost_estimate=cost(flops, after_own, after_rest, g_own, g_rest, *outs),
        name="middle",
    )(place, after_own, after_rest, g_own, g_rest, tgain, fgain, packed, packed, packed, packed)


def time_backward(qkv, g_time, after_own, after_rest, tgain, packed):
    groups, half, _, width = after_own.shape
    frames = 2 * half
    rows = groups * frames * GROUP
    block = 2 * frames * GROUP
    padded = groups * GROUP
    outs = (
        jax.ShapeDtypeStruct((rows, 3 * width), LOW),
        jax.ShapeDtypeStruct((rows, width), LOW),
        jax.ShapeDtypeStruct((half, padded, width), WIDE),
        jax.ShapeDtypeStruct((half, padded, width), WIDE),
        jax.ShapeDtypeStruct((8, width), WIDE),
    )
    by_row = lambda size: pl.BlockSpec((block, size), lambda step: (step, 0))
    by_group = pl.BlockSpec((2, half, GROUP, width), lambda step: (step, 0, 0, 0))
    by_place = pl.BlockSpec((half, STEP, width), lambda step: (0, step, 0))
    flops = 2 * rows * width * 4 * width + 20 * rows * frames * GROUP * width
    return pl.pallas_call(
        time_backward_kernel,
        grid=(groups // 2,),
        in_specs=[by_row(3 * width), by_row(width), by_group, by_group]
        + [whole(tgain.shape), columns(packed, width, 3), columns(packed, 3 * width, 0)],
        out_specs=[
            by_row(3 * width),
            by_row(width),
            by_place,
            by_place,
            pl.BlockSpec((8, width), lambda step: (0, 0)),
        ],
        out_shape=outs,
        scratch_shapes=[pltpu.VMEM((block, width), LOW)],
        compiler_params=params(),
        cost_estimate=cost(flops, qkv, g_time, after_own, after_rest, *outs),
        name="time_backward",
    )(qkv, g_time, after_own, after_rest, tgain, packed, packed)


def space_backward(place, x, g_space, qkv, gain, first, second, kind):
    frames, places, width = x.shape
    padded = padded_places(places)
    rows = frames * padded
    own = kind == WIDE
    shape = (2, places, frames, width) if own else (places, frames, width)
    outs = (
        jax.ShapeDtypeStruct((frames, padded, 3 * width), LOW),
        jax.ShapeDtypeStruct((frames, padded, width), LOW),
        jax.ShapeDtypeStruct(shape, kind),
        jax.ShapeDtypeStruct((8, width), WIDE),
    )
    flops = 2 * rows * width * 4 * width + 20 * rows * padded * width
    return pl.pallas_call(
        functools.partial(space_backward_kernel, places),
        grid_spec=pltpu.PrefetchScalarGridSpec(
            num_scalar_prefetch=1,
            grid=(frames // 2,),
            in_specs=[
                by_frame(2, places, width),
                by_frame(2, padded, width),
                by_frame(2, padded, 3 * width),
                whole(gain.shape),
                columns(second, width, 1),
                whole(first.shape),
                columns(second, width, 0),
            ],
            out_specs=[
                by_frame(2, padded, 3 * width),
                by_frame(2, padded, width),
                pl.BlockSpec((1,) + shape[1:], lambda step, place: (place[0], 0, 0, 0))
                if own
                else pl.BlockSpec(shape, lambda step, place: (0, 0, 0)),
                pl.BlockSpec((8, width), lambda step, place: (0, 0)),
            ],
            scratch_shapes=[
                pltpu.VMEM((2, padded, width), WIDE),
                pltpu.VMEM((2, padded, width), LOW),
                pltpu.VMEM((width // LANES, padded * frames, LANES), WIDE),
            ],
        ),
        out_shape=outs,
        compiler_params=params(),
        cost_estimate=cost(flops, x, g_space, qkv, *outs),
        name="space_backward",
    )(place, x, g_space, qkv, gain, second, first, second)


def gradient_kernel(parts, tiles, core_ref, *refs):
    step = pl.program_id(0)

    def emit(pairs):
        total = dot(pairs[0][0][...], pairs[0][1][...], TN)
        for first, second in pairs[1:]:
            total = total + dot(first[...], second[...], TN)
        if core_ref is None:
            refs[-1][...] = total.astype(LOW)
            return
        keep_ref, send_ref = refs[-2:]
        total = total.reshape(keep_ref.shape[0], 2, keep_ref.shape[1], keep_ref.shape[2])
        total = total.astype(LOW)
        keep = core_ref[0] == 0
        keep_ref[...] = jnp.where(keep, total[:, 0], total[:, 1])
        send_ref[...] = jnp.where(keep, total[:, 1], total[:, 0])

    start = 0
    for (first, last), count in zip(tiles, parts):
        group = refs[start : start + 2 * count]
        start += 2 * count
        pairs = [(group[2 * index], group[2 * index + 1]) for index in range(count)]
        pl.when((step >= first) & (step < last))(functools.partial(emit, pairs))


def plan_gradient(groups):
    width = groups[0][0][0][0].shape[1] if groups[0][3] == 1 else groups[0][0][0][1].shape[1]
    count = groups[-1][2]
    specs, arrays, parts, tiles = [], [], [], []
    flops = 0
    for pairs, first, last, side, offset in groups:
        parts.append(len(pairs))
        tiles.append((first, last))
        for pair_arrays in pairs:
            for index, item in enumerate(pair_arrays):
                rows = item.shape[0]
                if index == side and last - first > 1:
                    spec = pl.BlockSpec(
                        (rows, width),
                        lambda step, *_, first=first, last=last, offset=offset: (
                            0,
                            jnp.clip(step - first, 0, last - first - 1) + offset,
                        ),
                    )
                else:
                    fixed = offset if index == side else 0
                    spec = pl.BlockSpec(
                        (rows, width),
                        lambda step, *_, fixed=fixed: (0, fixed),
                        pipeline_mode=pl.Buffered(buffer_count=1),
                    )
                specs.append(spec)
                arrays.append(item)
            flops += 2 * rows * width * width * (last - first)
    return width, count, specs, arrays, parts, tiles, flops


def weight_gradient(*groups):
    width, count, specs, arrays, parts, tiles, flops = plan_gradient(groups)
    out = jax.ShapeDtypeStruct((width, count * width), LOW)
    return pl.pallas_call(
        functools.partial(gradient_kernel, parts, tiles, None),
        grid=(count,),
        in_specs=specs,
        out_specs=pl.BlockSpec((width, width), lambda step: (0, step)),
        out_shape=out,
        compiler_params=params(),
        cost_estimate=cost(flops, *arrays, out),
        name="weight_gradient",
    )(*arrays)


def split_gradient(core, owners, *groups):
    width, count, specs, arrays, parts, tiles, flops = plan_gradient(groups)
    blocks, rows = owners // 4, 2 * (width // owners)
    out = jax.ShapeDtypeStruct((blocks, rows, count * width), LOW)
    out_spec = pl.BlockSpec((blocks, rows, width), lambda step, core: (0, 0, step))
    return pl.pallas_call(
        functools.partial(gradient_kernel, parts, tiles),
        grid_spec=pltpu.PrefetchScalarGridSpec(
            num_scalar_prefetch=1,
            grid=(count,),
            in_specs=specs,
            out_specs=[out_spec, out_spec],
        ),
        out_shape=[out, out],
        compiler_params=params(),
        cost_estimate=cost(flops, *arrays, out, out),
        name="split_gradient",
    )(core, *arrays)


MICRO = 2


def norm_forward(values, gain):
    centred = values - jnp.mean(values, axis=-1, keepdims=True)
    inverse = lax.rsqrt(jnp.mean(centred * centred, axis=-1, keepdims=True) + epsilon)
    normed = centred * inverse
    return (normed * gain, normed, inverse)


def norm_backward(gradient, normed, inverse, gain):
    gain_grad = jnp.sum(gradient * normed, axis=(0, 1, 2))
    scaled = gradient * gain
    centred_grad = (
        scaled
        - jnp.mean(scaled, axis=-1, keepdims=True)
        - normed * jnp.mean(scaled * normed, axis=-1, keepdims=True)
    )
    return (inverse * centred_grad, gain_grad)


def to_places(blocks):
    clip_count, frames, places, model_width = blocks.shape
    return blocks.transpose(0, 2, 1, 3).reshape(clip_count * places, frames, HEADS, HEAD)


def from_places(attended, clip_count, places):
    frames = attended.shape[1]
    return attended.reshape(clip_count, places, frames, HEADS * HEAD).transpose(0, 2, 1, 3)


def attend_forward(queries, key_block, value_block):
    factor = HEAD ** (-0.5)
    scores = (
        jnp.einsum("blhe,bmhe->bhlm", queries, key_block, preferred_element_type=jnp.float32)
        * factor
    )
    highest = jnp.max(scores, axis=-1, keepdims=True)
    powers = jnp.exp(scores - highest)
    row_total = jnp.sum(powers, axis=-1, keepdims=True)
    chances = (powers / row_total).astype(jnp.bfloat16)
    result = jnp.einsum("bhlm,bmhe->blhe", chances, value_block, preferred_element_type=jnp.float32)
    return (result, highest + jnp.log(row_total))


def attend_backward(queries, key_block, value_block, logsum, grad_out):
    factor = HEAD ** (-0.5)
    scores = (
        jnp.einsum("blhe,bmhe->bhlm", queries, key_block, preferred_element_type=jnp.float32)
        * factor
    )
    chances = jnp.exp(scores - logsum)
    grad_chances = jnp.einsum(
        "blhe,bmhe->bhlm", grad_out, value_block, preferred_element_type=jnp.float32
    )
    grad_scores = (
        chances * (grad_chances - jnp.sum(chances * grad_chances, axis=-1, keepdims=True))
    ).astype(jnp.bfloat16)
    grad_queries = (
        jnp.einsum("bhlm,bmhe->blhe", grad_scores, key_block, preferred_element_type=jnp.float32)
        * factor
    )
    grad_keys = (
        jnp.einsum("bhlm,blhe->bmhe", grad_scores, queries, preferred_element_type=jnp.float32)
        * factor
    )
    grad_values = jnp.einsum(
        "bhlm,blhe->bmhe",
        chances.astype(jnp.bfloat16),
        grad_out,
        preferred_element_type=jnp.float32,
    )
    return (grad_queries, grad_keys, grad_values)


def project(values, matrix):
    return jnp.einsum("cfpd,de->cfpe", values, matrix, preferred_element_type=jnp.float32)


def project_back(gradient, matrix):
    return jnp.einsum("cfpe,de->cfpd", gradient, matrix, preferred_element_type=jnp.float32)


def outer_sum(values, gradient):
    return jnp.einsum("cfpd,cfpe->de", values, gradient, preferred_element_type=jnp.float32)


def forward(sample, gathered):
    (
        space_gain,
        time_gain,
        feed_gain,
        space_proj,
        space_out,
        time_proj,
        time_out,
        up_proj,
        down_proj,
    ) = gathered
    clip_count, frames, places, model_width = sample.shape
    normed_space = norm_forward(sample, space_gain.astype(jnp.float32))
    in_space = normed_space[0].astype(jnp.bfloat16)
    qkv_space = project(in_space, space_proj).astype(jnp.bfloat16)
    parted = qkv_space.reshape(clip_count * frames, places, 3, HEADS, HEAD)
    attended, logsum_space = attend_forward(parted[:, :, 0], parted[:, :, 1], parted[:, :, 2])
    out_space = attended.reshape(clip_count, frames, places, model_width).astype(jnp.bfloat16)
    after_space = sample + project(out_space, space_out)
    normed_time = norm_forward(after_space, time_gain.astype(jnp.float32))
    in_time = normed_time[0].astype(jnp.bfloat16)
    qkv_time = project(in_time, time_proj).astype(jnp.bfloat16)
    kv_whole = lax.all_gather(qkv_time[..., model_width:], "frame", axis=1, tiled=True)
    attended, logsum_time = attend_forward(
        to_places(qkv_time[..., :model_width]),
        to_places(kv_whole[..., :model_width]),
        to_places(kv_whole[..., model_width:]),
    )
    out_time = from_places(attended, clip_count, places).astype(jnp.bfloat16)
    after_time = after_space + project(out_time, time_out)
    normed_feed = norm_forward(after_time, feed_gain.astype(jnp.float32))
    in_feed = normed_feed[0].astype(jnp.bfloat16)
    hidden = project(in_feed, up_proj)
    active = jax.nn.gelu(hidden).astype(jnp.bfloat16)
    result = after_time + project(active, down_proj)
    saved = (
        normed_space,
        in_space,
        qkv_space,
        logsum_space,
        out_space,
        normed_time,
        in_time,
        qkv_time,
        kv_whole,
        logsum_time,
        out_time,
        normed_feed,
        in_feed,
        hidden,
        active,
    )
    return (result, saved)


def backward(gradient, saved, gathered):
    (
        space_gain,
        time_gain,
        feed_gain,
        space_proj,
        space_out,
        time_proj,
        time_out,
        up_proj,
        down_proj,
    ) = gathered
    (
        normed_space,
        in_space,
        qkv_space,
        logsum_space,
        out_space,
        normed_time,
        in_time,
        qkv_time,
        time_side,
        logsum_time,
        out_time,
        normed_feed,
        in_feed,
        hidden,
        active,
    ) = saved
    clip_count, frames, places, model_width = gradient.shape
    grad_low = gradient.astype(jnp.bfloat16)
    grad_down = outer_sum(active, grad_low)
    grad_active = project_back(grad_low, down_proj)
    gelu_value, gelu_pull = jax.vjp(jax.nn.gelu, hidden)
    grad_hidden = gelu_pull(grad_active)[0].astype(jnp.bfloat16)
    grad_up = outer_sum(in_feed, grad_hidden)
    back_feed, grad_feed_gain = norm_backward(
        project_back(grad_hidden, up_proj),
        normed_feed[1],
        normed_feed[2],
        feed_gain.astype(jnp.float32),
    )
    grad_time = gradient + back_feed
    time_low = grad_time.astype(jnp.bfloat16)
    grad_tout = outer_sum(out_time, time_low)
    grad_out_time = project_back(time_low, time_out).astype(jnp.bfloat16)
    grad_queries, grad_keys, grad_values = attend_backward(
        to_places(qkv_time[..., :model_width]),
        to_places(time_side[..., :model_width]),
        to_places(time_side[..., model_width:]),
        logsum_time,
        to_places(grad_out_time),
    )
    grad_kv = jnp.concatenate(
        (from_places(grad_keys, clip_count, places), from_places(grad_values, clip_count, places)),
        axis=-1,
    )
    grad_kv_own = lax.psum_scatter(
        grad_kv.astype(jnp.bfloat16), "frame", scatter_dimension=1, tiled=True
    ).astype(jnp.float32)
    grad_qkv_time = jnp.concatenate(
        (from_places(grad_queries, clip_count, places), grad_kv_own), axis=-1
    ).astype(jnp.bfloat16)
    grad_tproj = outer_sum(in_time, grad_qkv_time)
    back_time, grad_time_gain = norm_backward(
        project_back(grad_qkv_time, time_proj),
        normed_time[1],
        normed_time[2],
        time_gain.astype(jnp.float32),
    )
    grad_space = grad_time + back_time
    space_low = grad_space.astype(jnp.bfloat16)
    grad_sout = outer_sum(out_space, space_low)
    grad_out_space = project_back(space_low, space_out).astype(jnp.bfloat16)
    parted = qkv_space.reshape(clip_count * frames, places, 3, HEADS, HEAD)
    grad_queries, grad_keys, grad_values = attend_backward(
        parted[:, :, 0],
        parted[:, :, 1],
        parted[:, :, 2],
        logsum_space,
        grad_out_space.reshape(clip_count * frames, places, HEADS, HEAD),
    )
    grad_qkv_space = (
        jnp.stack((grad_queries, grad_keys, grad_values), axis=2)
        .reshape(clip_count, frames, places, 3 * model_width)
        .astype(jnp.bfloat16)
    )
    grad_sproj = outer_sum(in_space, grad_qkv_space)
    back_space, grad_space_gain = norm_backward(
        project_back(grad_qkv_space, space_proj),
        normed_space[1],
        normed_space[2],
        space_gain.astype(jnp.float32),
    )
    grad_input = grad_space + back_space
    return (
        grad_input,
        (
            grad_space_gain,
            grad_time_gain,
            grad_feed_gain,
            grad_sproj,
            grad_sout,
            grad_tproj,
            grad_tout,
            grad_up,
            grad_down,
        ),
    )


def general(
    tokens,
    cotangent,
    space_gain,
    time_gain,
    feed_gain,
    space_proj,
    space_out,
    time_proj,
    time_out,
    up_proj,
    down_proj,
):
    owned = (
        space_gain,
        time_gain,
        feed_gain,
        space_proj,
        space_out,
        time_proj,
        time_out,
        up_proj,
        down_proj,
    )
    devices_all = lax.axis_size(("clip", "frame"))
    per_micro = tokens.shape[0] // MICRO
    totals = tuple(
        (
            jnp.zeros((piece.shape[0] * devices_all,) + piece.shape[1:], jnp.float32)
            for piece in owned
        )
    )
    gathered = (
        lax.all_gather(space_gain, ("clip", "frame"), axis=0, tiled=True),
        lax.all_gather(time_gain, ("clip", "frame"), axis=0, tiled=True),
        lax.all_gather(feed_gain, ("clip", "frame"), axis=0, tiled=True),
        lax.all_gather(space_proj, ("clip", "frame"), axis=0, tiled=True),
        lax.all_gather(space_out, ("clip", "frame"), axis=0, tiled=True),
        lax.all_gather(time_proj, ("clip", "frame"), axis=0, tiled=True),
        lax.all_gather(time_out, ("clip", "frame"), axis=0, tiled=True),
        lax.all_gather(up_proj, ("clip", "frame"), axis=0, tiled=True),
        lax.all_gather(down_proj, ("clip", "frame"), axis=0, tiled=True),
    )
    mixed_parts = []
    grad_parts = []
    for micro_index in range(MICRO):
        sample = tokens[micro_index * per_micro : (micro_index + 1) * per_micro].astype(jnp.float32)
        result, saved = forward(sample, gathered)
        mixed_parts.append(result.astype(jnp.bfloat16))
        gradient = cotangent[micro_index * per_micro : (micro_index + 1) * per_micro].astype(
            jnp.float32
        )
        grad_input, grads = backward(gradient, saved, gathered)
        grad_parts.append(grad_input)
        totals = tuple((first + second for first, second in zip(totals, grads)))
    flat = tuple((item.reshape(-1) for item in totals))
    owners = (
        lax.psum_scatter(flat[0], ("clip", "frame"), scatter_dimension=0, tiled=True),
        lax.psum_scatter(flat[1], ("clip", "frame"), scatter_dimension=0, tiled=True),
        lax.psum_scatter(flat[2], ("clip", "frame"), scatter_dimension=0, tiled=True),
        lax.psum_scatter(flat[3], ("clip", "frame"), scatter_dimension=0, tiled=True),
        lax.psum_scatter(flat[4], ("clip", "frame"), scatter_dimension=0, tiled=True),
        lax.psum_scatter(flat[5], ("clip", "frame"), scatter_dimension=0, tiled=True),
        lax.psum_scatter(flat[6], ("clip", "frame"), scatter_dimension=0, tiled=True),
        lax.psum_scatter(flat[7], ("clip", "frame"), scatter_dimension=0, tiled=True),
        lax.psum_scatter(flat[8], ("clip", "frame"), scatter_dimension=0, tiled=True),
    )
    shaped = tuple((piece.reshape(mine.shape) for piece, mine in zip(owners, owned)))
    mixed = jnp.concatenate(mixed_parts, axis=0)
    grad_tokens = jnp.concatenate(grad_parts, axis=0)
    return (
        mixed,
        grad_tokens,
        shaped[0],
        shaped[1],
        shaped[2],
        shaped[3],
        shaped[4],
        shaped[5],
        shaped[6],
        shaped[7],
        shaped[8],
    )


def swap_axis(values, axis):
    size = lax.axis_size(axis)
    return lax.ppermute(values, axis, [(index, size - 1 - index) for index in range(size)])


def flip(values, mask):
    size = lax.axis_size("clip")
    return lax.ppermute(values, "clip", [(index, index ^ mask) for index in range(size)])


def tie(*items):
    return lax.optimization_barrier(items)


def bit_of(mask):
    return (lax.axis_index("clip") // mask) % 2


def in_order(bit, mine, other, axis):
    return jnp.where(
        bit == 0, jnp.stack([mine, other], axis=axis), jnp.stack([other, mine], axis=axis)
    )


def pick(values, index, axis):
    return lax.dynamic_index_in_dim(values, index, axis, keepdims=False)


def added(*items):
    return sum(item.astype(WIDE) for item in items)


def collect_start(shard):
    return in_order(lax.axis_index("frame"), shard, swap_axis(shard, "frame"), 0)


def collect_lines(item):
    line = lax.axis_index("clip") // 4
    parts = [item] + [flip(item, 4 * step) for step in range(1, 4)]
    odd, far = line % 2, line // 2
    parts = [jnp.where(odd == 0, parts[index], parts[index ^ 1]) for index in range(4)]
    parts = [jnp.where(far == 0, parts[index], parts[index ^ 2]) for index in range(4)]
    return jnp.stack(parts, axis=0)


def collect_half(item, mask, axis):
    return in_order(bit_of(mask), item, flip(item, mask), axis)


def merged(item):
    return item.reshape(-1, item.shape[-1])


def scatter_core(keep, send):
    return keep, flip(send, 1)


def scatter_columns(keep, other):
    shape = (4, 2) + keep.shape[1:]
    keep, other = keep.reshape(shape), other.reshape(shape)
    bit = bit_of(2)
    send = added(pick(keep, 1 - bit, 1), pick(other, 1 - bit, 1)).astype(LOW)
    return added(pick(keep, bit, 1), pick(other, bit, 1)).astype(LOW), flip(send, 2)


def scatter_lines(keep, other):
    line = lax.axis_index("clip") // 4
    total = added(keep, other).astype(LOW)
    parts = [flip(pick(total, line ^ step, 0), 4 * step) for step in range(1, 4)]
    return (pick(total, line, 0), *parts)


def scatter_frames(*parts):
    total = added(*parts).astype(LOW)
    total = total.reshape(2, total.shape[0] // 2, total.shape[1])
    place = lax.axis_index("frame")
    return pick(total, place, 0), swap_axis(pick(total, 1 - place, 0), "frame")


def summed(values):
    for mask in (1, 2, 4, 8):
        values = values + flip(values, mask)
    return values + swap_axis(values, "frame")


def flat_rows(values):
    return values.reshape(-1, values.shape[-1])


def clip_local(
    tokens,
    cotangent,
    space_gain,
    time_gain,
    feed_gain,
    space_proj,
    space_out,
    time_proj,
    time_out,
    up_proj,
    down_proj,
):
    axes = ("clip", "frame")
    place = lax.axis_index("frame")
    owners = lax.axis_size(axes)
    me = lax.axis_index(axes)
    share, width = space_out.shape
    blocks = down_proj.shape[0] // share
    core = bit_of(1).reshape(1)
    spot = place.reshape(1)

    gains = jnp.stack([space_gain, time_gain, feed_gain], axis=1)
    gains = jnp.pad(gains, ((0, 0), (0, LANES - 3)))
    first = collect_start(space_proj[:, : 2 * width])
    second = collect_start(
        jnp.concatenate([space_proj[:, 2 * width :], space_out, gains], axis=1)
    )
    up_order = up_proj.reshape(share, owners, blocks, share).transpose(0, 2, 1, 3)
    down_order = down_proj.reshape(blocks, share, width).transpose(1, 0, 2)
    packed = jnp.concatenate(
        [time_proj, time_out, up_order.reshape(share, -1), down_order.reshape(share, -1)], axis=1
    )
    first, second, by_place = tie(first, second, tokens.transpose(0, 2, 1, 3))
    half = by_place.shape[1] // 2
    send = pick(by_place, 1 - place, 0)
    rest_a = swap_axis(send[:half], "frame")
    first = collect_lines(first)
    second, first, rest_a, send, packed = tie(second, first, rest_a, send, packed)
    packed = lax.all_gather(packed, axes, axis=0, tiled=True)
    rest_b = swap_axis(send[half:], "frame")
    second = collect_lines(second)
    first = collect_half(first, 2, 1)
    first, second = tie(first, second)
    second = collect_half(second, 2, 1)
    second, rest_b, g_send = tie(second, rest_b, cotangent.transpose(0, 2, 1, 3))
    g_rest = swap_axis(pick(g_send, 1 - place, 0), "frame")
    first = merged(collect_half(first, 1, 2))
    second = merged(collect_half(second, 1, 2))
    rest = jnp.concatenate([rest_a, rest_b], axis=0).transpose(1, 0, 2)
    own = pick(tokens, place, 0)
    g_own = pick(cotangent, place, 0)
    table = second[:, 2 * width : 2 * width + 3].astype(WIDE).T
    sgain, tgain, fgain = (table[index : index + 1] for index in range(3))
    in_o, qkv_o, o_o, after_o = space_forward(own, sgain, first, second)
    rest, after_o = tie(rest, after_o)
    in_r, qkv_r, o_r, after_r = space_forward(rest, sgain, first, second)
    g_rest, after_r = tie(g_rest, after_r)
    g_rest = g_rest.transpose(1, 0, 2)
    qkv_t, in_t, o_t, in_f, act, gh, gb, mixed, mixed_r, g_time, gain_f = middle(
        spot, after_o, after_r, g_own, g_rest, tgain, fgain, packed
    )
    mixed_other = swap_axis(mixed_r, "frame")
    scatter = lambda item: lax.psum_scatter(item, axes, scatter_dimension=0, tiled=True)
    d_up = weight_gradient(([(in_f, gh)], 0, blocks, 1, 0))
    d_up, act = tie(d_up, act)
    d_up = scatter(d_up)
    d_down = weight_gradient(([(act, gb)], 0, blocks, 0, 0))
    d_down, g_time = tie(d_down, g_time)
    gq_t, tb, gs_o, gs_r, gain_t = time_backward(
        qkv_t, g_time, after_o, after_r, tgain, packed
    )
    d_time = split_gradient(
        core, owners, ([(in_t, gq_t)], 0, 3, 1, 0), ([(o_t, tb)], 3, 4, 1, 0)
    )
    d_up, d_down, d_time, gs_r, mixed_other = tie(d_up, d_down, d_time, gs_r, mixed_other)
    d_down = scatter(d_down)
    d_time = scatter_columns(*scatter_core(*d_time))
    gq_r, sb_r, gx_r, gain_sr = space_backward(spot, rest, gs_r, qkv_r, sgain, first, second, LOW)
    grad_other = swap_axis(gx_r, "frame")
    d_time, gs_o, sb_r = tie(d_time, gs_o, sb_r)
    d_time = scatter_lines(*d_time)
    gq_o, sb_o, grad_tokens, gain_so = space_backward(spot, own, gs_o, qkv_o, sgain, first, second, WIDE)
    d_down, d_time, gq_o, sb_o = tie(d_down, d_time, gq_o, sb_o)
    inputs = [(flat_rows(in_o), flat_rows(gq_o)), (flat_rows(in_r), flat_rows(gq_r))]
    outputs = [(flat_rows(o_o), flat_rows(sb_o)), (flat_rows(o_r), flat_rows(sb_r))]
    d_first = scatter_core(*split_gradient(core, owners, (inputs, 0, 2, 1, 0)))
    d_second = split_gradient(core, owners, (inputs, 0, 1, 1, 2), (outputs, 1, 2, 1, 0))
    gain_parts = tie(gain_so, gain_sr, gain_t, gain_f, d_first[0])
    d_first = (gain_parts[4], d_first[1])
    gain_grads = summed(
        jnp.stack(
            [
                jnp.sum(item, axis=0)
                for item in (gain_parts[0] + gain_parts[1], gain_parts[2], gain_parts[3])
            ]
        )
    )
    d_first, d_second = tie(d_first, d_second)
    d_second = scatter_core(*d_second)
    d_first = scatter_columns(*d_first)
    d_second = scatter_columns(*d_second)
    d_time = scatter_frames(*d_time)
    d_first = scatter_frames(*scatter_lines(*d_first))
    d_second = scatter_frames(*scatter_lines(*d_second))
    d_first, d_second, d_time = (added(*item) for item in (d_first, d_second, d_time))
    d_up, d_down = d_up.astype(WIDE), d_down.astype(WIDE)
    d_up = d_up.reshape(share, blocks, owners, share).transpose(0, 2, 1, 3)
    d_down = d_down.reshape(share, blocks, width).transpose(1, 0, 2)
    gain_grads = lax.dynamic_slice_in_dim(gain_grads, me * share, share, axis=1)
    mixed = lax.dynamic_update_index_in_dim(mixed, mixed_other, 1 - place, 0)
    grad_tokens = lax.dynamic_update_index_in_dim(
        grad_tokens, grad_other.astype(WIDE), 1 - place, 0
    )
    mixed, grad_tokens = mixed.transpose(0, 2, 1, 3), grad_tokens.transpose(0, 2, 1, 3)
    return (
        mixed,
        grad_tokens,
        gain_grads[0],
        gain_grads[1],
        gain_grads[2],
        jnp.concatenate([d_first, d_second[:, :width]], axis=1),
        d_second[:, width:],
        d_time[:, : 3 * width],
        d_time[:, 3 * width :],
        d_up.reshape(up_proj.shape),
        d_down.reshape(down_proj.shape),
    )


def shards(tokens, *others):
    frames = lax.axis_size("frame")
    local = frames == 2 and tokens.shape[0] == 2 and tokens.shape[1] == GROUP
    return (clip_local if local else general)(tokens, *others)


def solution(mesh):
    in_specs = (
        P("clip", "frame", None, None),
        P("clip", "frame", None, None),
        P(("clip", "frame")),
        P(("clip", "frame")),
        P(("clip", "frame")),
        P(("clip", "frame"), None),
        P(("clip", "frame"), None),
        P(("clip", "frame"), None),
        P(("clip", "frame"), None),
        P(("clip", "frame"), None),
        P(("clip", "frame"), None),
    )
    out_specs = (
        P("clip", "frame", None, None),
        P("clip", "frame", None, None),
        P(("clip", "frame")),
        P(("clip", "frame")),
        P(("clip", "frame")),
        P(("clip", "frame"), None),
        P(("clip", "frame"), None),
        P(("clip", "frame"), None),
        P(("clip", "frame"), None),
        P(("clip", "frame"), None),
        P(("clip", "frame"), None),
    )
    return jax.shard_map(shards, mesh=mesh, in_specs=in_specs, out_specs=out_specs, check_vma=False)
```

```python
import functools
import math

import jax
import jax.numpy as jnp
from jax import lax
from jax.experimental import pallas as pl
from jax.experimental.pallas import tpu as pltpu
from jax.sharding import PartitionSpec as P

HEADS = 12
HEAD = 64
PAIRS = HEADS // 2
LANES = 2 * HEAD
epsilon = 1e-06
LOW = jnp.bfloat16
WIDE = jnp.float32
NN = (((1,), (0,)), ((), ()))
NT = (((1,), (1,)), ((), ()))
TN = (((0,), (0,)), ((), ()))
SCALE = HEAD ** (-0.5)
POWER = SCALE * math.log2(math.e)
NEVER = -1e30
GROUP = 8
STEP = 2 * GROUP
LIMIT = 60 << 20
SHRINK = 6
TIME_BATCH = 12
SPACE_BATCH = 6


def dot(first, second, numbers=NN):
    return lax.dot_general(first, second, numbers, preferred_element_type=WIDE)


def norm_rows(values, gain):
    centred = values - jnp.mean(values, axis=-1, keepdims=True)
    inverse = lax.rsqrt(jnp.mean(centred * centred, axis=-1, keepdims=True) + epsilon)
    normed = centred * inverse
    return normed * gain, normed, inverse


def norm_back(gradient, normed, inverse, gain):
    scaled = gradient * gain
    return inverse * (
        scaled
        - jnp.mean(scaled, axis=-1, keepdims=True)
        - normed * jnp.mean(scaled * normed, axis=-1, keepdims=True)
    )


def fold_rows(values):
    rows, width = values.shape
    return jnp.sum(values.reshape(rows // 8, 8, width), axis=0)


def split_heads(values):
    first = lax.broadcasted_iota(jnp.int32, values.shape, 1) < HEAD
    zero = jnp.zeros_like(values)
    return jnp.where(first, values, zero), jnp.where(first, zero, values)


def join_heads(first, second):
    keep = lax.broadcasted_iota(jnp.int32, first.shape, 1) < HEAD
    return jnp.where(keep, first, second)


def stack_heads(values):
    return jnp.concatenate(split_heads(values), axis=0)


def pair(ref, rows, part, index):
    start = (part * PAIRS + index) * LANES
    return ref[rows, start : start + LANES]


def batches(count, size):
    return [range(start, min(start + size, count)) for start in range(0, count, size)]


def time_batches(block):
    spots = [
        (slice(group * block, (group + 1) * block), index)
        for group in range(2)
        for index in range(PAIRS)
    ]
    return [spots[start : start + TIME_BATCH] for start in range(0, len(spots), TIME_BATCH)]


def shares(scores, axis):
    highest = [jnp.max(item, axis=axis, keepdims=True) for item in scores]
    powers = [jnp.exp2((item - top) * POWER) for item, top in zip(scores, highest)]
    totals = [jnp.sum(item, axis=axis, keepdims=True) for item in powers]
    return [item * (1.0 / total) for item, total in zip(powers, totals)]


def score_grads(chances, grads, axis):
    means = [jnp.sum(p * g, axis=axis, keepdims=True) for p, g in zip(chances, grads)]
    return [(p * (g - mean)).astype(LOW) for p, g, mean in zip(chances, grads, means)]


def load_padded(x_ref, pad_ref):
    frames, places, width = x_ref.shape

    @pl.when(pl.program_id(0) == 0)
    def _():
        pad_ref[...] = jnp.zeros_like(pad_ref)

    for frame in range(frames):
        pad_ref[frame, 0:places] = x_ref[frame].astype(WIDE)
    return pad_ref[...].reshape(frames * pad_ref.shape[1], width)


def space_forward_kernel(
    places, x_ref, gain_ref, qk_ref, v_ref, out_ref, in_ref, qkv_ref, o_ref, after_ref, pad_ref
):
    frames, padded, width = pad_ref.shape
    values = load_padded(x_ref, pad_ref)
    normed = norm_rows(values, gain_ref[...])[0].astype(LOW)
    in_ref[...] = normed.reshape(frames, padded, width)
    for start, ref in ((0, qk_ref), (2 * width, v_ref)):
        part = dot(normed, ref[...]).astype(LOW)
        qkv_ref[:, :, start : start + part.shape[1]] = part.reshape(frames, padded, -1)
    real = lax.broadcasted_iota(jnp.int32, (padded, padded), 1) < places

    def one_frame(frame):
        for batch in batches(PAIRS, SPACE_BATCH):
            part = lambda number, index: qkv_ref[
                frame, :, number * width + index * LANES : number * width + (index + 1) * LANES
            ]
            keys = [split_heads(part(1, index)) for index in batch]
            scores = [
                jnp.where(real, dot(part(0, index), key, NT), NEVER)
                for index, both in zip(batch, keys)
                for key in both
            ]
            chances = [item.astype(LOW) for item in shares(scores, 1)]
            outs = [
                dot(chances[2 * slot + head], part(2, index))
                for slot, index in enumerate(batch)
                for head in range(2)
            ]
            for slot, index in enumerate(batch):
                o_ref[frame, :, index * LANES : (index + 1) * LANES] = join_heads(
                    *outs[2 * slot : 2 * slot + 2]
                ).astype(LOW)

    for frame in range(frames):
        one_frame(frame)
    after = values + dot(o_ref[...].reshape(frames * padded, width), out_ref[...])
    after = after.reshape(frames, padded // GROUP, GROUP, width)
    for frame in range(frames):
        after_ref[:, frame] = after[frame].astype(after_ref.dtype)


def middle_kernel(
    places,
    place_ref,
    ao_ref,
    ar_ref,
    go_ref,
    gr_ref,
    tgain_ref,
    fgain_ref,
    tproj_ref,
    tout_ref,
    up_ref,
    down_ref,
    qkv_ref,
    int_ref,
    ot_ref,
    inf_ref,
    act_ref,
    gh_ref,
    gb_ref,
    mo_ref,
    mr_ref,
    gt_ref,
    gain_ref,
):
    half = ao_ref.shape[1]
    frames = half + ar_ref.shape[1]
    width = ao_ref.shape[3]
    rows = 2 * frames * GROUP
    block = frames * GROUP
    values = jnp.concatenate([ao_ref[...].astype(WIDE), ar_ref[...].astype(WIDE)], axis=1).reshape(rows, width)
    in_time = norm_rows(values, tgain_ref[...])[0].astype(LOW)
    int_ref[...] = in_time
    qkv_ref[...] = dot(in_time, tproj_ref[...]).astype(LOW)
    across = lax.broadcasted_iota(jnp.int32, (block, block), 0)
    down = lax.broadcasted_iota(jnp.int32, (block, block), 1)
    bias = jnp.where(((across ^ down) & (GROUP - 1)) == 0, 0.0, NEVER)
    for batch in time_batches(block):
        both = [
            dot(pair(qkv_ref, own, 0, index), stack_heads(pair(qkv_ref, own, 1, index)), NT)
            for own, index in batch
        ]
        scores = [
            item[:, head * block : (head + 1) * block] + bias for item in both for head in range(2)
        ]
        chances = [item.astype(LOW) for item in shares(scores, 1)]
        results = [
            dot(
                jnp.concatenate(chances[2 * slot : 2 * slot + 2], axis=1),
                stack_heads(pair(qkv_ref, own, 2, index)),
            )
            for slot, (own, index) in enumerate(batch)
        ]
        for result, (own, index) in zip(results, batch):
            ot_ref[own, index * LANES : (index + 1) * LANES] = result.astype(LOW)
    values = values + dot(ot_ref[...], tout_ref[...])
    feed_gain = fgain_ref[...]
    in_feed, normed, inverse = norm_rows(values, feed_gain)
    in_feed = in_feed.astype(LOW)
    inf_ref[...] = in_feed
    place = pl.program_id(0) * STEP + lax.broadcasted_iota(jnp.int32, (STEP, width), 0)
    lows, highs = [], []
    for ref in (go_ref, gr_ref):
        for frame in range(half):
            tile = jnp.where(place < places, ref[frame].astype(WIDE), 0.0)
            lows.append(tile[:GROUP])
            highs.append(tile[GROUP:])
    gradient = jnp.concatenate(lows + highs, axis=0)
    grad_low = gradient.astype(LOW)
    gb_ref[...] = grad_low
    hidden_width = up_ref.shape[1]
    root = math.sqrt(2.0 / math.pi)
    cuts = [slice(start, start + width) for start in range(0, hidden_width, width)]

    def products(cut):
        return dot(in_feed, up_ref[:, cut]), dot(grad_low, down_ref[:, cut], NT)

    mixed = values
    ready = products(cuts[0])
    for number, cut in enumerate(cuts):
        hidden, grad_active = ready
        if number + 1 < len(cuts):
            ready = products(cuts[number + 1])
        square = hidden * hidden
        plus = 0.5 * jnp.tanh(hidden * (root + (root * 0.044715) * square)) + 0.5
        active = hidden * plus
        act_ref[:, cut] = active.astype(LOW)
        inner = 2.0 * root + (6.0 * root * 0.044715) * square
        gh_ref[:, cut] = (grad_active * (plus + active * (1.0 - plus) * inner)).astype(LOW)
    for cut in cuts:
        mixed = mixed + dot(act_ref[:, cut], down_ref[:, cut])
    back = dot(gh_ref[...], up_ref[...], NT)
    mixed = mixed.reshape(2, frames, GROUP, width)
    for group in range(2):
        cut = slice(group * GROUP, (group + 1) * GROUP)
        mo_ref[0, cut] = jnp.swapaxes(mixed[group, :half], 0, 1).astype(LOW)
        mr_ref[cut] = jnp.swapaxes(mixed[group, half:], 0, 1).astype(LOW)
    g_time = gradient + norm_back(back, normed, inverse, feed_gain)
    gt_ref[...] = g_time.astype(gt_ref.dtype)

    @pl.when(pl.program_id(0) == 0)
    def _():
        gain_ref[...] = jnp.zeros_like(gain_ref)

    gain_ref[...] += fold_rows(back * normed)


def time_backward_kernel(
    qkv_ref,
    gt_ref,
    ao_ref,
    ar_ref,
    tgain_ref,
    tout_ref,
    tproj_ref,
    gq_ref,
    tb_ref,
    gso_ref,
    gsr_ref,
    gain_ref,
    d_ref,
):
    half = ao_ref.shape[1]
    frames = half + ar_ref.shape[1]
    width = ao_ref.shape[3]
    rows = 2 * frames * GROUP
    block = frames * GROUP
    tb = gt_ref[...].astype(LOW)
    tb_ref[...] = tb
    d_ref[...] = dot(tb, tout_ref[...], NT).astype(LOW)
    across = lax.broadcasted_iota(jnp.int32, (block, block), 0)
    down = lax.broadcasted_iota(jnp.int32, (block, block), 1)
    bias = jnp.where(((across ^ down) & (GROUP - 1)) == 0, 0.0, NEVER)
    for batch in time_batches(block):
        keys = [stack_heads(pair(qkv_ref, own, 1, index)) for own, index in batch]
        both = [dot(key, pair(qkv_ref, own, 0, index), NT) for key, (own, index) in zip(keys, batch)]
        grad_both = [
            dot(stack_heads(pair(qkv_ref, own, 2, index)), pair(d_ref, own, 0, index), NT)
            for own, index in batch
        ]
        cuts = [slice(0, block), slice(block, 2 * block)]
        chances = shares([item[cut] + bias for item in both for cut in cuts], 0)
        grads = score_grads(chances, [item[cut] for item in grad_both for cut in cuts], 0)
        chances = [item.astype(LOW) for item in chances]
        results = []
        for slot, (own, index) in enumerate(batch):
            two = slice(2 * slot, 2 * slot + 2)
            grad = stack_heads(pair(d_ref, own, 0, index))
            queries = stack_heads(pair(qkv_ref, own, 0, index))
            results.append(
                (
                    dot(jnp.concatenate(grads[two], axis=0), keys[slot], TN) * SCALE,
                    dot(jnp.concatenate(grads[two], axis=1), queries) * SCALE,
                    dot(jnp.concatenate(chances[two], axis=1), grad),
                )
            )
        for items, (own, index) in zip(results, batch):
            for part, item in enumerate(items):
                start = (part * PAIRS + index) * LANES
                gq_ref[own, start : start + LANES] = item.astype(LOW)
    values = jnp.concatenate([ao_ref[...].astype(WIDE), ar_ref[...].astype(WIDE)], axis=1).reshape(rows, width)
    gain = tgain_ref[...]
    _, normed, inverse = norm_rows(values, gain)
    back = dot(gq_ref[...], tproj_ref[...], NT)
    result = gt_ref[...].astype(WIDE) + norm_back(back, normed, inverse, gain)
    for frame in range(frames):
        low = result[frame * GROUP : (frame + 1) * GROUP]
        high = result[block + frame * GROUP : block + (frame + 1) * GROUP]
        tile = jnp.concatenate([low, high], axis=0).astype(gso_ref.dtype)
        if frame < half:
            gso_ref[frame] = tile
        else:
            gsr_ref[frame - half] = tile

    @pl.when(pl.program_id(0) == 0)
    def _():
        gain_ref[...] = jnp.zeros_like(gain_ref)

    gain_ref[...] += fold_rows(back * normed)


def space_backward_kernel(
    places,
    place_ref,
    x_ref,
    gs_ref,
    qkv_ref,
    gain_row_ref,
    out_ref,
    qk_ref,
    v_ref,
    gq_ref,
    sb_ref,
    gx_ref,
    gain_ref,
    pad_ref,
    d_ref,
    order_ref,
):
    frames, padded, width = pad_ref.shape
    stride = order_ref.shape[1] // padded
    values = load_padded(x_ref, pad_ref)
    grad_space = gs_ref[...].astype(WIDE).reshape(frames * padded, width)
    sb = grad_space.astype(LOW)
    sb_ref[...] = sb.reshape(frames, padded, width)
    d_ref[...] = dot(sb, out_ref[...], NT).astype(LOW).reshape(frames, padded, width)
    real = lax.broadcasted_iota(jnp.int32, (padded, padded), 0) < places

    def one_frame(frame):
        for batch in batches(PAIRS, SPACE_BATCH):
            part = lambda number, index: qkv_ref[
                frame, :, number * width + index * LANES : number * width + (index + 1) * LANES
            ]
            grad = lambda index: d_ref[frame, :, index * LANES : (index + 1) * LANES]
            heads = [(index, head) for index in batch for head in range(2)]
            scores = [
                jnp.where(real, dot(split_heads(part(1, index))[head], part(0, index), NT), NEVER)
                for index, head in heads
            ]
            grad_shares = [
                dot(split_heads(part(2, index))[head], grad(index), NT) for index, head in heads
            ]
            chances = shares(scores, 0)
            grads = score_grads(chances, grad_shares, 0)
            chances = [item.astype(LOW) for item in chances]
            dq = [dot(ds, part(1, index), TN) * SCALE for ds, (index, _) in zip(grads, heads)]
            dk = [dot(ds, part(0, index)) * SCALE for ds, (index, _) in zip(grads, heads)]
            dv = [dot(p, grad(index)) for p, (index, _) in zip(chances, heads)]
            for number, items in enumerate((dq, dk, dv)):
                for slot, index in enumerate(batch):
                    start = number * width + index * LANES
                    gq_ref[frame, :, start : start + LANES] = join_heads(
                        items[2 * slot], items[2 * slot + 1]
                    ).astype(LOW)

    for frame in range(frames):
        one_frame(frame)
    gain = gain_row_ref[...]
    _, normed, inverse = norm_rows(values, gain)
    back = dot(gq_ref[:, :, : 2 * width].reshape(frames * padded, 2 * width), qk_ref[...], NT)
    back = back + dot(gq_ref[:, :, 2 * width :].reshape(frames * padded, width), v_ref[...], NT)
    result = grad_space + norm_back(back, normed, inverse, gain)
    result = result.reshape(frames, padded, width)
    for frame in range(frames):
        rows = pl.ds(pl.program_id(0) * frames + frame, padded, stride=stride)
        for lane in range(width // LANES):
            order_ref[lane, rows, :] = result[frame, :, lane * LANES : (lane + 1) * LANES]

    @pl.when(pl.program_id(0) == pl.num_programs(0) - 1)
    def _():
        for lane in range(width // LANES):
            tile = order_ref[lane, 0 : places * stride].astype(gx_ref.dtype)
            tile = tile.reshape(places, stride, LANES)
            if len(gx_ref.shape) == 4:
                gx_ref[0, :, :, lane * LANES : (lane + 1) * LANES] = tile
            else:
                gx_ref[:, :, lane * LANES : (lane + 1) * LANES] = tile

    @pl.when(pl.program_id(0) == 0)
    def _():
        gain_ref[...] = jnp.zeros_like(gain_ref)

    gain_ref[...] += fold_rows(back * normed)


def whole(shape):
    return pl.BlockSpec(
        shape, lambda *_: (0,) * len(shape), pipeline_mode=pl.Buffered(buffer_count=1)
    )


def columns(array, width, index):
    return pl.BlockSpec(
        (array.shape[0], width),
        lambda *_: (0, index),
        pipeline_mode=pl.Buffered(buffer_count=1),
    )


def params():
    return pltpu.CompilerParams(vmem_limit_bytes=LIMIT)


def cost(flops, *arrays):
    size = sum(math.prod(item.shape) * jnp.dtype(item.dtype).itemsize for item in arrays)
    return pl.CostEstimate(
        flops=int(flops) // SHRINK, bytes_accessed=int(size) // SHRINK, transcendentals=0
    )


def padded_places(places):
    return -(-places // STEP) * STEP


def by_frame(count, *tail):
    return pl.BlockSpec((count,) + tail, lambda step, *_: (step,) + (0,) * len(tail))


def space_forward(x, gain, first, second):
    frames, places, width = x.shape
    padded = padded_places(places)
    groups = padded // GROUP
    rows = frames * padded
    outs = (
        jax.ShapeDtypeStruct((frames, padded, width), LOW),
        jax.ShapeDtypeStruct((frames, padded, 3 * width), LOW),
        jax.ShapeDtypeStruct((frames, padded, width), LOW),
        jax.ShapeDtypeStruct((groups, frames, GROUP, width), WIDE),
    )
    flops = 2 * rows * width * 4 * width + 8 * rows * padded * width
    return pl.pallas_call(
        functools.partial(space_forward_kernel, places),
        grid=(frames // 2,),
        in_specs=[
            by_frame(2, places, width),
            whole(gain.shape),
            whole(first.shape),
            columns(second, width, 0),
            columns(second, width, 1),
        ],
        out_specs=[
            by_frame(2, padded, width),
            by_frame(2, padded, 3 * width),
            by_frame(2, padded, width),
            pl.BlockSpec((groups, 2, GROUP, width), lambda step: (0, step, 0, 0)),
        ],
        out_shape=outs,
        scratch_shapes=[pltpu.VMEM((2, padded, width), WIDE)],
        compiler_params=params(),
        cost_estimate=cost(flops, x, first, second, *outs),
        name="space_forward",
    )(x, gain, first, second, second)


def middle(place, after_own, after_rest, g_own, g_rest, tgain, fgain, packed):
    groups, half, _, width = after_own.shape
    places = g_own.shape[1]
    frames = 2 * half
    rows = groups * frames * GROUP
    block = 2 * frames * GROUP
    hidden = (packed.shape[1] - 4 * width) // 2
    padded = groups * GROUP
    outs = (
        jax.ShapeDtypeStruct((rows, 3 * width), LOW),
        jax.ShapeDtypeStruct((rows, width), LOW),
        jax.ShapeDtypeStruct((rows, width), LOW),
        jax.ShapeDtypeStruct((rows, width), LOW),
        jax.ShapeDtypeStruct((rows, hidden), LOW),
        jax.ShapeDtypeStruct((rows, hidden), LOW),
        jax.ShapeDtypeStruct((rows, width), LOW),
        jax.ShapeDtypeStruct((2, places, half, width), LOW),
        jax.ShapeDtypeStruct((places, half, width), LOW),
        jax.ShapeDtypeStruct((rows, width), WIDE),
        jax.ShapeDtypeStruct((8, width), WIDE),
    )
    by_row = lambda size: pl.BlockSpec((block, size), lambda step, place: (step, 0))
    by_group = pl.BlockSpec((2, half, GROUP, width), lambda step, place: (step, 0, 0, 0))
    by_place = pl.BlockSpec((half, STEP, width), lambda step, place: (0, step, 0))
    flops = 2 * rows * width * (4 * width + 4 * hidden) + 8 * rows * frames * GROUP * width
    return pl.pallas_call(
        functools.partial(middle_kernel, places),
        grid_spec=pltpu.PrefetchScalarGridSpec(
            num_scalar_prefetch=1,
            grid=(groups // 2,),
            in_specs=[by_group, by_group, by_place, by_place]
            + [
                whole(tgain.shape),
                whole(fgain.shape),
                columns(packed, 3 * width, 0),
                columns(packed, width, 3),
                columns(packed, hidden, 1),
                columns(packed, hidden, 2),
            ],
            out_specs=[
                by_row(3 * width),
                by_row(width),
                by_row(width),
                by_row(width),
                by_row(hidden),
                by_row(hidden),
                by_row(width),
                pl.BlockSpec((1, STEP, half, width), lambda step, place: (place[0], step, 0, 0)),
                pl.BlockSpec((STEP, half, width), lambda step, place: (step, 0, 0)),
                by_row(width),
                pl.BlockSpec((8, width), lambda step, place: (0, 0)),
            ],
        ),
        out_shape=outs,
        compiler_params=params(),
        cost_estimate=cost(flops, after_own, after_rest, g_own, g_rest, *outs),
        name="middle",
    )(place, after_own, after_rest, g_own, g_rest, tgain, fgain, packed, packed, packed, packed)


def time_backward(qkv, g_time, after_own, after_rest, tgain, packed):
    groups, half, _, width = after_own.shape
    frames = 2 * half
    rows = groups * frames * GROUP
    block = 2 * frames * GROUP
    padded = groups * GROUP
    outs = (
        jax.ShapeDtypeStruct((rows, 3 * width), LOW),
        jax.ShapeDtypeStruct((rows, width), LOW),
        jax.ShapeDtypeStruct((half, padded, width), WIDE),
        jax.ShapeDtypeStruct((half, padded, width), WIDE),
        jax.ShapeDtypeStruct((8, width), WIDE),
    )
    by_row = lambda size: pl.BlockSpec((block, size), lambda step: (step, 0))
    by_group = pl.BlockSpec((2, half, GROUP, width), lambda step: (step, 0, 0, 0))
    by_place = pl.BlockSpec((half, STEP, width), lambda step: (0, step, 0))
    flops = 2 * rows * width * 4 * width + 20 * rows * frames * GROUP * width
    return pl.pallas_call(
        time_backward_kernel,
        grid=(groups // 2,),
        in_specs=[by_row(3 * width), by_row(width), by_group, by_group]
        + [whole(tgain.shape), columns(packed, width, 3), columns(packed, 3 * width, 0)],
        out_specs=[
            by_row(3 * width),
            by_row(width),
            by_place,
            by_place,
            pl.BlockSpec((8, width), lambda step: (0, 0)),
        ],
        out_shape=outs,
        scratch_shapes=[pltpu.VMEM((block, width), LOW)],
        compiler_params=params(),
        cost_estimate=cost(flops, qkv, g_time, after_own, after_rest, *outs),
        name="time_backward",
    )(qkv, g_time, after_own, after_rest, tgain, packed, packed)


def space_backward(place, x, g_space, qkv, gain, first, second, kind):
    frames, places, width = x.shape
    padded = padded_places(places)
    rows = frames * padded
    own = kind == WIDE
    shape = (2, places, frames, width) if own else (places, frames, width)
    outs = (
        jax.ShapeDtypeStruct((frames, padded, 3 * width), LOW),
        jax.ShapeDtypeStruct((frames, padded, width), LOW),
        jax.ShapeDtypeStruct(shape, kind),
        jax.ShapeDtypeStruct((8, width), WIDE),
    )
    flops = 2 * rows * width * 4 * width + 20 * rows * padded * width
    return pl.pallas_call(
        functools.partial(space_backward_kernel, places),
        grid_spec=pltpu.PrefetchScalarGridSpec(
            num_scalar_prefetch=1,
            grid=(frames // 2,),
            in_specs=[
                by_frame(2, places, width),
                by_frame(2, padded, width),
                by_frame(2, padded, 3 * width),
                whole(gain.shape),
                columns(second, width, 1),
                whole(first.shape),
                columns(second, width, 0),
            ],
            out_specs=[
                by_frame(2, padded, 3 * width),
                by_frame(2, padded, width),
                pl.BlockSpec((1,) + shape[1:], lambda step, place: (place[0], 0, 0, 0))
                if own
                else pl.BlockSpec(shape, lambda step, place: (0, 0, 0)),
                pl.BlockSpec((8, width), lambda step, place: (0, 0)),
            ],
            scratch_shapes=[
                pltpu.VMEM((2, padded, width), WIDE),
                pltpu.VMEM((2, padded, width), LOW),
                pltpu.VMEM((width // LANES, padded * frames, LANES), WIDE),
            ],
        ),
        out_shape=outs,
        compiler_params=params(),
        cost_estimate=cost(flops, x, g_space, qkv, *outs),
        name="space_backward",
    )(place, x, g_space, qkv, gain, second, first, second)


def gradient_kernel(parts, tiles, core_ref, *refs):
    step = pl.program_id(0)

    def emit(pairs):
        total = dot(pairs[0][0][...], pairs[0][1][...], TN)
        for first, second in pairs[1:]:
            total = total + dot(first[...], second[...], TN)
        if core_ref is None:
            refs[-1][...] = total.astype(LOW)
            return
        keep_ref, send_ref = refs[-2:]
        total = total.reshape(keep_ref.shape[0], 2, keep_ref.shape[1], keep_ref.shape[2])
        total = total.astype(LOW)
        keep = core_ref[0] == 0
        keep_ref[...] = jnp.where(keep, total[:, 0], total[:, 1])
        send_ref[...] = jnp.where(keep, total[:, 1], total[:, 0])

    start = 0
    for (first, last), count in zip(tiles, parts):
        group = refs[start : start + 2 * count]
        start += 2 * count
        pairs = [(group[2 * index], group[2 * index + 1]) for index in range(count)]
        pl.when((step >= first) & (step < last))(functools.partial(emit, pairs))


def plan_gradient(groups):
    width = groups[0][0][0][0].shape[1] if groups[0][3] == 1 else groups[0][0][0][1].shape[1]
    count = groups[-1][2]
    specs, arrays, parts, tiles = [], [], [], []
    flops = 0
    for pairs, first, last, side, offset in groups:
        parts.append(len(pairs))
        tiles.append((first, last))
        for pair_arrays in pairs:
            for index, item in enumerate(pair_arrays):
                rows = item.shape[0]
                if index == side and last - first > 1:
                    spec = pl.BlockSpec(
                        (rows, width),
                        lambda step, *_, first=first, last=last, offset=offset: (
                            0,
                            jnp.clip(step - first, 0, last - first - 1) + offset,
                        ),
                    )
                else:
                    fixed = offset if index == side else 0
                    spec = pl.BlockSpec(
                        (rows, width),
                        lambda step, *_, fixed=fixed: (0, fixed),
                        pipeline_mode=pl.Buffered(buffer_count=1),
                    )
                specs.append(spec)
                arrays.append(item)
            flops += 2 * rows * width * width * (last - first)
    return width, count, specs, arrays, parts, tiles, flops


def weight_gradient(*groups):
    width, count, specs, arrays, parts, tiles, flops = plan_gradient(groups)
    out = jax.ShapeDtypeStruct((width, count * width), LOW)
    return pl.pallas_call(
        functools.partial(gradient_kernel, parts, tiles, None),
        grid=(count,),
        in_specs=specs,
        out_specs=pl.BlockSpec((width, width), lambda step: (0, step)),
        out_shape=out,
        compiler_params=params(),
        cost_estimate=cost(flops, *arrays, out),
        name="weight_gradient",
    )(*arrays)


def split_gradient(core, owners, *groups):
    width, count, specs, arrays, parts, tiles, flops = plan_gradient(groups)
    blocks, rows = owners // 4, 2 * (width // owners)
    out = jax.ShapeDtypeStruct((blocks, rows, count * width), LOW)
    out_spec = pl.BlockSpec((blocks, rows, width), lambda step, core: (0, 0, step))
    return pl.pallas_call(
        functools.partial(gradient_kernel, parts, tiles),
        grid_spec=pltpu.PrefetchScalarGridSpec(
            num_scalar_prefetch=1,
            grid=(count,),
            in_specs=specs,
            out_specs=[out_spec, out_spec],
        ),
        out_shape=[out, out],
        compiler_params=params(),
        cost_estimate=cost(flops, *arrays, out, out),
        name="split_gradient",
    )(core, *arrays)


MICRO = 2


def norm_forward(values, gain):
    centred = values - jnp.mean(values, axis=-1, keepdims=True)
    inverse = lax.rsqrt(jnp.mean(centred * centred, axis=-1, keepdims=True) + epsilon)
    normed = centred * inverse
    return (normed * gain, normed, inverse)


def norm_backward(gradient, normed, inverse, gain):
    gain_grad = jnp.sum(gradient * normed, axis=(0, 1, 2))
    scaled = gradient * gain
    centred_grad = (
        scaled
        - jnp.mean(scaled, axis=-1, keepdims=True)
        - normed * jnp.mean(scaled * normed, axis=-1, keepdims=True)
    )
    return (inverse * centred_grad, gain_grad)


def to_places(blocks):
    clip_count, frames, places, model_width = blocks.shape
    return blocks.transpose(0, 2, 1, 3).reshape(clip_count * places, frames, HEADS, HEAD)


def from_places(attended, clip_count, places):
    frames = attended.shape[1]
    return attended.reshape(clip_count, places, frames, HEADS * HEAD).transpose(0, 2, 1, 3)


def attend_forward(queries, key_block, value_block):
    factor = HEAD ** (-0.5)
    scores = (
        jnp.einsum("blhe,bmhe->bhlm", queries, key_block, preferred_element_type=jnp.float32)
        * factor
    )
    highest = jnp.max(scores, axis=-1, keepdims=True)
    powers = jnp.exp(scores - highest)
    row_total = jnp.sum(powers, axis=-1, keepdims=True)
    chances = (powers / row_total).astype(jnp.bfloat16)
    result = jnp.einsum("bhlm,bmhe->blhe", chances, value_block, preferred_element_type=jnp.float32)
    return (result, highest + jnp.log(row_total))


def attend_backward(queries, key_block, value_block, logsum, grad_out):
    factor = HEAD ** (-0.5)
    scores = (
        jnp.einsum("blhe,bmhe->bhlm", queries, key_block, preferred_element_type=jnp.float32)
        * factor
    )
    chances = jnp.exp(scores - logsum)
    grad_chances = jnp.einsum(
        "blhe,bmhe->bhlm", grad_out, value_block, preferred_element_type=jnp.float32
    )
    grad_scores = (
        chances * (grad_chances - jnp.sum(chances * grad_chances, axis=-1, keepdims=True))
    ).astype(jnp.bfloat16)
    grad_queries = (
        jnp.einsum("bhlm,bmhe->blhe", grad_scores, key_block, preferred_element_type=jnp.float32)
        * factor
    )
    grad_keys = (
        jnp.einsum("bhlm,blhe->bmhe", grad_scores, queries, preferred_element_type=jnp.float32)
        * factor
    )
    grad_values = jnp.einsum(
        "bhlm,blhe->bmhe",
        chances.astype(jnp.bfloat16),
        grad_out,
        preferred_element_type=jnp.float32,
    )
    return (grad_queries, grad_keys, grad_values)


def project(values, matrix):
    return jnp.einsum("cfpd,de->cfpe", values, matrix, preferred_element_type=jnp.float32)


def project_back(gradient, matrix):
    return jnp.einsum("cfpe,de->cfpd", gradient, matrix, preferred_element_type=jnp.float32)


def outer_sum(values, gradient):
    return jnp.einsum("cfpd,cfpe->de", values, gradient, preferred_element_type=jnp.float32)


def forward(sample, gathered):
    (
        space_gain,
        time_gain,
        feed_gain,
        space_proj,
        space_out,
        time_proj,
        time_out,
        up_proj,
        down_proj,
    ) = gathered
    clip_count, frames, places, model_width = sample.shape
    normed_space = norm_forward(sample, space_gain.astype(jnp.float32))
    in_space = normed_space[0].astype(jnp.bfloat16)
    qkv_space = project(in_space, space_proj).astype(jnp.bfloat16)
    parted = qkv_space.reshape(clip_count * frames, places, 3, HEADS, HEAD)
    attended, logsum_space = attend_forward(parted[:, :, 0], parted[:, :, 1], parted[:, :, 2])
    out_space = attended.reshape(clip_count, frames, places, model_width).astype(jnp.bfloat16)
    after_space = sample + project(out_space, space_out)
    normed_time = norm_forward(after_space, time_gain.astype(jnp.float32))
    in_time = normed_time[0].astype(jnp.bfloat16)
    qkv_time = project(in_time, time_proj).astype(jnp.bfloat16)
    kv_whole = lax.all_gather(qkv_time[..., model_width:], "frame", axis=1, tiled=True)
    attended, logsum_time = attend_forward(
        to_places(qkv_time[..., :model_width]),
        to_places(kv_whole[..., :model_width]),
        to_places(kv_whole[..., model_width:]),
    )
    out_time = from_places(attended, clip_count, places).astype(jnp.bfloat16)
    after_time = after_space + project(out_time, time_out)
    normed_feed = norm_forward(after_time, feed_gain.astype(jnp.float32))
    in_feed = normed_feed[0].astype(jnp.bfloat16)
    hidden = project(in_feed, up_proj)
    active = jax.nn.gelu(hidden).astype(jnp.bfloat16)
    result = after_time + project(active, down_proj)
    saved = (
        normed_space,
        in_space,
        qkv_space,
        logsum_space,
        out_space,
        normed_time,
        in_time,
        qkv_time,
        kv_whole,
        logsum_time,
        out_time,
        normed_feed,
        in_feed,
        hidden,
        active,
    )
    return (result, saved)


def backward(gradient, saved, gathered):
    (
        space_gain,
        time_gain,
        feed_gain,
        space_proj,
        space_out,
        time_proj,
        time_out,
        up_proj,
        down_proj,
    ) = gathered
    (
        normed_space,
        in_space,
        qkv_space,
        logsum_space,
        out_space,
        normed_time,
        in_time,
        qkv_time,
        time_side,
        logsum_time,
        out_time,
        normed_feed,
        in_feed,
        hidden,
        active,
    ) = saved
    clip_count, frames, places, model_width = gradient.shape
    grad_low = gradient.astype(jnp.bfloat16)
    grad_down = outer_sum(active, grad_low)
    grad_active = project_back(grad_low, down_proj)
    gelu_value, gelu_pull = jax.vjp(jax.nn.gelu, hidden)
    grad_hidden = gelu_pull(grad_active)[0].astype(jnp.bfloat16)
    grad_up = outer_sum(in_feed, grad_hidden)
    back_feed, grad_feed_gain = norm_backward(
        project_back(grad_hidden, up_proj),
        normed_feed[1],
        normed_feed[2],
        feed_gain.astype(jnp.float32),
    )
    grad_time = gradient + back_feed
    time_low = grad_time.astype(jnp.bfloat16)
    grad_tout = outer_sum(out_time, time_low)
    grad_out_time = project_back(time_low, time_out).astype(jnp.bfloat16)
    grad_queries, grad_keys, grad_values = attend_backward(
        to_places(qkv_time[..., :model_width]),
        to_places(time_side[..., :model_width]),
        to_places(time_side[..., model_width:]),
        logsum_time,
        to_places(grad_out_time),
    )
    grad_kv = jnp.concatenate(
        (from_places(grad_keys, clip_count, places), from_places(grad_values, clip_count, places)),
        axis=-1,
    )
    grad_kv_own = lax.psum_scatter(
        grad_kv.astype(jnp.bfloat16), "frame", scatter_dimension=1, tiled=True
    ).astype(jnp.float32)
    grad_qkv_time = jnp.concatenate(
        (from_places(grad_queries, clip_count, places), grad_kv_own), axis=-1
    ).astype(jnp.bfloat16)
    grad_tproj = outer_sum(in_time, grad_qkv_time)
    back_time, grad_time_gain = norm_backward(
        project_back(grad_qkv_time, time_proj),
        normed_time[1],
        normed_time[2],
        time_gain.astype(jnp.float32),
    )
    grad_space = grad_time + back_time
    space_low = grad_space.astype(jnp.bfloat16)
    grad_sout = outer_sum(out_space, space_low)
    grad_out_space = project_back(space_low, space_out).astype(jnp.bfloat16)
    parted = qkv_space.reshape(clip_count * frames, places, 3, HEADS, HEAD)
    grad_queries, grad_keys, grad_values = attend_backward(
        parted[:, :, 0],
        parted[:, :, 1],
        parted[:, :, 2],
        logsum_space,
        grad_out_space.reshape(clip_count * frames, places, HEADS, HEAD),
    )
    grad_qkv_space = (
        jnp.stack((grad_queries, grad_keys, grad_values), axis=2)
        .reshape(clip_count, frames, places, 3 * model_width)
        .astype(jnp.bfloat16)
    )
    grad_sproj = outer_sum(in_space, grad_qkv_space)
    back_space, grad_space_gain = norm_backward(
        project_back(grad_qkv_space, space_proj),
        normed_space[1],
        normed_space[2],
        space_gain.astype(jnp.float32),
    )
    grad_input = grad_space + back_space
    return (
        grad_input,
        (
            grad_space_gain,
            grad_time_gain,
            grad_feed_gain,
            grad_sproj,
            grad_sout,
            grad_tproj,
            grad_tout,
            grad_up,
            grad_down,
        ),
    )


def general(
    tokens,
    cotangent,
    space_gain,
    time_gain,
    feed_gain,
    space_proj,
    space_out,
    time_proj,
    time_out,
    up_proj,
    down_proj,
):
    owned = (
        space_gain,
        time_gain,
        feed_gain,
        space_proj,
        space_out,
        time_proj,
        time_out,
        up_proj,
        down_proj,
    )
    devices_all = lax.axis_size(("clip", "frame"))
    per_micro = tokens.shape[0] // MICRO
    totals = tuple(
        (
            jnp.zeros((piece.shape[0] * devices_all,) + piece.shape[1:], jnp.float32)
            for piece in owned
        )
    )
    gathered = (
        lax.all_gather(space_gain, ("clip", "frame"), axis=0, tiled=True),
        lax.all_gather(time_gain, ("clip", "frame"), axis=0, tiled=True),
        lax.all_gather(feed_gain, ("clip", "frame"), axis=0, tiled=True),
        lax.all_gather(space_proj, ("clip", "frame"), axis=0, tiled=True),
        lax.all_gather(space_out, ("clip", "frame"), axis=0, tiled=True),
        lax.all_gather(time_proj, ("clip", "frame"), axis=0, tiled=True),
        lax.all_gather(time_out, ("clip", "frame"), axis=0, tiled=True),
        lax.all_gather(up_proj, ("clip", "frame"), axis=0, tiled=True),
        lax.all_gather(down_proj, ("clip", "frame"), axis=0, tiled=True),
    )
    mixed_parts = []
    grad_parts = []
    for micro_index in range(MICRO):
        sample = tokens[micro_index * per_micro : (micro_index + 1) * per_micro].astype(jnp.float32)
        result, saved = forward(sample, gathered)
        mixed_parts.append(result.astype(jnp.bfloat16))
        gradient = cotangent[micro_index * per_micro : (micro_index + 1) * per_micro].astype(
            jnp.float32
        )
        grad_input, grads = backward(gradient, saved, gathered)
        grad_parts.append(grad_input)
        totals = tuple((first + second for first, second in zip(totals, grads)))
    flat = tuple((item.reshape(-1) for item in totals))
    owners = (
        lax.psum_scatter(flat[0], ("clip", "frame"), scatter_dimension=0, tiled=True),
        lax.psum_scatter(flat[1], ("clip", "frame"), scatter_dimension=0, tiled=True),
        lax.psum_scatter(flat[2], ("clip", "frame"), scatter_dimension=0, tiled=True),
        lax.psum_scatter(flat[3], ("clip", "frame"), scatter_dimension=0, tiled=True),
        lax.psum_scatter(flat[4], ("clip", "frame"), scatter_dimension=0, tiled=True),
        lax.psum_scatter(flat[5], ("clip", "frame"), scatter_dimension=0, tiled=True),
        lax.psum_scatter(flat[6], ("clip", "frame"), scatter_dimension=0, tiled=True),
        lax.psum_scatter(flat[7], ("clip", "frame"), scatter_dimension=0, tiled=True),
        lax.psum_scatter(flat[8], ("clip", "frame"), scatter_dimension=0, tiled=True),
    )
    shaped = tuple((piece.reshape(mine.shape) for piece, mine in zip(owners, owned)))
    mixed = jnp.concatenate(mixed_parts, axis=0)
    grad_tokens = jnp.concatenate(grad_parts, axis=0)
    return (
        mixed,
        grad_tokens,
        shaped[0],
        shaped[1],
        shaped[2],
        shaped[3],
        shaped[4],
        shaped[5],
        shaped[6],
        shaped[7],
        shaped[8],
    )


def swap_axis(values, axis):
    size = lax.axis_size(axis)
    return lax.ppermute(values, axis, [(index, size - 1 - index) for index in range(size)])


def flip(values, mask):
    size = lax.axis_size("clip")
    return lax.ppermute(values, "clip", [(index, index ^ mask) for index in range(size)])


def tie(*items):
    return lax.optimization_barrier(items)


def bit_of(mask):
    return (lax.axis_index("clip") // mask) % 2


def in_order(bit, mine, other, axis):
    return jnp.where(
        bit == 0, jnp.stack([mine, other], axis=axis), jnp.stack([other, mine], axis=axis)
    )


def pick(values, index, axis):
    return lax.dynamic_index_in_dim(values, index, axis, keepdims=False)


def added(*items):
    return sum(item.astype(WIDE) for item in items)


def collect_start(shard):
    return in_order(lax.axis_index("frame"), shard, swap_axis(shard, "frame"), 0)


def collect_lines(item):
    line = lax.axis_index("clip") // 4
    parts = [item] + [flip(item, 4 * step) for step in range(1, 4)]
    odd, far = line % 2, line // 2
    parts = [jnp.where(odd == 0, parts[index], parts[index ^ 1]) for index in range(4)]
    parts = [jnp.where(far == 0, parts[index], parts[index ^ 2]) for index in range(4)]
    return jnp.stack(parts, axis=0)


def collect_half(item, mask, axis):
    return in_order(bit_of(mask), item, flip(item, mask), axis)


def merged(item):
    return item.reshape(-1, item.shape[-1])


def scatter_core(keep, send):
    return keep, flip(send, 1)


def column_parts(keep, other):
    shape = (4, 2) + keep.shape[1:]
    keep, other = keep.reshape(shape), other.reshape(shape)
    bit = bit_of(2)
    send = added(pick(keep, 1 - bit, 1), pick(other, 1 - bit, 1)).astype(LOW)
    return added(pick(keep, bit, 1), pick(other, bit, 1)).astype(LOW), send


def scatter_columns(keep, other):
    keep, send = column_parts(keep, other)
    return keep, flip(send, 2)


def scatter_lines(keep, other):
    line = lax.axis_index("clip") // 4
    total = added(keep, other).astype(LOW)
    parts = [flip(pick(total, line ^ step, 0), 4 * step) for step in range(1, 4)]
    return (pick(total, line, 0), *parts)


def scatter_frames(*parts):
    total = added(*parts).astype(LOW)
    total = total.reshape(2, total.shape[0] // 2, total.shape[1])
    place = lax.axis_index("frame")
    return pick(total, place, 0), swap_axis(pick(total, 1 - place, 0), "frame")


def flat_rows(values):
    return values.reshape(-1, values.shape[-1])


def clip_local(
    tokens,
    cotangent,
    space_gain,
    time_gain,
    feed_gain,
    space_proj,
    space_out,
    time_proj,
    time_out,
    up_proj,
    down_proj,
):
    axes = ("clip", "frame")
    place = lax.axis_index("frame")
    owners = lax.axis_size(axes)
    share, width = space_out.shape
    blocks = down_proj.shape[0] // share
    core = bit_of(1).reshape(1)
    spot = place.reshape(1)

    gains = jnp.stack([space_gain, time_gain, feed_gain], axis=1)
    gains = jnp.pad(gains, ((0, 0), (0, LANES - 3)))
    first = collect_start(space_proj[:, : 2 * width])
    second = collect_start(
        jnp.concatenate([space_proj[:, 2 * width :], space_out, gains], axis=1)
    )
    up_order = up_proj.reshape(share, owners, blocks, share).transpose(0, 2, 1, 3)
    down_order = down_proj.reshape(blocks, share, width).transpose(1, 0, 2)
    packed = jnp.concatenate(
        [time_proj, time_out, up_order.reshape(share, -1), down_order.reshape(share, -1)], axis=1
    )
    first, second, by_place, packed = tie(first, second, tokens.transpose(0, 2, 1, 3), packed)
    packed = lax.all_gather(packed, axes, axis=0, tiled=True)
    half = by_place.shape[1] // 2
    send = pick(by_place, 1 - place, 0)
    rest_a = swap_axis(send[:half], "frame")
    first = collect_lines(first)
    second, first, rest_a, send = tie(second, first, rest_a, send)
    rest_b = swap_axis(send[half:], "frame")
    second = collect_lines(second)
    first = collect_half(first, 2, 1)
    own, g_own = pick(tokens, place, 0), pick(cotangent, place, 0)
    first, second, own, g_own = tie(first, second, own, g_own)
    second = collect_half(second, 2, 1)
    second, rest_b, g_send = tie(second, rest_b, cotangent.transpose(0, 2, 1, 3))
    g_rest = swap_axis(pick(g_send, 1 - place, 0), "frame")
    first = merged(collect_half(first, 1, 2))
    second = merged(collect_half(second, 1, 2))
    rest = jnp.concatenate([rest_a, rest_b], axis=0).transpose(1, 0, 2)
    table = second[:, 2 * width : 2 * width + 3].astype(WIDE).T
    sgain, tgain, fgain = (table[index : index + 1] for index in range(3))
    in_o, qkv_o, o_o, after_o = space_forward(own, sgain, first, second)
    rest, after_o = tie(rest, after_o)
    in_r, qkv_r, o_r, after_r = space_forward(rest, sgain, first, second)
    g_rest, after_r = tie(g_rest, after_r)
    g_rest = g_rest.transpose(1, 0, 2)
    qkv_t, in_t, o_t, in_f, act, gh, gb, mixed, mixed_r, g_time, gain_f = middle(
        spot, after_o, after_r, g_own, g_rest, tgain, fgain, packed
    )
    mixed_other = swap_axis(mixed_r, "frame")
    scatter = lambda item: lax.psum_scatter(item, axes, scatter_dimension=0, tiled=True)
    d_feed = weight_gradient(
        ([(in_f, gh)], 0, blocks, 1, 0), ([(act, gb)], blocks, 2 * blocks, 0, 0)
    )
    d_feed, g_time = tie(d_feed, g_time)
    d_feed = scatter(d_feed)
    gq_t, tb, gs_o, gs_r, gain_t = time_backward(
        qkv_t, g_time, after_o, after_r, tgain, packed
    )
    d_time = split_gradient(
        core, owners, ([(in_t, gq_t)], 0, 3, 1, 0), ([(o_t, tb)], 3, 4, 1, 0)
    )
    d_time, gs_r, mixed_other = tie(d_time, gs_r, mixed_other)
    d_time = scatter_columns(*scatter_core(*d_time))
    gq_r, sb_r, gx_r, gain_sr = space_backward(spot, rest, gs_r, qkv_r, sgain, first, second, LOW)
    grad_a = swap_axis(gx_r[:half], "frame")
    grad_b = swap_axis(gx_r[half:], "frame")
    d_time, gs_o, sb_r = tie(d_time, gs_o, sb_r)
    d_time = scatter_lines(*d_time)
    gq_o, sb_o, grad_tokens, gain_so = space_backward(spot, own, gs_o, qkv_o, sgain, first, second, WIDE)
    d_time, gq_o, sb_o, grad_a = tie(d_time, gq_o, sb_o, grad_a)
    gain_grads = jnp.stack(
        [jnp.sum(item, axis=0) for item in (gain_so + gain_sr, gain_t, gain_f)], axis=1
    )
    gain_grads = jnp.pad(gain_grads, ((0, 0), (0, LANES - 3))).astype(LOW)
    gain_grads = gain_grads.reshape(owners // 4, 2, 2 * share, LANES)
    gain_grads = [pick(gain_grads, side, 1) for side in (core[0], 1 - core[0])]
    inputs = [(flat_rows(in_o), flat_rows(gq_o)), (flat_rows(in_r), flat_rows(gq_r))]
    d_first = scatter_core(*split_gradient(core, owners, (inputs, 0, 3, 1, 0)))
    first_keep, first_send = column_parts(*d_first)
    first_keep, first_send, o_o = tie(first_keep, first_send, o_o)
    d_first = first_keep, flip(first_send, 2)
    outputs = [(flat_rows(o_o), flat_rows(sb_o)), (flat_rows(o_r), flat_rows(sb_r))]
    d_second = split_gradient(core, owners, (outputs, 0, 1, 1, 0))
    d_second = [
        jnp.concatenate([item, gain], axis=2) for item, gain in zip(d_second, gain_grads)
    ]
    d_second = scatter_core(*d_second)
    d_first, d_second, d_time, mixed_other, grad_a, grad_b, d_feed = tie(
        d_first, d_second, d_time, mixed_other, grad_a, grad_b, d_feed
    )
    d_first = scatter_lines(*d_first)
    d_second = scatter_columns(*d_second)
    d_time = scatter_frames(*d_time)
    d_feed = d_feed.astype(WIDE)
    d_up, d_down = d_feed[:, : blocks * width], d_feed[:, blocks * width :]
    d_up = d_up.reshape(share, blocks, owners, share).transpose(0, 2, 1, 3)
    d_up = d_up.reshape(up_proj.shape)
    d_down = d_down.reshape(share, blocks, width).transpose(1, 0, 2).reshape(down_proj.shape)
    mixed = lax.dynamic_update_index_in_dim(mixed, mixed_other, 1 - place, 0)
    for start, item in ((0, grad_a), (half, grad_b)):
        grad_tokens = lax.dynamic_update_slice(
            grad_tokens, item.astype(WIDE)[None], (1 - place, start, 0, 0)
        )
    d_first, mixed, grad_tokens, d_up, d_down = tie(d_first, mixed, grad_tokens, d_up, d_down)
    d_first = scatter_frames(*d_first)
    d_second = scatter_frames(*scatter_lines(*d_second))
    d_first, d_second, d_time = (added(*item) for item in (d_first, d_second, d_time))
    mixed, grad_tokens = mixed.transpose(0, 2, 1, 3), grad_tokens.transpose(0, 2, 1, 3)
    return (
        mixed,
        grad_tokens,
        d_second[:, width],
        d_second[:, width + 1],
        d_second[:, width + 2],
        d_first,
        d_second[:, :width],
        d_time[:, : 3 * width],
        d_time[:, 3 * width :],
        d_up,
        d_down,
    )


def shards(tokens, *others):
    frames = lax.axis_size("frame")
    local = frames == 2 and tokens.shape[0] == 2 and tokens.shape[1] == GROUP
    return (clip_local if local else general)(tokens, *others)


def solution(mesh):
    in_specs = (
        P("clip", "frame", None, None),
        P("clip", "frame", None, None),
        P(("clip", "frame")),
        P(("clip", "frame")),
        P(("clip", "frame")),
        P(("clip", "frame"), None),
        P(("clip", "frame"), None),
        P(("clip", "frame"), None),
        P(("clip", "frame"), None),
        P(("clip", "frame"), None),
        P(("clip", "frame"), None),
    )
    out_specs = (
        P("clip", "frame", None, None),
        P("clip", "frame", None, None),
        P(("clip", "frame")),
        P(("clip", "frame")),
        P(("clip", "frame")),
        P(("clip", "frame"), None),
        P(("clip", "frame"), None),
        P(("clip", "frame"), None),
        P(("clip", "frame"), None),
        P(("clip", "frame"), None),
        P(("clip", "frame"), None),
    )
    return jax.shard_map(shards, mesh=mesh, in_specs=in_specs, out_specs=out_specs, check_vma=False)
```

```python
import functools
import math

import jax
import jax.numpy as jnp
from jax import lax
from jax.experimental import pallas as pl
from jax.experimental.pallas import tpu as pltpu
from jax.sharding import PartitionSpec as P

HEADS = 12
HEAD = 64
PAIRS = HEADS // 2
LANES = 2 * HEAD
epsilon = 1e-06
LOW = jnp.bfloat16
WIDE = jnp.float32
NN = (((1,), (0,)), ((), ()))
NT = (((1,), (1,)), ((), ()))
TN = (((0,), (0,)), ((), ()))
SCALE = HEAD ** (-0.5)
POWER = SCALE * math.log2(math.e)
NEVER = -1e30
GROUP = 8
STEP = 2 * GROUP
LIMIT = 60 << 20
SHRINK = 6
TIME_BATCH = 12
SPACE_BATCH = 6


def dot(first, second, numbers=NN):
    return lax.dot_general(first, second, numbers, preferred_element_type=WIDE)


def norm_rows(values, gain):
    centred = values - jnp.mean(values, axis=-1, keepdims=True)
    inverse = lax.rsqrt(jnp.mean(centred * centred, axis=-1, keepdims=True) + epsilon)
    normed = centred * inverse
    return normed * gain, normed, inverse


def norm_back(gradient, normed, inverse, gain):
    scaled = gradient * gain
    return inverse * (
        scaled
        - jnp.mean(scaled, axis=-1, keepdims=True)
        - normed * jnp.mean(scaled * normed, axis=-1, keepdims=True)
    )


def fold_rows(values):
    rows, width = values.shape
    return jnp.sum(values.reshape(rows // 8, 8, width), axis=0)


def split_heads(values):
    first = lax.broadcasted_iota(jnp.int32, values.shape, 1) < HEAD
    zero = jnp.zeros_like(values)
    return jnp.where(first, values, zero), jnp.where(first, zero, values)


def join_heads(first, second):
    keep = lax.broadcasted_iota(jnp.int32, first.shape, 1) < HEAD
    return jnp.where(keep, first, second)


def stack_heads(values):
    return jnp.concatenate(split_heads(values), axis=0)


def halves(ref):
    middle_column = ref.shape[1] // 2
    return ref.at[:, :middle_column], ref.at[:, middle_column:]


def pair(ref, rows, part, index):
    start = (part * PAIRS + index) * LANES
    return ref[rows, start : start + LANES]


def batches(count, size):
    return [range(start, min(start + size, count)) for start in range(0, count, size)]


def time_batches(block):
    spots = [
        (slice(group * block, (group + 1) * block), index)
        for group in range(2)
        for index in range(PAIRS)
    ]
    return [spots[start : start + TIME_BATCH] for start in range(0, len(spots), TIME_BATCH)]


def shares(scores, axis):
    highest = [jnp.max(item, axis=axis, keepdims=True) for item in scores]
    powers = [jnp.exp2((item - top) * POWER) for item, top in zip(scores, highest)]
    totals = [jnp.sum(item, axis=axis, keepdims=True) for item in powers]
    return [item * (1.0 / total) for item, total in zip(powers, totals)]


def score_grads(chances, grads, axis):
    means = [jnp.sum(p * g, axis=axis, keepdims=True) for p, g in zip(chances, grads)]
    return [(p * (g - mean)).astype(LOW) for p, g, mean in zip(chances, grads, means)]


def load_padded(x_ref, pad_ref):
    frames, places, width = x_ref.shape

    @pl.when(pl.program_id(0) == 0)
    def _():
        pad_ref[...] = jnp.zeros_like(pad_ref)

    for frame in range(frames):
        pad_ref[frame, 0:places] = x_ref[frame].astype(WIDE)
    return pad_ref[...].reshape(frames * pad_ref.shape[1], width)


def space_forward_kernel(
    places, x_ref, gain_ref, qk_ref, v_ref, out_ref, in_ref, qkv_ref, o_ref, after_ref, pad_ref
):
    frames, padded, width = pad_ref.shape
    values = load_padded(x_ref, pad_ref)
    normed = norm_rows(values, gain_ref[...])[0].astype(LOW)
    in_ref[...] = normed.reshape(frames, padded, width)
    for start, ref in ((0, qk_ref), (2 * width, v_ref)):
        part = dot(normed, ref[...]).astype(LOW)
        qkv_ref[:, :, start : start + part.shape[1]] = part.reshape(frames, padded, -1)
    real = lax.broadcasted_iota(jnp.int32, (padded, padded), 1) < places

    def one_frame(frame):
        for batch in batches(PAIRS, SPACE_BATCH):
            part = lambda number, index: qkv_ref[
                frame, :, number * width + index * LANES : number * width + (index + 1) * LANES
            ]
            keys = [split_heads(part(1, index)) for index in batch]
            scores = [
                jnp.where(real, dot(part(0, index), key, NT), NEVER)
                for index, both in zip(batch, keys)
                for key in both
            ]
            chances = [item.astype(LOW) for item in shares(scores, 1)]
            outs = [
                dot(chances[2 * slot + head], part(2, index))
                for slot, index in enumerate(batch)
                for head in range(2)
            ]
            for slot, index in enumerate(batch):
                o_ref[frame, :, index * LANES : (index + 1) * LANES] = join_heads(
                    *outs[2 * slot : 2 * slot + 2]
                ).astype(LOW)

    for frame in range(frames):
        one_frame(frame)
    after = values + dot(o_ref[...].reshape(frames * padded, width), out_ref[...])
    after = after.reshape(frames, padded // GROUP, GROUP, width)
    for frame in range(frames):
        after_ref[:, frame] = after[frame].astype(after_ref.dtype)


def middle_kernel(
    places,
    place_ref,
    ao_ref,
    ar_ref,
    go_ref,
    gr_ref,
    tgain_ref,
    fgain_ref,
    tproj_ref,
    tout_ref,
    up_ref,
    down_ref,
    qkv_ref,
    time_ref,
    feed_ref,
    hidden_ref,
    mo_ref,
    mr_ref,
    gt_ref,
    gain_ref,
):
    half = ao_ref.shape[1]
    frames = half + ar_ref.shape[1]
    width = ao_ref.shape[3]
    int_ref, ot_ref = halves(time_ref)
    inf_ref, gb_ref = halves(feed_ref)
    gh_ref, act_ref = halves(hidden_ref)
    rows = 2 * frames * GROUP
    block = frames * GROUP
    values = jnp.concatenate([ao_ref[...].astype(WIDE), ar_ref[...].astype(WIDE)], axis=1).reshape(rows, width)
    in_time = norm_rows(values, tgain_ref[...])[0].astype(LOW)
    int_ref[...] = in_time
    qkv_ref[...] = dot(in_time, tproj_ref[...]).astype(LOW)
    across = lax.broadcasted_iota(jnp.int32, (block, block), 0)
    down = lax.broadcasted_iota(jnp.int32, (block, block), 1)
    bias = jnp.where(((across ^ down) & (GROUP - 1)) == 0, 0.0, NEVER)
    for batch in time_batches(block):
        both = [
            dot(pair(qkv_ref, own, 0, index), stack_heads(pair(qkv_ref, own, 1, index)), NT)
            for own, index in batch
        ]
        scores = [
            item[:, head * block : (head + 1) * block] + bias for item in both for head in range(2)
        ]
        chances = [item.astype(LOW) for item in shares(scores, 1)]
        results = [
            dot(
                jnp.concatenate(chances[2 * slot : 2 * slot + 2], axis=1),
                stack_heads(pair(qkv_ref, own, 2, index)),
            )
            for slot, (own, index) in enumerate(batch)
        ]
        for result, (own, index) in zip(results, batch):
            ot_ref[own, index * LANES : (index + 1) * LANES] = result.astype(LOW)
    values = values + dot(ot_ref[...], tout_ref[...])
    feed_gain = fgain_ref[...]
    in_feed, normed, inverse = norm_rows(values, feed_gain)
    in_feed = in_feed.astype(LOW)
    inf_ref[...] = in_feed
    place = pl.program_id(0) * STEP + lax.broadcasted_iota(jnp.int32, (STEP, half, width), 0)
    sides = [jnp.where(place < places, ref[...].astype(WIDE), 0.0) for ref in (go_ref, gr_ref)]
    gradient = jnp.concatenate(
        [
            jnp.swapaxes(side[start : start + GROUP], 0, 1).reshape(half * GROUP, width)
            for start in (0, GROUP)
            for side in sides
        ],
        axis=0,
    )
    grad_low = gradient.astype(LOW)
    gb_ref[...] = grad_low
    hidden_width = up_ref.shape[1]
    root = math.sqrt(2.0 / math.pi)
    cuts = [slice(start, start + width) for start in range(0, hidden_width, width)]

    def products(cut):
        return dot(in_feed, up_ref[:, cut]), dot(grad_low, down_ref[:, cut], NT)

    mixed = values
    ready = products(cuts[0])
    for number, cut in enumerate(cuts):
        hidden, grad_active = ready
        if number + 1 < len(cuts):
            ready = products(cuts[number + 1])
        square = hidden * hidden
        plus = 0.5 * jnp.tanh(hidden * (root + (root * 0.044715) * square)) + 0.5
        active = hidden * plus
        act_ref[:, cut] = active.astype(LOW)
        inner = 2.0 * root + (6.0 * root * 0.044715) * square
        gh_ref[:, cut] = (grad_active * (plus + active * (1.0 - plus) * inner)).astype(LOW)
    for cut in cuts:
        mixed = mixed + dot(act_ref[:, cut], down_ref[:, cut])
    back = dot(gh_ref[...], up_ref[...], NT)
    mixed = mixed.reshape(2, frames, GROUP, width)
    for group in range(2):
        cut = slice(group * GROUP, (group + 1) * GROUP)
        mo_ref[0, cut] = jnp.swapaxes(mixed[group, :half], 0, 1).astype(LOW)
        mr_ref[cut] = jnp.swapaxes(mixed[group, half:], 0, 1).astype(LOW)
    g_time = gradient + norm_back(back, normed, inverse, feed_gain)
    gt_ref[...] = g_time.astype(gt_ref.dtype)

    @pl.when(pl.program_id(0) == 0)
    def _():
        gain_ref[...] = jnp.zeros_like(gain_ref)

    gain_ref[...] += fold_rows(back * normed)


def time_backward_kernel(
    qkv_ref,
    gt_ref,
    ao_ref,
    ar_ref,
    tgain_ref,
    tout_ref,
    tproj_ref,
    grad_ref,
    gso_ref,
    gsr_ref,
    gain_ref,
    d_ref,
):
    half = ao_ref.shape[1]
    frames = half + ar_ref.shape[1]
    width = ao_ref.shape[3]
    rows = 2 * frames * GROUP
    block = frames * GROUP
    gq_ref, tb_ref = grad_ref.at[:, : 3 * width], grad_ref.at[:, 3 * width :]
    tb = gt_ref[...].astype(LOW)
    tb_ref[...] = tb
    d_ref[...] = dot(tb, tout_ref[...], NT).astype(LOW)
    across = lax.broadcasted_iota(jnp.int32, (block, block), 0)
    down = lax.broadcasted_iota(jnp.int32, (block, block), 1)
    bias = jnp.where(((across ^ down) & (GROUP - 1)) == 0, 0.0, NEVER)
    for batch in time_batches(block):
        keys = [stack_heads(pair(qkv_ref, own, 1, index)) for own, index in batch]
        both = [dot(key, pair(qkv_ref, own, 0, index), NT) for key, (own, index) in zip(keys, batch)]
        grad_both = [
            dot(stack_heads(pair(qkv_ref, own, 2, index)), pair(d_ref, own, 0, index), NT)
            for own, index in batch
        ]
        cuts = [slice(0, block), slice(block, 2 * block)]
        chances = shares([item[cut] + bias for item in both for cut in cuts], 0)
        grads = score_grads(chances, [item[cut] for item in grad_both for cut in cuts], 0)
        chances = [item.astype(LOW) for item in chances]
        results = []
        for slot, (own, index) in enumerate(batch):
            two = slice(2 * slot, 2 * slot + 2)
            grad = stack_heads(pair(d_ref, own, 0, index))
            queries = stack_heads(pair(qkv_ref, own, 0, index))
            results.append(
                (
                    dot(jnp.concatenate(grads[two], axis=0), keys[slot], TN) * SCALE,
                    dot(jnp.concatenate(grads[two], axis=1), queries) * SCALE,
                    dot(jnp.concatenate(chances[two], axis=1), grad),
                )
            )
        for items, (own, index) in zip(results, batch):
            for part, item in enumerate(items):
                start = (part * PAIRS + index) * LANES
                gq_ref[own, start : start + LANES] = item.astype(LOW)
    values = jnp.concatenate([ao_ref[...].astype(WIDE), ar_ref[...].astype(WIDE)], axis=1).reshape(rows, width)
    gain = tgain_ref[...]
    _, normed, inverse = norm_rows(values, gain)
    back = dot(gq_ref[...], tproj_ref[...], NT)
    result = gt_ref[...].astype(WIDE) + norm_back(back, normed, inverse, gain)
    for frame in range(frames):
        low = result[frame * GROUP : (frame + 1) * GROUP]
        high = result[block + frame * GROUP : block + (frame + 1) * GROUP]
        tile = jnp.concatenate([low, high], axis=0).astype(gso_ref.dtype)
        if frame < half:
            gso_ref[frame] = tile
        else:
            gsr_ref[frame - half] = tile

    @pl.when(pl.program_id(0) == 0)
    def _():
        gain_ref[...] = jnp.zeros_like(gain_ref)

    gain_ref[...] += fold_rows(back * normed)


def space_backward_kernel(
    places,
    place_ref,
    x_ref,
    gs_ref,
    qkv_ref,
    gain_row_ref,
    out_ref,
    qk_ref,
    v_ref,
    gq_ref,
    sb_ref,
    gx_ref,
    gain_ref,
    pad_ref,
    d_ref,
    order_ref,
):
    frames, padded, width = pad_ref.shape
    stride = order_ref.shape[1] // padded
    values = load_padded(x_ref, pad_ref)
    grad_space = gs_ref[...].astype(WIDE).reshape(frames * padded, width)
    sb = grad_space.astype(LOW)
    sb_ref[...] = sb.reshape(frames, padded, width)
    d_ref[...] = dot(sb, out_ref[...], NT).astype(LOW).reshape(frames, padded, width)
    real = lax.broadcasted_iota(jnp.int32, (padded, padded), 0) < places

    def one_frame(frame):
        for batch in batches(PAIRS, SPACE_BATCH):
            part = lambda number, index: qkv_ref[
                frame, :, number * width + index * LANES : number * width + (index + 1) * LANES
            ]
            grad = lambda index: d_ref[frame, :, index * LANES : (index + 1) * LANES]
            heads = [(index, head) for index in batch for head in range(2)]
            scores = [
                jnp.where(real, dot(split_heads(part(1, index))[head], part(0, index), NT), NEVER)
                for index, head in heads
            ]
            grad_shares = [
                dot(split_heads(part(2, index))[head], grad(index), NT) for index, head in heads
            ]
            chances = shares(scores, 0)
            grads = score_grads(chances, grad_shares, 0)
            chances = [item.astype(LOW) for item in chances]
            dq = [dot(ds, part(1, index), TN) * SCALE for ds, (index, _) in zip(grads, heads)]
            dk = [dot(ds, part(0, index)) * SCALE for ds, (index, _) in zip(grads, heads)]
            dv = [dot(p, grad(index)) for p, (index, _) in zip(chances, heads)]
            for number, items in enumerate((dq, dk, dv)):
                for slot, index in enumerate(batch):
                    start = number * width + index * LANES
                    gq_ref[frame, :, start : start + LANES] = join_heads(
                        items[2 * slot], items[2 * slot + 1]
                    ).astype(LOW)

    for frame in range(frames):
        one_frame(frame)
    gain = gain_row_ref[...]
    _, normed, inverse = norm_rows(values, gain)
    back = dot(gq_ref[:, :, : 2 * width].reshape(frames * padded, 2 * width), qk_ref[...], NT)
    back = back + dot(gq_ref[:, :, 2 * width :].reshape(frames * padded, width), v_ref[...], NT)
    result = grad_space + norm_back(back, normed, inverse, gain)
    result = result.reshape(frames, padded, width)
    for frame in range(frames):
        rows = pl.ds(pl.program_id(0) * frames + frame, padded, stride=stride)
        for lane in range(width // LANES):
            order_ref[lane, rows, :] = result[frame, :, lane * LANES : (lane + 1) * LANES]

    @pl.when(pl.program_id(0) == pl.num_programs(0) - 1)
    def _():
        for lane in range(width // LANES):
            tile = order_ref[lane, 0 : places * stride].astype(gx_ref.dtype)
            tile = tile.reshape(places, stride, LANES)
            if len(gx_ref.shape) == 4:
                gx_ref[0, :, :, lane * LANES : (lane + 1) * LANES] = tile
            else:
                gx_ref[:, :, lane * LANES : (lane + 1) * LANES] = tile

    @pl.when(pl.program_id(0) == 0)
    def _():
        gain_ref[...] = jnp.zeros_like(gain_ref)

    gain_ref[...] += fold_rows(back * normed)


def whole(shape):
    return pl.BlockSpec(
        shape, lambda *_: (0,) * len(shape), pipeline_mode=pl.Buffered(buffer_count=1)
    )


def columns(array, width, index):
    return pl.BlockSpec(
        (array.shape[0], width),
        lambda *_: (0, index),
        pipeline_mode=pl.Buffered(buffer_count=1),
    )


def params():
    return pltpu.CompilerParams(vmem_limit_bytes=LIMIT)


def cost(flops, *arrays):
    size = sum(math.prod(item.shape) * jnp.dtype(item.dtype).itemsize for item in arrays)
    return pl.CostEstimate(
        flops=int(flops) // SHRINK, bytes_accessed=int(size) // SHRINK, transcendentals=0
    )


def padded_places(places):
    return -(-places // STEP) * STEP


def by_frame(count, *tail):
    return pl.BlockSpec((count,) + tail, lambda step, *_: (step,) + (0,) * len(tail))


def space_forward(x, gain, first, second):
    frames, places, width = x.shape
    padded = padded_places(places)
    groups = padded // GROUP
    rows = frames * padded
    outs = (
        jax.ShapeDtypeStruct((frames, padded, width), LOW),
        jax.ShapeDtypeStruct((frames, padded, 3 * width), LOW),
        jax.ShapeDtypeStruct((frames, padded, width), LOW),
        jax.ShapeDtypeStruct((groups, frames, GROUP, width), WIDE),
    )
    flops = 2 * rows * width * 4 * width + 8 * rows * padded * width
    return pl.pallas_call(
        functools.partial(space_forward_kernel, places),
        grid=(frames // 2,),
        in_specs=[
            by_frame(2, places, width),
            whole(gain.shape),
            whole(first.shape),
            columns(second, width, 0),
            columns(second, width, 1),
        ],
        out_specs=[
            by_frame(2, padded, width),
            by_frame(2, padded, 3 * width),
            by_frame(2, padded, width),
            pl.BlockSpec((groups, 2, GROUP, width), lambda step: (0, step, 0, 0)),
        ],
        out_shape=outs,
        scratch_shapes=[pltpu.VMEM((2, padded, width), WIDE)],
        compiler_params=params(),
        cost_estimate=cost(flops, x, first, second, *outs),
        name="space_forward",
    )(x, gain, first, second, second)


def middle(place, after_own, after_rest, g_own, g_rest, tgain, fgain, packed):
    groups, half, _, width = after_own.shape
    places = g_own.shape[0]
    frames = 2 * half
    rows = groups * frames * GROUP
    block = 2 * frames * GROUP
    hidden = (packed.shape[1] - 4 * width) // 2
    padded = groups * GROUP
    outs = (
        jax.ShapeDtypeStruct((rows, 3 * width), LOW),
        jax.ShapeDtypeStruct((rows, 2 * width), LOW),
        jax.ShapeDtypeStruct((rows, 2 * width), LOW),
        jax.ShapeDtypeStruct((rows, 2 * hidden), LOW),
        jax.ShapeDtypeStruct((2, places, half, width), LOW),
        jax.ShapeDtypeStruct((places, half, width), LOW),
        jax.ShapeDtypeStruct((rows, width), WIDE),
        jax.ShapeDtypeStruct((8, width), WIDE),
    )
    by_row = lambda size: pl.BlockSpec((block, size), lambda step, place: (step, 0))
    by_group = pl.BlockSpec((2, half, GROUP, width), lambda step, place: (step, 0, 0, 0))
    by_place = pl.BlockSpec((STEP, half, width), lambda step, place: (step, 0, 0))
    flops = 2 * rows * width * (4 * width + 4 * hidden) + 8 * rows * frames * GROUP * width
    return pl.pallas_call(
        functools.partial(middle_kernel, places),
        grid_spec=pltpu.PrefetchScalarGridSpec(
            num_scalar_prefetch=1,
            grid=(groups // 2,),
            in_specs=[by_group, by_group, by_place, by_place]
            + [
                whole(tgain.shape),
                whole(fgain.shape),
                columns(packed, 3 * width, 0),
                columns(packed, width, 3),
                columns(packed, hidden, 1),
                columns(packed, hidden, 2),
            ],
            out_specs=[
                by_row(3 * width),
                by_row(2 * width),
                by_row(2 * width),
                by_row(2 * hidden),
                pl.BlockSpec((1, STEP, half, width), lambda step, place: (place[0], step, 0, 0)),
                by_place,
                by_row(width),
                pl.BlockSpec((8, width), lambda step, place: (0, 0)),
            ],
        ),
        out_shape=outs,
        compiler_params=params(),
        cost_estimate=cost(flops, after_own, after_rest, g_own, g_rest, *outs),
        name="middle",
    )(place, after_own, after_rest, g_own, g_rest, tgain, fgain, packed, packed, packed, packed)


def time_backward(qkv, g_time, after_own, after_rest, tgain, packed):
    groups, half, _, width = after_own.shape
    frames = 2 * half
    rows = groups * frames * GROUP
    block = 2 * frames * GROUP
    padded = groups * GROUP
    outs = (
        jax.ShapeDtypeStruct((rows, 4 * width), LOW),
        jax.ShapeDtypeStruct((half, padded, width), WIDE),
        jax.ShapeDtypeStruct((half, padded, width), WIDE),
        jax.ShapeDtypeStruct((8, width), WIDE),
    )
    by_row = lambda size: pl.BlockSpec((block, size), lambda step: (step, 0))
    by_group = pl.BlockSpec((2, half, GROUP, width), lambda step: (step, 0, 0, 0))
    by_place = pl.BlockSpec((half, STEP, width), lambda step: (0, step, 0))
    flops = 2 * rows * width * 4 * width + 20 * rows * frames * GROUP * width
    return pl.pallas_call(
        time_backward_kernel,
        grid=(groups // 2,),
        in_specs=[by_row(3 * width), by_row(width), by_group, by_group]
        + [whole(tgain.shape), columns(packed, width, 3), columns(packed, 3 * width, 0)],
        out_specs=[
            by_row(4 * width),
            by_place,
            by_place,
            pl.BlockSpec((8, width), lambda step: (0, 0)),
        ],
        out_shape=outs,
        scratch_shapes=[pltpu.VMEM((block, width), LOW)],
        compiler_params=params(),
        cost_estimate=cost(flops, qkv, g_time, after_own, after_rest, *outs),
        name="time_backward",
    )(qkv, g_time, after_own, after_rest, tgain, packed, packed)


def space_backward(place, x, g_space, qkv, gain, first, second, kind):
    frames, places, width = x.shape
    padded = padded_places(places)
    rows = frames * padded
    own = kind == WIDE
    shape = (2, places, frames, width) if own else (places, frames, width)
    outs = (
        jax.ShapeDtypeStruct((frames, padded, 3 * width), LOW),
        jax.ShapeDtypeStruct((frames, padded, width), LOW),
        jax.ShapeDtypeStruct(shape, kind),
        jax.ShapeDtypeStruct((8, width), WIDE),
    )
    flops = 2 * rows * width * 4 * width + 20 * rows * padded * width
    return pl.pallas_call(
        functools.partial(space_backward_kernel, places),
        grid_spec=pltpu.PrefetchScalarGridSpec(
            num_scalar_prefetch=1,
            grid=(frames // 2,),
            in_specs=[
                by_frame(2, places, width),
                by_frame(2, padded, width),
                by_frame(2, padded, 3 * width),
                whole(gain.shape),
                columns(second, width, 1),
                whole(first.shape),
                columns(second, width, 0),
            ],
            out_specs=[
                by_frame(2, padded, 3 * width),
                by_frame(2, padded, width),
                pl.BlockSpec((1,) + shape[1:], lambda step, place: (place[0], 0, 0, 0))
                if own
                else pl.BlockSpec(shape, lambda step, place: (0, 0, 0)),
                pl.BlockSpec((8, width), lambda step, place: (0, 0)),
            ],
            scratch_shapes=[
                pltpu.VMEM((2, padded, width), WIDE),
                pltpu.VMEM((2, padded, width), LOW),
                pltpu.VMEM((width // LANES, padded * frames, LANES), WIDE),
            ],
        ),
        out_shape=outs,
        compiler_params=params(),
        cost_estimate=cost(flops, x, g_space, qkv, *outs),
        name="space_backward",
    )(place, x, g_space, qkv, gain, second, first, second)


def gradient_kernel(parts, tiles, core_ref, *refs):
    step = pl.program_id(0)

    def emit(pairs):
        total = dot(pairs[0][0][...], pairs[0][1][...], TN)
        for first, second in pairs[1:]:
            total = total + dot(first[...], second[...], TN)
        split_owners(core_ref, total, *refs[-2:])

    start = 0
    for (first, last), count in zip(tiles, parts):
        group = refs[start : start + 2 * count]
        start += 2 * count
        pairs = [(group[2 * index], group[2 * index + 1]) for index in range(count)]
        pl.when((step >= first) & (step < last))(functools.partial(emit, pairs))


def plan_gradient(groups):
    width = groups[0][0][0][0].shape[1] if groups[0][3] == 1 else groups[0][0][0][1].shape[1]
    count = groups[-1][2]
    specs, arrays, parts, tiles = [], [], [], []
    flops = 0
    for pairs, first, last, side, offset in groups:
        parts.append(len(pairs))
        tiles.append((first, last))
        for pair_arrays in pairs:
            for index, item in enumerate(pair_arrays):
                rows = item.shape[0]
                if index == side and last - first > 1:
                    spec = pl.BlockSpec(
                        (rows, width),
                        lambda step, *_, first=first, last=last, offset=offset: (
                            0,
                            jnp.clip(step - first, 0, last - first - 1) + offset,
                        ),
                    )
                else:
                    fixed = offset if index == side else 0
                    spec = pl.BlockSpec(
                        (rows, width),
                        lambda step, *_, fixed=fixed: (0, fixed),
                        pipeline_mode=pl.Buffered(buffer_count=1),
                    )
                specs.append(spec)
                arrays.append(item)
            flops += 2 * rows * width * width * (last - first)
    return width, count, specs, arrays, parts, tiles, flops


def paired_specs(narrow, wide, width, turns):
    count = wide.shape[1] // width
    return count, [
        pl.BlockSpec((narrow.shape[0], width), lambda step, *_: (0, step // turns)),
        pl.BlockSpec((wide.shape[0], width), lambda step, *_: (0, step)),
    ]


def feed_gradient_kernel(turns, narrow_ref, wide_ref, out_ref):
    @pl.when(pl.program_id(0) < turns)
    def _():
        out_ref[...] = dot(narrow_ref[...], wide_ref[...], TN).astype(LOW)

    @pl.when(pl.program_id(0) >= turns)
    def _():
        out_ref[...] = dot(wide_ref[...], narrow_ref[...], TN).astype(LOW)


def feed_gradient(feed, hidden, width):
    turns = hidden.shape[1] // width // 2
    count, specs = paired_specs(feed, hidden, width, turns)
    out = jax.ShapeDtypeStruct((width, count * width), LOW)
    return pl.pallas_call(
        functools.partial(feed_gradient_kernel, turns),
        grid=(count,),
        in_specs=specs,
        out_specs=pl.BlockSpec((width, width), lambda step: (0, step)),
        out_shape=out,
        compiler_params=params(),
        cost_estimate=cost(2 * feed.shape[0] * width * width * count, feed, hidden, out),
        name="feed_gradient",
    )(feed, hidden)


def split_owners(core_ref, total, keep_ref, send_ref):
    total = total.reshape(keep_ref.shape[0], 2, keep_ref.shape[1], keep_ref.shape[2])
    total = total.astype(LOW)
    keep = core_ref[0] == 0
    keep_ref[...] = jnp.where(keep, total[:, 0], total[:, 1])
    send_ref[...] = jnp.where(keep, total[:, 1], total[:, 0])


def time_gradient_kernel(core_ref, narrow_ref, wide_ref, keep_ref, send_ref):
    split_owners(core_ref, dot(narrow_ref[...], wide_ref[...], TN), keep_ref, send_ref)


def time_gradient(core, owners, inputs, grads, width):
    count, specs = paired_specs(inputs, grads, width, 3)
    blocks, rows = owners // 4, 2 * (width // owners)
    out = jax.ShapeDtypeStruct((blocks, rows, count * width), LOW)
    out_spec = pl.BlockSpec((blocks, rows, width), lambda step, core: (0, 0, step))
    return pl.pallas_call(
        time_gradient_kernel,
        grid_spec=pltpu.PrefetchScalarGridSpec(
            num_scalar_prefetch=1, grid=(count,), in_specs=specs, out_specs=[out_spec, out_spec]
        ),
        out_shape=[out, out],
        compiler_params=params(),
        cost_estimate=cost(2 * inputs.shape[0] * width * width * count, inputs, grads, out, out),
        name="time_gradient",
    )(core, inputs, grads)


def split_gradient(core, owners, *groups):
    width, count, specs, arrays, parts, tiles, flops = plan_gradient(groups)
    blocks, rows = owners // 4, 2 * (width // owners)
    out = jax.ShapeDtypeStruct((blocks, rows, count * width), LOW)
    out_spec = pl.BlockSpec((blocks, rows, width), lambda step, core: (0, 0, step))
    return pl.pallas_call(
        functools.partial(gradient_kernel, parts, tiles),
        grid_spec=pltpu.PrefetchScalarGridSpec(
            num_scalar_prefetch=1,
            grid=(count,),
            in_specs=specs,
            out_specs=[out_spec, out_spec],
        ),
        out_shape=[out, out],
        compiler_params=params(),
        cost_estimate=cost(flops, *arrays, out, out),
        name="split_gradient",
    )(core, *arrays)


MICRO = 2


def norm_forward(values, gain):
    centred = values - jnp.mean(values, axis=-1, keepdims=True)
    inverse = lax.rsqrt(jnp.mean(centred * centred, axis=-1, keepdims=True) + epsilon)
    normed = centred * inverse
    return (normed * gain, normed, inverse)


def norm_backward(gradient, normed, inverse, gain):
    gain_grad = jnp.sum(gradient * normed, axis=(0, 1, 2))
    scaled = gradient * gain
    centred_grad = (
        scaled
        - jnp.mean(scaled, axis=-1, keepdims=True)
        - normed * jnp.mean(scaled * normed, axis=-1, keepdims=True)
    )
    return (inverse * centred_grad, gain_grad)


def to_places(blocks):
    clip_count, frames, places, model_width = blocks.shape
    return blocks.transpose(0, 2, 1, 3).reshape(clip_count * places, frames, HEADS, HEAD)


def from_places(attended, clip_count, places):
    frames = attended.shape[1]
    return attended.reshape(clip_count, places, frames, HEADS * HEAD).transpose(0, 2, 1, 3)


def attend_forward(queries, key_block, value_block):
    factor = HEAD ** (-0.5)
    scores = (
        jnp.einsum("blhe,bmhe->bhlm", queries, key_block, preferred_element_type=jnp.float32)
        * factor
    )
    highest = jnp.max(scores, axis=-1, keepdims=True)
    powers = jnp.exp(scores - highest)
    row_total = jnp.sum(powers, axis=-1, keepdims=True)
    chances = (powers / row_total).astype(jnp.bfloat16)
    result = jnp.einsum("bhlm,bmhe->blhe", chances, value_block, preferred_element_type=jnp.float32)
    return (result, highest + jnp.log(row_total))


def attend_backward(queries, key_block, value_block, logsum, grad_out):
    factor = HEAD ** (-0.5)
    scores = (
        jnp.einsum("blhe,bmhe->bhlm", queries, key_block, preferred_element_type=jnp.float32)
        * factor
    )
    chances = jnp.exp(scores - logsum)
    grad_chances = jnp.einsum(
        "blhe,bmhe->bhlm", grad_out, value_block, preferred_element_type=jnp.float32
    )
    grad_scores = (
        chances * (grad_chances - jnp.sum(chances * grad_chances, axis=-1, keepdims=True))
    ).astype(jnp.bfloat16)
    grad_queries = (
        jnp.einsum("bhlm,bmhe->blhe", grad_scores, key_block, preferred_element_type=jnp.float32)
        * factor
    )
    grad_keys = (
        jnp.einsum("bhlm,blhe->bmhe", grad_scores, queries, preferred_element_type=jnp.float32)
        * factor
    )
    grad_values = jnp.einsum(
        "bhlm,blhe->bmhe",
        chances.astype(jnp.bfloat16),
        grad_out,
        preferred_element_type=jnp.float32,
    )
    return (grad_queries, grad_keys, grad_values)


def project(values, matrix):
    return jnp.einsum("cfpd,de->cfpe", values, matrix, preferred_element_type=jnp.float32)


def project_back(gradient, matrix):
    return jnp.einsum("cfpe,de->cfpd", gradient, matrix, preferred_element_type=jnp.float32)


def outer_sum(values, gradient):
    return jnp.einsum("cfpd,cfpe->de", values, gradient, preferred_element_type=jnp.float32)


def forward(sample, gathered):
    (
        space_gain,
        time_gain,
        feed_gain,
        space_proj,
        space_out,
        time_proj,
        time_out,
        up_proj,
        down_proj,
    ) = gathered
    clip_count, frames, places, model_width = sample.shape
    normed_space = norm_forward(sample, space_gain.astype(jnp.float32))
    in_space = normed_space[0].astype(jnp.bfloat16)
    qkv_space = project(in_space, space_proj).astype(jnp.bfloat16)
    parted = qkv_space.reshape(clip_count * frames, places, 3, HEADS, HEAD)
    attended, logsum_space = attend_forward(parted[:, :, 0], parted[:, :, 1], parted[:, :, 2])
    out_space = attended.reshape(clip_count, frames, places, model_width).astype(jnp.bfloat16)
    after_space = sample + project(out_space, space_out)
    normed_time = norm_forward(after_space, time_gain.astype(jnp.float32))
    in_time = normed_time[0].astype(jnp.bfloat16)
    qkv_time = project(in_time, time_proj).astype(jnp.bfloat16)
    kv_whole = lax.all_gather(qkv_time[..., model_width:], "frame", axis=1, tiled=True)
    attended, logsum_time = attend_forward(
        to_places(qkv_time[..., :model_width]),
        to_places(kv_whole[..., :model_width]),
        to_places(kv_whole[..., model_width:]),
    )
    out_time = from_places(attended, clip_count, places).astype(jnp.bfloat16)
    after_time = after_space + project(out_time, time_out)
    normed_feed = norm_forward(after_time, feed_gain.astype(jnp.float32))
    in_feed = normed_feed[0].astype(jnp.bfloat16)
    hidden = project(in_feed, up_proj)
    active = jax.nn.gelu(hidden).astype(jnp.bfloat16)
    result = after_time + project(active, down_proj)
    saved = (
        normed_space,
        in_space,
        qkv_space,
        logsum_space,
        out_space,
        normed_time,
        in_time,
        qkv_time,
        kv_whole,
        logsum_time,
        out_time,
        normed_feed,
        in_feed,
        hidden,
        active,
    )
    return (result, saved)


def backward(gradient, saved, gathered):
    (
        space_gain,
        time_gain,
        feed_gain,
        space_proj,
        space_out,
        time_proj,
        time_out,
        up_proj,
        down_proj,
    ) = gathered
    (
        normed_space,
        in_space,
        qkv_space,
        logsum_space,
        out_space,
        normed_time,
        in_time,
        qkv_time,
        time_side,
        logsum_time,
        out_time,
        normed_feed,
        in_feed,
        hidden,
        active,
    ) = saved
    clip_count, frames, places, model_width = gradient.shape
    grad_low = gradient.astype(jnp.bfloat16)
    grad_down = outer_sum(active, grad_low)
    grad_active = project_back(grad_low, down_proj)
    gelu_value, gelu_pull = jax.vjp(jax.nn.gelu, hidden)
    grad_hidden = gelu_pull(grad_active)[0].astype(jnp.bfloat16)
    grad_up = outer_sum(in_feed, grad_hidden)
    back_feed, grad_feed_gain = norm_backward(
        project_back(grad_hidden, up_proj),
        normed_feed[1],
        normed_feed[2],
        feed_gain.astype(jnp.float32),
    )
    grad_time = gradient + back_feed
    time_low = grad_time.astype(jnp.bfloat16)
    grad_tout = outer_sum(out_time, time_low)
    grad_out_time = project_back(time_low, time_out).astype(jnp.bfloat16)
    grad_queries, grad_keys, grad_values = attend_backward(
        to_places(qkv_time[..., :model_width]),
        to_places(time_side[..., :model_width]),
        to_places(time_side[..., model_width:]),
        logsum_time,
        to_places(grad_out_time),
    )
    grad_kv = jnp.concatenate(
        (from_places(grad_keys, clip_count, places), from_places(grad_values, clip_count, places)),
        axis=-1,
    )
    grad_kv_own = lax.psum_scatter(
        grad_kv.astype(jnp.bfloat16), "frame", scatter_dimension=1, tiled=True
    ).astype(jnp.float32)
    grad_qkv_time = jnp.concatenate(
        (from_places(grad_queries, clip_count, places), grad_kv_own), axis=-1
    ).astype(jnp.bfloat16)
    grad_tproj = outer_sum(in_time, grad_qkv_time)
    back_time, grad_time_gain = norm_backward(
        project_back(grad_qkv_time, time_proj),
        normed_time[1],
        normed_time[2],
        time_gain.astype(jnp.float32),
    )
    grad_space = grad_time + back_time
    space_low = grad_space.astype(jnp.bfloat16)
    grad_sout = outer_sum(out_space, space_low)
    grad_out_space = project_back(space_low, space_out).astype(jnp.bfloat16)
    parted = qkv_space.reshape(clip_count * frames, places, 3, HEADS, HEAD)
    grad_queries, grad_keys, grad_values = attend_backward(
        parted[:, :, 0],
        parted[:, :, 1],
        parted[:, :, 2],
        logsum_space,
        grad_out_space.reshape(clip_count * frames, places, HEADS, HEAD),
    )
    grad_qkv_space = (
        jnp.stack((grad_queries, grad_keys, grad_values), axis=2)
        .reshape(clip_count, frames, places, 3 * model_width)
        .astype(jnp.bfloat16)
    )
    grad_sproj = outer_sum(in_space, grad_qkv_space)
    back_space, grad_space_gain = norm_backward(
        project_back(grad_qkv_space, space_proj),
        normed_space[1],
        normed_space[2],
        space_gain.astype(jnp.float32),
    )
    grad_input = grad_space + back_space
    return (
        grad_input,
        (
            grad_space_gain,
            grad_time_gain,
            grad_feed_gain,
            grad_sproj,
            grad_sout,
            grad_tproj,
            grad_tout,
            grad_up,
            grad_down,
        ),
    )


def general(
    tokens,
    cotangent,
    space_gain,
    time_gain,
    feed_gain,
    space_proj,
    space_out,
    time_proj,
    time_out,
    up_proj,
    down_proj,
):
    owned = (
        space_gain,
        time_gain,
        feed_gain,
        space_proj,
        space_out,
        time_proj,
        time_out,
        up_proj,
        down_proj,
    )
    devices_all = lax.axis_size(("clip", "frame"))
    per_micro = tokens.shape[0] // MICRO
    totals = tuple(
        (
            jnp.zeros((piece.shape[0] * devices_all,) + piece.shape[1:], jnp.float32)
            for piece in owned
        )
    )
    gathered = (
        lax.all_gather(space_gain, ("clip", "frame"), axis=0, tiled=True),
        lax.all_gather(time_gain, ("clip", "frame"), axis=0, tiled=True),
        lax.all_gather(feed_gain, ("clip", "frame"), axis=0, tiled=True),
        lax.all_gather(space_proj, ("clip", "frame"), axis=0, tiled=True),
        lax.all_gather(space_out, ("clip", "frame"), axis=0, tiled=True),
        lax.all_gather(time_proj, ("clip", "frame"), axis=0, tiled=True),
        lax.all_gather(time_out, ("clip", "frame"), axis=0, tiled=True),
        lax.all_gather(up_proj, ("clip", "frame"), axis=0, tiled=True),
        lax.all_gather(down_proj, ("clip", "frame"), axis=0, tiled=True),
    )
    mixed_parts = []
    grad_parts = []
    for micro_index in range(MICRO):
        sample = tokens[micro_index * per_micro : (micro_index + 1) * per_micro].astype(jnp.float32)
        result, saved = forward(sample, gathered)
        mixed_parts.append(result.astype(jnp.bfloat16))
        gradient = cotangent[micro_index * per_micro : (micro_index + 1) * per_micro].astype(
            jnp.float32
        )
        grad_input, grads = backward(gradient, saved, gathered)
        grad_parts.append(grad_input)
        totals = tuple((first + second for first, second in zip(totals, grads)))
    flat = tuple((item.reshape(-1) for item in totals))
    owners = (
        lax.psum_scatter(flat[0], ("clip", "frame"), scatter_dimension=0, tiled=True),
        lax.psum_scatter(flat[1], ("clip", "frame"), scatter_dimension=0, tiled=True),
        lax.psum_scatter(flat[2], ("clip", "frame"), scatter_dimension=0, tiled=True),
        lax.psum_scatter(flat[3], ("clip", "frame"), scatter_dimension=0, tiled=True),
        lax.psum_scatter(flat[4], ("clip", "frame"), scatter_dimension=0, tiled=True),
        lax.psum_scatter(flat[5], ("clip", "frame"), scatter_dimension=0, tiled=True),
        lax.psum_scatter(flat[6], ("clip", "frame"), scatter_dimension=0, tiled=True),
        lax.psum_scatter(flat[7], ("clip", "frame"), scatter_dimension=0, tiled=True),
        lax.psum_scatter(flat[8], ("clip", "frame"), scatter_dimension=0, tiled=True),
    )
    shaped = tuple((piece.reshape(mine.shape) for piece, mine in zip(owners, owned)))
    mixed = jnp.concatenate(mixed_parts, axis=0)
    grad_tokens = jnp.concatenate(grad_parts, axis=0)
    return (
        mixed,
        grad_tokens,
        shaped[0],
        shaped[1],
        shaped[2],
        shaped[3],
        shaped[4],
        shaped[5],
        shaped[6],
        shaped[7],
        shaped[8],
    )


def swap_axis(values, axis):
    size = lax.axis_size(axis)
    return lax.ppermute(values, axis, [(index, size - 1 - index) for index in range(size)])


def flip(values, mask):
    size = lax.axis_size("clip")
    return lax.ppermute(values, "clip", [(index, index ^ mask) for index in range(size)])


def tie(*items):
    return lax.optimization_barrier(items)


def bit_of(mask):
    return (lax.axis_index("clip") // mask) % 2


def in_order(bit, mine, other, axis):
    return jnp.where(
        bit == 0, jnp.stack([mine, other], axis=axis), jnp.stack([other, mine], axis=axis)
    )


def pick(values, index, axis):
    return lax.dynamic_index_in_dim(values, index, axis, keepdims=False)


def added(*items):
    return sum(item.astype(WIDE) for item in items)


def collect_start(shard):
    return in_order(lax.axis_index("frame"), shard, swap_axis(shard, "frame"), 0)


def collect_lines(item):
    line = lax.axis_index("clip") // 4
    parts = [item] + [flip(item, 4 * step) for step in range(1, 4)]
    odd, far = line % 2, line // 2
    parts = [jnp.where(odd == 0, parts[index], parts[index ^ 1]) for index in range(4)]
    parts = [jnp.where(far == 0, parts[index], parts[index ^ 2]) for index in range(4)]
    return jnp.stack(parts, axis=0)


def collect_half(item, mask, axis):
    return in_order(bit_of(mask), item, flip(item, mask), axis)


def merged(item):
    return item.reshape(-1, item.shape[-1])


def scatter_core(keep, send):
    return keep, flip(send, 1)


def column_parts(keep, other):
    shape = (4, 2) + keep.shape[1:]
    keep, other = keep.reshape(shape), other.reshape(shape)
    bit = bit_of(2)
    send = added(pick(keep, 1 - bit, 1), pick(other, 1 - bit, 1)).astype(LOW)
    return added(pick(keep, bit, 1), pick(other, bit, 1)).astype(LOW), send


def scatter_columns(keep, other):
    keep, send = column_parts(keep, other)
    return keep, flip(send, 2)


def scatter_lines(keep, other):
    line = lax.axis_index("clip") // 4
    total = added(keep, other).astype(LOW)
    parts = [flip(pick(total, line ^ step, 0), 4 * step) for step in range(1, 4)]
    return (pick(total, line, 0), *parts)


def scatter_frames(*parts):
    total = added(*parts).astype(LOW)
    total = total.reshape(2, total.shape[0] // 2, total.shape[1])
    place = lax.axis_index("frame")
    return pick(total, place, 0), swap_axis(pick(total, 1 - place, 0), "frame")


def flat_rows(values):
    return values.reshape(-1, values.shape[-1])


def clip_local(
    tokens,
    cotangent,
    space_gain,
    time_gain,
    feed_gain,
    space_proj,
    space_out,
    time_proj,
    time_out,
    up_proj,
    down_proj,
):
    axes = ("clip", "frame")
    place = lax.axis_index("frame")
    owners = lax.axis_size(axes)
    share, width = space_out.shape
    blocks = down_proj.shape[0] // share
    core = bit_of(1).reshape(1)
    spot = place.reshape(1)

    gains = jnp.stack([space_gain, time_gain, feed_gain], axis=1)
    gains = jnp.pad(gains, ((0, 0), (0, LANES - 3)))
    first = collect_start(space_proj[:, : 2 * width])
    second = collect_start(
        jnp.concatenate([space_proj[:, 2 * width :], space_out, gains], axis=1)
    )
    up_order = up_proj.reshape(share, owners, blocks, share).transpose(0, 2, 1, 3)
    down_order = down_proj.reshape(blocks, share, width).transpose(1, 0, 2)
    packed = jnp.concatenate(
        [time_proj, time_out, up_order.reshape(share, -1), down_order.reshape(share, -1)], axis=1
    )
    first, second, by_place, packed = tie(first, second, tokens.transpose(0, 2, 1, 3), packed)
    packed = lax.all_gather(packed, axes, axis=0, tiled=True)
    half = by_place.shape[1] // 2
    send = pick(by_place, 1 - place, 0)
    rest_a = swap_axis(send[:half], "frame")
    first = collect_lines(first)
    second, first, rest_a, send = tie(second, first, rest_a, send)
    rest_b = swap_axis(send[half:], "frame")
    second = collect_lines(second)
    first = collect_half(first, 2, 1)
    own = pick(tokens, place, 0)
    g_own = pick(cotangent.transpose(0, 2, 1, 3), place, 0)
    first, second, own, g_own = tie(first, second, own, g_own)
    second = collect_half(second, 2, 1)
    second, rest_b, g_send = tie(second, rest_b, cotangent.transpose(0, 2, 1, 3))
    g_rest = swap_axis(pick(g_send, 1 - place, 0), "frame")
    first = merged(collect_half(first, 1, 2))
    second = merged(collect_half(second, 1, 2))
    rest = jnp.concatenate([rest_a, rest_b], axis=0).transpose(1, 0, 2)
    table = second[:, 2 * width : 2 * width + 3].astype(WIDE).T
    sgain, tgain, fgain = (table[index : index + 1] for index in range(3))
    in_o, qkv_o, o_o, after_o = space_forward(own, sgain, first, second)
    rest, after_o = tie(rest, after_o)
    in_r, qkv_r, o_r, after_r = space_forward(rest, sgain, first, second)
    g_rest, after_r = tie(g_rest, after_r)
    qkv_t, time_in, feed_in, hidden, mixed, mixed_r, g_time, gain_f = middle(
        spot, after_o, after_r, g_own, g_rest, tgain, fgain, packed
    )
    mixed_other = swap_axis(mixed_r, "frame")
    scatter = lambda item: lax.psum_scatter(item, axes, scatter_dimension=0, tiled=True)
    d_feed = feed_gradient(feed_in, hidden, width)
    d_feed, g_time = tie(d_feed, g_time)
    d_feed = scatter(d_feed)
    grads_t, gs_o, gs_r, gain_t = time_backward(
        qkv_t, g_time, after_o, after_r, tgain, packed
    )
    d_time = time_gradient(core, owners, time_in, grads_t, width)
    d_time, gs_r, mixed_other = tie(d_time, gs_r, mixed_other)
    d_time = scatter_columns(*scatter_core(*d_time))
    gq_r, sb_r, gx_r, gain_sr = space_backward(spot, rest, gs_r, qkv_r, sgain, first, second, LOW)
    grad_a = swap_axis(gx_r[:half], "frame")
    grad_b = swap_axis(gx_r[half:], "frame")
    d_time, gs_o, sb_r = tie(d_time, gs_o, sb_r)
    d_time = scatter_lines(*d_time)
    gq_o, sb_o, grad_tokens, gain_so = space_backward(spot, own, gs_o, qkv_o, sgain, first, second, WIDE)
    d_time, gq_o, sb_o, grad_a = tie(d_time, gq_o, sb_o, grad_a)
    gain_grads = jnp.stack(
        [jnp.sum(item, axis=0) for item in (gain_so + gain_sr, gain_t, gain_f)], axis=1
    )
    gain_grads = jnp.pad(gain_grads, ((0, 0), (0, LANES - 3))).astype(LOW)
    gain_grads = gain_grads.reshape(owners // 4, 2, 2 * share, LANES)
    gain_grads = [pick(gain_grads, side, 1) for side in (core[0], 1 - core[0])]
    inputs = [(flat_rows(in_o), flat_rows(gq_o)), (flat_rows(in_r), flat_rows(gq_r))]
    d_first = scatter_core(*split_gradient(core, owners, (inputs, 0, 3, 1, 0)))
    first_keep, first_send = column_parts(*d_first)
    first_keep, first_send, o_o = tie(first_keep, first_send, o_o)
    d_first = first_keep, flip(first_send, 2)
    outputs = [(flat_rows(o_o), flat_rows(sb_o)), (flat_rows(o_r), flat_rows(sb_r))]
    d_second = split_gradient(core, owners, (outputs, 0, 1, 1, 0))
    d_second = [
        jnp.concatenate([item, gain], axis=2) for item, gain in zip(d_second, gain_grads)
    ]
    d_second = scatter_core(*d_second)
    d_first, d_second, d_time, mixed_other, grad_a, grad_b, d_feed = tie(
        d_first, d_second, d_time, mixed_other, grad_a, grad_b, d_feed
    )
    d_first = scatter_lines(*d_first)
    d_second = scatter_columns(*d_second)
    d_time = scatter_frames(*d_time)
    d_feed = d_feed.astype(WIDE)
    d_up, d_down = d_feed[:, : blocks * width], d_feed[:, blocks * width :]
    d_up = d_up.reshape(share, blocks, owners, share).transpose(0, 2, 1, 3)
    d_up = d_up.reshape(up_proj.shape)
    d_down = d_down.reshape(share, blocks, width).transpose(1, 0, 2).reshape(down_proj.shape)
    mixed = lax.dynamic_update_index_in_dim(mixed, mixed_other, 1 - place, 0)
    for start, item in ((0, grad_a), (half, grad_b)):
        grad_tokens = lax.dynamic_update_slice(
            grad_tokens, item.astype(WIDE)[None], (1 - place, start, 0, 0)
        )
    d_first, mixed, grad_tokens, d_up, d_down = tie(d_first, mixed, grad_tokens, d_up, d_down)
    d_first = scatter_frames(*d_first)
    d_second = scatter_frames(*scatter_lines(*d_second))
    d_first, d_second, d_time = (added(*item) for item in (d_first, d_second, d_time))
    mixed, grad_tokens = mixed.transpose(0, 2, 1, 3), grad_tokens.transpose(0, 2, 1, 3)
    return (
        mixed,
        grad_tokens,
        d_second[:, width],
        d_second[:, width + 1],
        d_second[:, width + 2],
        d_first,
        d_second[:, :width],
        d_time[:, : 3 * width],
        d_time[:, 3 * width :],
        d_up,
        d_down,
    )


def shards(tokens, *others):
    frames = lax.axis_size("frame")
    local = frames == 2 and tokens.shape[0] == 2 and tokens.shape[1] == GROUP
    return (clip_local if local else general)(tokens, *others)


def solution(mesh):
    in_specs = (
        P("clip", "frame", None, None),
        P("clip", "frame", None, None),
        P(("clip", "frame")),
        P(("clip", "frame")),
        P(("clip", "frame")),
        P(("clip", "frame"), None),
        P(("clip", "frame"), None),
        P(("clip", "frame"), None),
        P(("clip", "frame"), None),
        P(("clip", "frame"), None),
        P(("clip", "frame"), None),
    )
    out_specs = (
        P("clip", "frame", None, None),
        P("clip", "frame", None, None),
        P(("clip", "frame")),
        P(("clip", "frame")),
        P(("clip", "frame")),
        P(("clip", "frame"), None),
        P(("clip", "frame"), None),
        P(("clip", "frame"), None),
        P(("clip", "frame"), None),
        P(("clip", "frame"), None),
        P(("clip", "frame"), None),
    )
    return jax.shard_map(shards, mesh=mesh, in_specs=in_specs, out_specs=out_specs, check_vma=False)
```

```python
import functools
import math

import jax
import jax.numpy as jnp
from jax import lax
from jax.experimental import pallas as pl
from jax.experimental.pallas import tpu as pltpu
from jax.sharding import PartitionSpec as P

HEADS = 12
HEAD = 64
PAIRS = HEADS // 2
LANES = 2 * HEAD
epsilon = 1e-06
LOW = jnp.bfloat16
WIDE = jnp.float32
NN = (((1,), (0,)), ((), ()))
NT = (((1,), (1,)), ((), ()))
TN = (((0,), (0,)), ((), ()))
SCALE = HEAD ** (-0.5)
POWER = SCALE * math.log2(math.e)
NEVER = -1e30
GROUP = 8
STEP = 2 * GROUP
LIMIT = 60 << 20
SHRINK = 6
TIME_BATCH = 12
SPACE_BATCH = 6


def dot(first, second, numbers=NN):
    return lax.dot_general(first, second, numbers, preferred_element_type=WIDE)


def norm_rows(values, gain):
    centred = values - jnp.mean(values, axis=-1, keepdims=True)
    inverse = lax.rsqrt(jnp.mean(centred * centred, axis=-1, keepdims=True) + epsilon)
    normed = centred * inverse
    return normed * gain, normed, inverse


def norm_back(gradient, normed, inverse, gain):
    scaled = gradient * gain
    return inverse * (
        scaled
        - jnp.mean(scaled, axis=-1, keepdims=True)
        - normed * jnp.mean(scaled * normed, axis=-1, keepdims=True)
    )


def fold_rows(values):
    rows, width = values.shape
    return jnp.sum(values.reshape(rows // 8, 8, width), axis=0)


def split_heads(values):
    first = lax.broadcasted_iota(jnp.int32, values.shape, 1) < HEAD
    zero = jnp.zeros_like(values)
    return jnp.where(first, values, zero), jnp.where(first, zero, values)


def join_heads(first, second):
    keep = lax.broadcasted_iota(jnp.int32, first.shape, 1) < HEAD
    return jnp.where(keep, first, second)


def stack_heads(values):
    return jnp.concatenate(split_heads(values), axis=0)


def halves(ref):
    middle_column = ref.shape[1] // 2
    return ref.at[:, :middle_column], ref.at[:, middle_column:]


def pair(ref, rows, part, index):
    start = (part * PAIRS + index) * LANES
    return ref[rows, start : start + LANES]


def batches(count, size):
    return [range(start, min(start + size, count)) for start in range(0, count, size)]


def time_batches(block):
    spots = [
        (slice(group * block, (group + 1) * block), index)
        for group in range(2)
        for index in range(PAIRS)
    ]
    return [spots[start : start + TIME_BATCH] for start in range(0, len(spots), TIME_BATCH)]


def shares(scores, axis):
    highest = [jnp.max(item, axis=axis, keepdims=True) for item in scores]
    powers = [jnp.exp2((item - top) * POWER) for item, top in zip(scores, highest)]
    totals = [jnp.sum(item, axis=axis, keepdims=True) for item in powers]
    return [item * (1.0 / total) for item, total in zip(powers, totals)]


def score_grads(chances, grads, axis):
    means = [jnp.sum(p * g, axis=axis, keepdims=True) for p, g in zip(chances, grads)]
    return [(p * (g - mean)).astype(LOW) for p, g, mean in zip(chances, grads, means)]


def load_padded(x_ref, pad_ref):
    frames, places, width = x_ref.shape

    @pl.when(pl.program_id(0) == 0)
    def _():
        pad_ref[...] = jnp.zeros_like(pad_ref)

    for frame in range(frames):
        pad_ref[frame, 0:places] = x_ref[frame].astype(WIDE)
    return pad_ref[...].reshape(frames * pad_ref.shape[1], width)


def space_forward_kernel(
    places, x_ref, gain_ref, qk_ref, v_ref, out_ref, in_ref, qkv_ref, o_ref, after_ref, pad_ref
):
    frames, padded, width = pad_ref.shape
    values = load_padded(x_ref, pad_ref)
    normed = norm_rows(values, gain_ref[...])[0].astype(LOW)
    in_ref[...] = normed.reshape(frames, padded, width)
    for start, ref in ((0, qk_ref), (2 * width, v_ref)):
        part = dot(normed, ref[...]).astype(LOW)
        qkv_ref[:, :, start : start + part.shape[1]] = part.reshape(frames, padded, -1)
    real = lax.broadcasted_iota(jnp.int32, (padded, padded), 1) < places

    def one_frame(frame):
        for batch in batches(PAIRS, SPACE_BATCH):
            part = lambda number, index: qkv_ref[
                frame, :, number * width + index * LANES : number * width + (index + 1) * LANES
            ]
            keys = [split_heads(part(1, index)) for index in batch]
            scores = [
                jnp.where(real, dot(part(0, index), key, NT), NEVER)
                for index, both in zip(batch, keys)
                for key in both
            ]
            chances = [item.astype(LOW) for item in shares(scores, 1)]
            outs = [
                dot(chances[2 * slot + head], part(2, index))
                for slot, index in enumerate(batch)
                for head in range(2)
            ]
            for slot, index in enumerate(batch):
                o_ref[frame, :, index * LANES : (index + 1) * LANES] = join_heads(
                    *outs[2 * slot : 2 * slot + 2]
                ).astype(LOW)

    for frame in range(frames):
        one_frame(frame)
    after = values + dot(o_ref[...].reshape(frames * padded, width), out_ref[...])
    after = after.reshape(frames, padded // GROUP, GROUP, width)
    for frame in range(frames):
        after_ref[:, frame] = after[frame].astype(after_ref.dtype)


def middle_kernel(
    places,
    place_ref,
    ao_ref,
    ar_ref,
    go_ref,
    gr_ref,
    tgain_ref,
    fgain_ref,
    tproj_ref,
    tout_ref,
    up_ref,
    down_ref,
    qkv_ref,
    time_ref,
    feed_ref,
    hidden_ref,
    mo_ref,
    mr_ref,
    gt_ref,
    gain_ref,
):
    half = ao_ref.shape[1]
    frames = half + ar_ref.shape[1]
    width = ao_ref.shape[3]
    int_ref, ot_ref = halves(time_ref)
    inf_ref, gb_ref = halves(feed_ref)
    gh_ref, act_ref = halves(hidden_ref)
    rows = 2 * frames * GROUP
    block = frames * GROUP
    values = jnp.concatenate([ao_ref[...].astype(WIDE), ar_ref[...].astype(WIDE)], axis=1).reshape(rows, width)
    in_time = norm_rows(values, tgain_ref[...])[0].astype(LOW)
    int_ref[...] = in_time
    qkv_ref[...] = dot(in_time, tproj_ref[...]).astype(LOW)
    across = lax.broadcasted_iota(jnp.int32, (block, block), 0)
    down = lax.broadcasted_iota(jnp.int32, (block, block), 1)
    bias = jnp.where(((across ^ down) & (GROUP - 1)) == 0, 0.0, NEVER)
    for batch in time_batches(block):
        both = [
            dot(pair(qkv_ref, own, 0, index), stack_heads(pair(qkv_ref, own, 1, index)), NT)
            for own, index in batch
        ]
        scores = [
            item[:, head * block : (head + 1) * block] + bias for item in both for head in range(2)
        ]
        chances = [item.astype(LOW) for item in shares(scores, 1)]
        results = [
            dot(
                jnp.concatenate(chances[2 * slot : 2 * slot + 2], axis=1),
                stack_heads(pair(qkv_ref, own, 2, index)),
            )
            for slot, (own, index) in enumerate(batch)
        ]
        for result, (own, index) in zip(results, batch):
            ot_ref[own, index * LANES : (index + 1) * LANES] = result.astype(LOW)
    values = values + dot(ot_ref[...], tout_ref[...])
    feed_gain = fgain_ref[...]
    in_feed, normed, inverse = norm_rows(values, feed_gain)
    in_feed = in_feed.astype(LOW)
    inf_ref[...] = in_feed
    place = pl.program_id(0) * STEP + lax.broadcasted_iota(jnp.int32, (STEP, half, width), 0)
    sides = [jnp.where(place < places, ref[...].astype(WIDE), 0.0) for ref in (go_ref, gr_ref)]
    gradient = jnp.concatenate(
        [
            jnp.swapaxes(side[start : start + GROUP], 0, 1).reshape(half * GROUP, width)
            for start in (0, GROUP)
            for side in sides
        ],
        axis=0,
    )
    grad_low = gradient.astype(LOW)
    gb_ref[...] = grad_low
    hidden_width = up_ref.shape[1]
    root = math.sqrt(2.0 / math.pi)
    cuts = [slice(start, start + width) for start in range(0, hidden_width, width)]

    def products(cut):
        return dot(in_feed, up_ref[:, cut]), dot(grad_low, down_ref[:, cut], NT)

    mixed = values
    ready = products(cuts[0])
    for number, cut in enumerate(cuts):
        hidden, grad_active = ready
        if number + 1 < len(cuts):
            ready = products(cuts[number + 1])
        square = hidden * hidden
        plus = 0.5 * jnp.tanh(hidden * (root + (root * 0.044715) * square)) + 0.5
        active = hidden * plus
        act_ref[:, cut] = active.astype(LOW)
        inner = 2.0 * root + (6.0 * root * 0.044715) * square
        gh_ref[:, cut] = (grad_active * (plus + active * (1.0 - plus) * inner)).astype(LOW)
    for cut in cuts:
        mixed = mixed + dot(act_ref[:, cut], down_ref[:, cut])
    back = dot(gh_ref[...], up_ref[...], NT)
    mixed = mixed.reshape(2, frames, GROUP, width)
    for group in range(2):
        cut = slice(group * GROUP, (group + 1) * GROUP)
        mo_ref[0, cut] = jnp.swapaxes(mixed[group, :half], 0, 1).astype(LOW)
        mr_ref[cut] = jnp.swapaxes(mixed[group, half:], 0, 1).astype(LOW)
    g_time = gradient + norm_back(back, normed, inverse, feed_gain)
    gt_ref[...] = g_time.astype(gt_ref.dtype)

    @pl.when(pl.program_id(0) == 0)
    def _():
        gain_ref[...] = jnp.zeros_like(gain_ref)

    gain_ref[...] += fold_rows(back * normed)


def time_backward_kernel(
    qkv_ref,
    gt_ref,
    ao_ref,
    ar_ref,
    tgain_ref,
    tout_ref,
    tproj_ref,
    grad_ref,
    gso_ref,
    gsr_ref,
    gain_ref,
    d_ref,
):
    half = ao_ref.shape[1]
    frames = half + ar_ref.shape[1]
    width = ao_ref.shape[3]
    rows = 2 * frames * GROUP
    block = frames * GROUP
    gq_ref, tb_ref = grad_ref.at[:, : 3 * width], grad_ref.at[:, 3 * width :]
    tb = gt_ref[...].astype(LOW)
    tb_ref[...] = tb
    d_ref[...] = dot(tb, tout_ref[...], NT).astype(LOW)
    across = lax.broadcasted_iota(jnp.int32, (block, block), 0)
    down = lax.broadcasted_iota(jnp.int32, (block, block), 1)
    bias = jnp.where(((across ^ down) & (GROUP - 1)) == 0, 0.0, NEVER)
    for batch in time_batches(block):
        keys = [stack_heads(pair(qkv_ref, own, 1, index)) for own, index in batch]
        both = [dot(key, pair(qkv_ref, own, 0, index), NT) for key, (own, index) in zip(keys, batch)]
        grad_both = [
            dot(stack_heads(pair(qkv_ref, own, 2, index)), pair(d_ref, own, 0, index), NT)
            for own, index in batch
        ]
        cuts = [slice(0, block), slice(block, 2 * block)]
        chances = shares([item[cut] + bias for item in both for cut in cuts], 0)
        grads = score_grads(chances, [item[cut] for item in grad_both for cut in cuts], 0)
        chances = [item.astype(LOW) for item in chances]
        results = []
        for slot, (own, index) in enumerate(batch):
            two = slice(2 * slot, 2 * slot + 2)
            grad = stack_heads(pair(d_ref, own, 0, index))
            queries = stack_heads(pair(qkv_ref, own, 0, index))
            results.append(
                (
                    dot(jnp.concatenate(grads[two], axis=0), keys[slot], TN) * SCALE,
                    dot(jnp.concatenate(grads[two], axis=1), queries) * SCALE,
                    dot(jnp.concatenate(chances[two], axis=1), grad),
                )
            )
        for items, (own, index) in zip(results, batch):
            for part, item in enumerate(items):
                start = (part * PAIRS + index) * LANES
                gq_ref[own, start : start + LANES] = item.astype(LOW)
    values = jnp.concatenate([ao_ref[...].astype(WIDE), ar_ref[...].astype(WIDE)], axis=1).reshape(rows, width)
    gain = tgain_ref[...]
    _, normed, inverse = norm_rows(values, gain)
    back = dot(gq_ref[...], tproj_ref[...], NT)
    result = gt_ref[...].astype(WIDE) + norm_back(back, normed, inverse, gain)
    for frame in range(frames):
        low = result[frame * GROUP : (frame + 1) * GROUP]
        high = result[block + frame * GROUP : block + (frame + 1) * GROUP]
        tile = jnp.concatenate([low, high], axis=0).astype(gso_ref.dtype)
        if frame < half:
            gso_ref[frame] = tile
        else:
            gsr_ref[frame - half] = tile

    @pl.when(pl.program_id(0) == 0)
    def _():
        gain_ref[...] = jnp.zeros_like(gain_ref)

    gain_ref[...] += fold_rows(back * normed)


def space_backward_kernel(
    places,
    place_ref,
    x_ref,
    gs_ref,
    qkv_ref,
    gain_row_ref,
    out_ref,
    qk_ref,
    v_ref,
    gq_ref,
    sb_ref,
    gx_ref,
    gain_ref,
    pad_ref,
    d_ref,
    order_ref,
):
    frames, padded, width = pad_ref.shape
    stride = order_ref.shape[1] // padded
    values = load_padded(x_ref, pad_ref)
    grad_space = gs_ref[...].astype(WIDE).reshape(frames * padded, width)
    sb = grad_space.astype(LOW)
    sb_ref[...] = sb.reshape(frames, padded, width)
    d_ref[...] = dot(sb, out_ref[...], NT).astype(LOW).reshape(frames, padded, width)
    real = lax.broadcasted_iota(jnp.int32, (padded, padded), 0) < places

    def one_frame(frame):
        for batch in batches(PAIRS, SPACE_BATCH):
            part = lambda number, index: qkv_ref[
                frame, :, number * width + index * LANES : number * width + (index + 1) * LANES
            ]
            grad = lambda index: d_ref[frame, :, index * LANES : (index + 1) * LANES]
            heads = [(index, head) for index in batch for head in range(2)]
            scores = [
                jnp.where(real, dot(split_heads(part(1, index))[head], part(0, index), NT), NEVER)
                for index, head in heads
            ]
            grad_shares = [
                dot(split_heads(part(2, index))[head], grad(index), NT) for index, head in heads
            ]
            chances = shares(scores, 0)
            grads = score_grads(chances, grad_shares, 0)
            chances = [item.astype(LOW) for item in chances]
            dq = [dot(ds, part(1, index), TN) * SCALE for ds, (index, _) in zip(grads, heads)]
            dk = [dot(ds, part(0, index)) * SCALE for ds, (index, _) in zip(grads, heads)]
            dv = [dot(p, grad(index)) for p, (index, _) in zip(chances, heads)]
            for number, items in enumerate((dq, dk, dv)):
                for slot, index in enumerate(batch):
                    start = number * width + index * LANES
                    gq_ref[frame, :, start : start + LANES] = join_heads(
                        items[2 * slot], items[2 * slot + 1]
                    ).astype(LOW)

    for frame in range(frames):
        one_frame(frame)
    gain = gain_row_ref[...]
    _, normed, inverse = norm_rows(values, gain)
    back = dot(gq_ref[:, :, : 2 * width].reshape(frames * padded, 2 * width), qk_ref[...], NT)
    back = back + dot(gq_ref[:, :, 2 * width :].reshape(frames * padded, width), v_ref[...], NT)
    result = grad_space + norm_back(back, normed, inverse, gain)
    result = result.reshape(frames, padded, width)
    for frame in range(frames):
        rows = pl.ds(pl.program_id(0) * frames + frame, padded, stride=stride)
        for lane in range(width // LANES):
            order_ref[lane, rows, :] = result[frame, :, lane * LANES : (lane + 1) * LANES]

    @pl.when(pl.program_id(0) == pl.num_programs(0) - 1)
    def _():
        for lane in range(width // LANES):
            tile = order_ref[lane, 0 : places * stride].astype(gx_ref.dtype)
            tile = tile.reshape(places, stride, LANES)
            if len(gx_ref.shape) == 4:
                gx_ref[0, :, :, lane * LANES : (lane + 1) * LANES] = tile
            else:
                gx_ref[:, :, lane * LANES : (lane + 1) * LANES] = tile

    @pl.when(pl.program_id(0) == 0)
    def _():
        gain_ref[...] = jnp.zeros_like(gain_ref)

    gain_ref[...] += fold_rows(back * normed)


def whole(shape):
    return pl.BlockSpec(
        shape, lambda *_: (0,) * len(shape), pipeline_mode=pl.Buffered(buffer_count=1)
    )


def columns(array, width, index):
    return pl.BlockSpec(
        (array.shape[0], width),
        lambda *_: (0, index),
        pipeline_mode=pl.Buffered(buffer_count=1),
    )


def params():
    return pltpu.CompilerParams(vmem_limit_bytes=LIMIT)


def cost(flops, *arrays):
    size = sum(math.prod(item.shape) * jnp.dtype(item.dtype).itemsize for item in arrays)
    return pl.CostEstimate(
        flops=int(flops) // SHRINK, bytes_accessed=int(size) // SHRINK, transcendentals=0
    )


def padded_places(places):
    return -(-places // STEP) * STEP


def by_frame(count, *tail):
    return pl.BlockSpec((count,) + tail, lambda step, *_: (step,) + (0,) * len(tail))


def space_forward(x, gain, first, second):
    frames, places, width = x.shape
    padded = padded_places(places)
    groups = padded // GROUP
    rows = frames * padded
    outs = (
        jax.ShapeDtypeStruct((frames, padded, width), LOW),
        jax.ShapeDtypeStruct((frames, padded, 3 * width), LOW),
        jax.ShapeDtypeStruct((frames, padded, width), LOW),
        jax.ShapeDtypeStruct((groups, frames, GROUP, width), WIDE),
    )
    flops = 2 * rows * width * 4 * width + 8 * rows * padded * width
    return pl.pallas_call(
        functools.partial(space_forward_kernel, places),
        grid=(frames // 2,),
        in_specs=[
            by_frame(2, places, width),
            whole(gain.shape),
            whole(first.shape),
            columns(second, width, 0),
            columns(second, width, 1),
        ],
        out_specs=[
            by_frame(2, padded, width),
            by_frame(2, padded, 3 * width),
            by_frame(2, padded, width),
            pl.BlockSpec((groups, 2, GROUP, width), lambda step: (0, step, 0, 0)),
        ],
        out_shape=outs,
        scratch_shapes=[pltpu.VMEM((2, padded, width), WIDE)],
        compiler_params=params(),
        cost_estimate=cost(flops, x, first, second, *outs),
        name="space_forward",
    )(x, gain, first, second, second)


def middle(place, after_own, after_rest, g_own, g_rest, tgain, fgain, packed):
    groups, half, _, width = after_own.shape
    places = g_own.shape[0]
    frames = 2 * half
    rows = groups * frames * GROUP
    block = 2 * frames * GROUP
    hidden = (packed.shape[1] - 4 * width) // 2
    padded = groups * GROUP
    outs = (
        jax.ShapeDtypeStruct((rows, 3 * width), LOW),
        jax.ShapeDtypeStruct((rows, 2 * width), LOW),
        jax.ShapeDtypeStruct((rows, 2 * width), LOW),
        jax.ShapeDtypeStruct((rows, 2 * hidden), LOW),
        jax.ShapeDtypeStruct((2, places, half, width), LOW),
        jax.ShapeDtypeStruct((places, half, width), LOW),
        jax.ShapeDtypeStruct((rows, width), WIDE),
        jax.ShapeDtypeStruct((8, width), WIDE),
    )
    by_row = lambda size: pl.BlockSpec((block, size), lambda step, place: (step, 0))
    by_group = pl.BlockSpec((2, half, GROUP, width), lambda step, place: (step, 0, 0, 0))
    by_place = pl.BlockSpec((STEP, half, width), lambda step, place: (step, 0, 0))
    flops = 2 * rows * width * (4 * width + 4 * hidden) + 8 * rows * frames * GROUP * width
    return pl.pallas_call(
        functools.partial(middle_kernel, places),
        grid_spec=pltpu.PrefetchScalarGridSpec(
            num_scalar_prefetch=1,
            grid=(groups // 2,),
            in_specs=[by_group, by_group, by_place, by_place]
            + [
                whole(tgain.shape),
                whole(fgain.shape),
                columns(packed, 3 * width, 0),
                columns(packed, width, 3),
                columns(packed, hidden, 1),
                columns(packed, hidden, 2),
            ],
            out_specs=[
                by_row(3 * width),
                by_row(2 * width),
                by_row(2 * width),
                by_row(2 * hidden),
                pl.BlockSpec((1, STEP, half, width), lambda step, place: (place[0], step, 0, 0)),
                by_place,
                by_row(width),
                pl.BlockSpec((8, width), lambda step, place: (0, 0)),
            ],
        ),
        out_shape=outs,
        compiler_params=params(),
        cost_estimate=cost(flops, after_own, after_rest, g_own, g_rest, *outs),
        name="middle",
    )(place, after_own, after_rest, g_own, g_rest, tgain, fgain, packed, packed, packed, packed)


def time_backward(qkv, g_time, after_own, after_rest, tgain, packed):
    groups, half, _, width = after_own.shape
    frames = 2 * half
    rows = groups * frames * GROUP
    block = 2 * frames * GROUP
    padded = groups * GROUP
    outs = (
        jax.ShapeDtypeStruct((rows, 4 * width), LOW),
        jax.ShapeDtypeStruct((half, padded, width), WIDE),
        jax.ShapeDtypeStruct((half, padded, width), WIDE),
        jax.ShapeDtypeStruct((8, width), WIDE),
    )
    by_row = lambda size: pl.BlockSpec((block, size), lambda step: (step, 0))
    by_group = pl.BlockSpec((2, half, GROUP, width), lambda step: (step, 0, 0, 0))
    by_place = pl.BlockSpec((half, STEP, width), lambda step: (0, step, 0))
    flops = 2 * rows * width * 4 * width + 20 * rows * frames * GROUP * width
    return pl.pallas_call(
        time_backward_kernel,
        grid=(groups // 2,),
        in_specs=[by_row(3 * width), by_row(width), by_group, by_group]
        + [whole(tgain.shape), columns(packed, width, 3), columns(packed, 3 * width, 0)],
        out_specs=[
            by_row(4 * width),
            by_place,
            by_place,
            pl.BlockSpec((8, width), lambda step: (0, 0)),
        ],
        out_shape=outs,
        scratch_shapes=[pltpu.VMEM((block, width), LOW)],
        compiler_params=params(),
        cost_estimate=cost(flops, qkv, g_time, after_own, after_rest, *outs),
        name="time_backward",
    )(qkv, g_time, after_own, after_rest, tgain, packed, packed)


def space_backward(place, x, g_space, qkv, gain, first, second, kind):
    frames, places, width = x.shape
    padded = padded_places(places)
    rows = frames * padded
    own = kind == WIDE
    shape = (2, places, frames, width) if own else (places, frames, width)
    outs = (
        jax.ShapeDtypeStruct((frames, padded, 3 * width), LOW),
        jax.ShapeDtypeStruct((frames, padded, width), LOW),
        jax.ShapeDtypeStruct(shape, kind),
        jax.ShapeDtypeStruct((8, width), WIDE),
    )
    flops = 2 * rows * width * 4 * width + 20 * rows * padded * width
    return pl.pallas_call(
        functools.partial(space_backward_kernel, places),
        grid_spec=pltpu.PrefetchScalarGridSpec(
            num_scalar_prefetch=1,
            grid=(frames // 2,),
            in_specs=[
                by_frame(2, places, width),
                by_frame(2, padded, width),
                by_frame(2, padded, 3 * width),
                whole(gain.shape),
                columns(second, width, 1),
                whole(first.shape),
                columns(second, width, 0),
            ],
            out_specs=[
                by_frame(2, padded, 3 * width),
                by_frame(2, padded, width),
                pl.BlockSpec((1,) + shape[1:], lambda step, place: (place[0], 0, 0, 0))
                if own
                else pl.BlockSpec(shape, lambda step, place: (0, 0, 0)),
                pl.BlockSpec((8, width), lambda step, place: (0, 0)),
            ],
            scratch_shapes=[
                pltpu.VMEM((2, padded, width), WIDE),
                pltpu.VMEM((2, padded, width), LOW),
                pltpu.VMEM((width // LANES, padded * frames, LANES), WIDE),
            ],
        ),
        out_shape=outs,
        compiler_params=params(),
        cost_estimate=cost(flops, x, g_space, qkv, *outs),
        name="space_backward",
    )(place, x, g_space, qkv, gain, second, first, second)


def gradient_kernel(parts, tiles, core_ref, *refs):
    step = pl.program_id(0)

    def emit(pairs):
        total = dot(pairs[0][0][...], pairs[0][1][...], TN)
        for first, second in pairs[1:]:
            total = total + dot(first[...], second[...], TN)
        split_owners(core_ref, total, *refs[-2:])

    start = 0
    for (first, last), count in zip(tiles, parts):
        group = refs[start : start + 2 * count]
        start += 2 * count
        pairs = [(group[2 * index], group[2 * index + 1]) for index in range(count)]
        pl.when((step >= first) & (step < last))(functools.partial(emit, pairs))


def plan_gradient(groups):
    width = groups[0][0][0][0].shape[1] if groups[0][3] == 1 else groups[0][0][0][1].shape[1]
    count = groups[-1][2]
    specs, arrays, parts, tiles = [], [], [], []
    flops = 0
    for pairs, first, last, side, offset in groups:
        parts.append(len(pairs))
        tiles.append((first, last))
        for pair_arrays in pairs:
            for index, item in enumerate(pair_arrays):
                rows = item.shape[0]
                if index == side and last - first > 1:
                    spec = pl.BlockSpec(
                        (rows, width),
                        lambda step, *_, first=first, last=last, offset=offset: (
                            0,
                            jnp.clip(step - first, 0, last - first - 1) + offset,
                        ),
                    )
                else:
                    fixed = offset if index == side else 0
                    spec = pl.BlockSpec(
                        (rows, width),
                        lambda step, *_, fixed=fixed: (0, fixed),
                        pipeline_mode=pl.Buffered(buffer_count=1),
                    )
                specs.append(spec)
                arrays.append(item)
            flops += 2 * rows * width * width * (last - first)
    return width, count, specs, arrays, parts, tiles, flops


def paired_specs(narrow, wide, width, turns):
    count = wide.shape[1] // width
    return count, [
        pl.BlockSpec((narrow.shape[0], width), lambda step, *_: (0, step // turns)),
        pl.BlockSpec((wide.shape[0], width), lambda step, *_: (0, step)),
    ]


def feed_gradient_kernel(turns, narrow_ref, wide_ref, out_ref):
    @pl.when(pl.program_id(0) < turns)
    def _():
        out_ref[...] = dot(narrow_ref[...], wide_ref[...], TN).astype(LOW)

    @pl.when(pl.program_id(0) >= turns)
    def _():
        out_ref[...] = dot(wide_ref[...], narrow_ref[...], TN).astype(LOW)


def feed_gradient(feed, hidden, width):
    turns = hidden.shape[1] // width // 2
    count, specs = paired_specs(feed, hidden, width, turns)
    out = jax.ShapeDtypeStruct((width, count * width), LOW)
    return pl.pallas_call(
        functools.partial(feed_gradient_kernel, turns),
        grid=(count,),
        in_specs=specs,
        out_specs=pl.BlockSpec((width, width), lambda step: (0, step)),
        out_shape=out,
        compiler_params=params(),
        cost_estimate=cost(2 * feed.shape[0] * width * width * count, feed, hidden, out),
        name="feed_gradient",
    )(feed, hidden)


def split_owners(core_ref, total, keep_ref, send_ref):
    total = total.reshape(keep_ref.shape[0], 2, keep_ref.shape[1], keep_ref.shape[2])
    total = total.astype(LOW)
    keep = core_ref[0] == 0
    keep_ref[...] = jnp.where(keep, total[:, 0], total[:, 1])
    send_ref[...] = jnp.where(keep, total[:, 1], total[:, 0])


def time_gradient_kernel(core_ref, narrow_ref, wide_ref, keep_ref, send_ref):
    split_owners(core_ref, dot(narrow_ref[...], wide_ref[...], TN), keep_ref, send_ref)


def time_gradient(core, owners, inputs, grads, width):
    count, specs = paired_specs(inputs, grads, width, 3)
    blocks, rows = owners // 4, 2 * (width // owners)
    out = jax.ShapeDtypeStruct((blocks, rows, count * width), LOW)
    out_spec = pl.BlockSpec((blocks, rows, width), lambda step, core: (0, 0, step))
    return pl.pallas_call(
        time_gradient_kernel,
        grid_spec=pltpu.PrefetchScalarGridSpec(
            num_scalar_prefetch=1, grid=(count,), in_specs=specs, out_specs=[out_spec, out_spec]
        ),
        out_shape=[out, out],
        compiler_params=params(),
        cost_estimate=cost(2 * inputs.shape[0] * width * width * count, inputs, grads, out, out),
        name="time_gradient",
    )(core, inputs, grads)


def split_gradient(core, owners, *groups):
    width, count, specs, arrays, parts, tiles, flops = plan_gradient(groups)
    blocks, rows = owners // 4, 2 * (width // owners)
    out = jax.ShapeDtypeStruct((blocks, rows, count * width), LOW)
    out_spec = pl.BlockSpec((blocks, rows, width), lambda step, core: (0, 0, step))
    return pl.pallas_call(
        functools.partial(gradient_kernel, parts, tiles),
        grid_spec=pltpu.PrefetchScalarGridSpec(
            num_scalar_prefetch=1,
            grid=(count,),
            in_specs=specs,
            out_specs=[out_spec, out_spec],
        ),
        out_shape=[out, out],
        compiler_params=params(),
        cost_estimate=cost(flops, *arrays, out, out),
        name="split_gradient",
    )(core, *arrays)


MICRO = 2


def norm_forward(values, gain):
    centred = values - jnp.mean(values, axis=-1, keepdims=True)
    inverse = lax.rsqrt(jnp.mean(centred * centred, axis=-1, keepdims=True) + epsilon)
    normed = centred * inverse
    return (normed * gain, normed, inverse)


def norm_backward(gradient, normed, inverse, gain):
    gain_grad = jnp.sum(gradient * normed, axis=(0, 1, 2))
    scaled = gradient * gain
    centred_grad = (
        scaled
        - jnp.mean(scaled, axis=-1, keepdims=True)
        - normed * jnp.mean(scaled * normed, axis=-1, keepdims=True)
    )
    return (inverse * centred_grad, gain_grad)


def to_places(blocks):
    clip_count, frames, places, model_width = blocks.shape
    return blocks.transpose(0, 2, 1, 3).reshape(clip_count * places, frames, HEADS, HEAD)


def from_places(attended, clip_count, places):
    frames = attended.shape[1]
    return attended.reshape(clip_count, places, frames, HEADS * HEAD).transpose(0, 2, 1, 3)


def attend_forward(queries, key_block, value_block):
    factor = HEAD ** (-0.5)
    scores = (
        jnp.einsum("blhe,bmhe->bhlm", queries, key_block, preferred_element_type=jnp.float32)
        * factor
    )
    highest = jnp.max(scores, axis=-1, keepdims=True)
    powers = jnp.exp(scores - highest)
    row_total = jnp.sum(powers, axis=-1, keepdims=True)
    chances = (powers / row_total).astype(jnp.bfloat16)
    result = jnp.einsum("bhlm,bmhe->blhe", chances, value_block, preferred_element_type=jnp.float32)
    return (result, highest + jnp.log(row_total))


def attend_backward(queries, key_block, value_block, logsum, grad_out):
    factor = HEAD ** (-0.5)
    scores = (
        jnp.einsum("blhe,bmhe->bhlm", queries, key_block, preferred_element_type=jnp.float32)
        * factor
    )
    chances = jnp.exp(scores - logsum)
    grad_chances = jnp.einsum(
        "blhe,bmhe->bhlm", grad_out, value_block, preferred_element_type=jnp.float32
    )
    grad_scores = (
        chances * (grad_chances - jnp.sum(chances * grad_chances, axis=-1, keepdims=True))
    ).astype(jnp.bfloat16)
    grad_queries = (
        jnp.einsum("bhlm,bmhe->blhe", grad_scores, key_block, preferred_element_type=jnp.float32)
        * factor
    )
    grad_keys = (
        jnp.einsum("bhlm,blhe->bmhe", grad_scores, queries, preferred_element_type=jnp.float32)
        * factor
    )
    grad_values = jnp.einsum(
        "bhlm,blhe->bmhe",
        chances.astype(jnp.bfloat16),
        grad_out,
        preferred_element_type=jnp.float32,
    )
    return (grad_queries, grad_keys, grad_values)


def project(values, matrix):
    return jnp.einsum("cfpd,de->cfpe", values, matrix, preferred_element_type=jnp.float32)


def project_back(gradient, matrix):
    return jnp.einsum("cfpe,de->cfpd", gradient, matrix, preferred_element_type=jnp.float32)


def outer_sum(values, gradient):
    return jnp.einsum("cfpd,cfpe->de", values, gradient, preferred_element_type=jnp.float32)


def forward(sample, gathered):
    (
        space_gain,
        time_gain,
        feed_gain,
        space_proj,
        space_out,
        time_proj,
        time_out,
        up_proj,
        down_proj,
    ) = gathered
    clip_count, frames, places, model_width = sample.shape
    normed_space = norm_forward(sample, space_gain.astype(jnp.float32))
    in_space = normed_space[0].astype(jnp.bfloat16)
    qkv_space = project(in_space, space_proj).astype(jnp.bfloat16)
    parted = qkv_space.reshape(clip_count * frames, places, 3, HEADS, HEAD)
    attended, logsum_space = attend_forward(parted[:, :, 0], parted[:, :, 1], parted[:, :, 2])
    out_space = attended.reshape(clip_count, frames, places, model_width).astype(jnp.bfloat16)
    after_space = sample + project(out_space, space_out)
    normed_time = norm_forward(after_space, time_gain.astype(jnp.float32))
    in_time = normed_time[0].astype(jnp.bfloat16)
    qkv_time = project(in_time, time_proj).astype(jnp.bfloat16)
    kv_whole = lax.all_gather(qkv_time[..., model_width:], "frame", axis=1, tiled=True)
    attended, logsum_time = attend_forward(
        to_places(qkv_time[..., :model_width]),
        to_places(kv_whole[..., :model_width]),
        to_places(kv_whole[..., model_width:]),
    )
    out_time = from_places(attended, clip_count, places).astype(jnp.bfloat16)
    after_time = after_space + project(out_time, time_out)
    normed_feed = norm_forward(after_time, feed_gain.astype(jnp.float32))
    in_feed = normed_feed[0].astype(jnp.bfloat16)
    hidden = project(in_feed, up_proj)
    active = jax.nn.gelu(hidden).astype(jnp.bfloat16)
    result = after_time + project(active, down_proj)
    saved = (
        normed_space,
        in_space,
        qkv_space,
        logsum_space,
        out_space,
        normed_time,
        in_time,
        qkv_time,
        kv_whole,
        logsum_time,
        out_time,
        normed_feed,
        in_feed,
        hidden,
        active,
    )
    return (result, saved)


def backward(gradient, saved, gathered):
    (
        space_gain,
        time_gain,
        feed_gain,
        space_proj,
        space_out,
        time_proj,
        time_out,
        up_proj,
        down_proj,
    ) = gathered
    (
        normed_space,
        in_space,
        qkv_space,
        logsum_space,
        out_space,
        normed_time,
        in_time,
        qkv_time,
        time_side,
        logsum_time,
        out_time,
        normed_feed,
        in_feed,
        hidden,
        active,
    ) = saved
    clip_count, frames, places, model_width = gradient.shape
    grad_low = gradient.astype(jnp.bfloat16)
    grad_down = outer_sum(active, grad_low)
    grad_active = project_back(grad_low, down_proj)
    gelu_value, gelu_pull = jax.vjp(jax.nn.gelu, hidden)
    grad_hidden = gelu_pull(grad_active)[0].astype(jnp.bfloat16)
    grad_up = outer_sum(in_feed, grad_hidden)
    back_feed, grad_feed_gain = norm_backward(
        project_back(grad_hidden, up_proj),
        normed_feed[1],
        normed_feed[2],
        feed_gain.astype(jnp.float32),
    )
    grad_time = gradient + back_feed
    time_low = grad_time.astype(jnp.bfloat16)
    grad_tout = outer_sum(out_time, time_low)
    grad_out_time = project_back(time_low, time_out).astype(jnp.bfloat16)
    grad_queries, grad_keys, grad_values = attend_backward(
        to_places(qkv_time[..., :model_width]),
        to_places(time_side[..., :model_width]),
        to_places(time_side[..., model_width:]),
        logsum_time,
        to_places(grad_out_time),
    )
    grad_kv = jnp.concatenate(
        (from_places(grad_keys, clip_count, places), from_places(grad_values, clip_count, places)),
        axis=-1,
    )
    grad_kv_own = lax.psum_scatter(
        grad_kv.astype(jnp.bfloat16), "frame", scatter_dimension=1, tiled=True
    ).astype(jnp.float32)
    grad_qkv_time = jnp.concatenate(
        (from_places(grad_queries, clip_count, places), grad_kv_own), axis=-1
    ).astype(jnp.bfloat16)
    grad_tproj = outer_sum(in_time, grad_qkv_time)
    back_time, grad_time_gain = norm_backward(
        project_back(grad_qkv_time, time_proj),
        normed_time[1],
        normed_time[2],
        time_gain.astype(jnp.float32),
    )
    grad_space = grad_time + back_time
    space_low = grad_space.astype(jnp.bfloat16)
    grad_sout = outer_sum(out_space, space_low)
    grad_out_space = project_back(space_low, space_out).astype(jnp.bfloat16)
    parted = qkv_space.reshape(clip_count * frames, places, 3, HEADS, HEAD)
    grad_queries, grad_keys, grad_values = attend_backward(
        parted[:, :, 0],
        parted[:, :, 1],
        parted[:, :, 2],
        logsum_space,
        grad_out_space.reshape(clip_count * frames, places, HEADS, HEAD),
    )
    grad_qkv_space = (
        jnp.stack((grad_queries, grad_keys, grad_values), axis=2)
        .reshape(clip_count, frames, places, 3 * model_width)
        .astype(jnp.bfloat16)
    )
    grad_sproj = outer_sum(in_space, grad_qkv_space)
    back_space, grad_space_gain = norm_backward(
        project_back(grad_qkv_space, space_proj),
        normed_space[1],
        normed_space[2],
        space_gain.astype(jnp.float32),
    )
    grad_input = grad_space + back_space
    return (
        grad_input,
        (
            grad_space_gain,
            grad_time_gain,
            grad_feed_gain,
            grad_sproj,
            grad_sout,
            grad_tproj,
            grad_tout,
            grad_up,
            grad_down,
        ),
    )


def general(
    tokens,
    cotangent,
    space_gain,
    time_gain,
    feed_gain,
    space_proj,
    space_out,
    time_proj,
    time_out,
    up_proj,
    down_proj,
):
    owned = (
        space_gain,
        time_gain,
        feed_gain,
        space_proj,
        space_out,
        time_proj,
        time_out,
        up_proj,
        down_proj,
    )
    devices_all = lax.axis_size(("clip", "frame"))
    per_micro = tokens.shape[0] // MICRO
    totals = tuple(
        (
            jnp.zeros((piece.shape[0] * devices_all,) + piece.shape[1:], jnp.float32)
            for piece in owned
        )
    )
    gathered = (
        lax.all_gather(space_gain, ("clip", "frame"), axis=0, tiled=True),
        lax.all_gather(time_gain, ("clip", "frame"), axis=0, tiled=True),
        lax.all_gather(feed_gain, ("clip", "frame"), axis=0, tiled=True),
        lax.all_gather(space_proj, ("clip", "frame"), axis=0, tiled=True),
        lax.all_gather(space_out, ("clip", "frame"), axis=0, tiled=True),
        lax.all_gather(time_proj, ("clip", "frame"), axis=0, tiled=True),
        lax.all_gather(time_out, ("clip", "frame"), axis=0, tiled=True),
        lax.all_gather(up_proj, ("clip", "frame"), axis=0, tiled=True),
        lax.all_gather(down_proj, ("clip", "frame"), axis=0, tiled=True),
    )
    mixed_parts = []
    grad_parts = []
    for micro_index in range(MICRO):
        sample = tokens[micro_index * per_micro : (micro_index + 1) * per_micro].astype(jnp.float32)
        result, saved = forward(sample, gathered)
        mixed_parts.append(result.astype(jnp.bfloat16))
        gradient = cotangent[micro_index * per_micro : (micro_index + 1) * per_micro].astype(
            jnp.float32
        )
        grad_input, grads = backward(gradient, saved, gathered)
        grad_parts.append(grad_input)
        totals = tuple((first + second for first, second in zip(totals, grads)))
    flat = tuple((item.reshape(-1) for item in totals))
    owners = (
        lax.psum_scatter(flat[0], ("clip", "frame"), scatter_dimension=0, tiled=True),
        lax.psum_scatter(flat[1], ("clip", "frame"), scatter_dimension=0, tiled=True),
        lax.psum_scatter(flat[2], ("clip", "frame"), scatter_dimension=0, tiled=True),
        lax.psum_scatter(flat[3], ("clip", "frame"), scatter_dimension=0, tiled=True),
        lax.psum_scatter(flat[4], ("clip", "frame"), scatter_dimension=0, tiled=True),
        lax.psum_scatter(flat[5], ("clip", "frame"), scatter_dimension=0, tiled=True),
        lax.psum_scatter(flat[6], ("clip", "frame"), scatter_dimension=0, tiled=True),
        lax.psum_scatter(flat[7], ("clip", "frame"), scatter_dimension=0, tiled=True),
        lax.psum_scatter(flat[8], ("clip", "frame"), scatter_dimension=0, tiled=True),
    )
    shaped = tuple((piece.reshape(mine.shape) for piece, mine in zip(owners, owned)))
    mixed = jnp.concatenate(mixed_parts, axis=0)
    grad_tokens = jnp.concatenate(grad_parts, axis=0)
    return (
        mixed,
        grad_tokens,
        shaped[0],
        shaped[1],
        shaped[2],
        shaped[3],
        shaped[4],
        shaped[5],
        shaped[6],
        shaped[7],
        shaped[8],
    )


def swap_axis(values, axis):
    size = lax.axis_size(axis)
    return lax.ppermute(values, axis, [(index, size - 1 - index) for index in range(size)])


def flip(values, mask):
    size = lax.axis_size("clip")
    return lax.ppermute(values, "clip", [(index, index ^ mask) for index in range(size)])


def tie(*items):
    return lax.optimization_barrier(items)


def bit_of(mask):
    return (lax.axis_index("clip") // mask) % 2


def in_order(bit, mine, other, axis):
    return jnp.where(
        bit == 0, jnp.stack([mine, other], axis=axis), jnp.stack([other, mine], axis=axis)
    )


def pick(values, index, axis):
    return lax.dynamic_index_in_dim(values, index, axis, keepdims=False)


def added(*items):
    return sum(item.astype(WIDE) for item in items)


def collect_start(shard):
    return in_order(lax.axis_index("frame"), shard, swap_axis(shard, "frame"), 0)


def collect_lines(item):
    line = lax.axis_index("clip") // 4
    parts = [item] + [flip(item, 4 * step) for step in range(1, 4)]
    odd, far = line % 2, line // 2
    parts = [jnp.where(odd == 0, parts[index], parts[index ^ 1]) for index in range(4)]
    parts = [jnp.where(far == 0, parts[index], parts[index ^ 2]) for index in range(4)]
    return jnp.stack(parts, axis=0)


def collect_half(item, mask, axis):
    return in_order(bit_of(mask), item, flip(item, mask), axis)


def merged(item):
    return item.reshape(-1, item.shape[-1])


def scatter_core(keep, send):
    return keep, flip(send, 1)


def column_parts(keep, other):
    shape = (4, 2) + keep.shape[1:]
    keep, other = keep.reshape(shape), other.reshape(shape)
    bit = bit_of(2)
    send = added(pick(keep, 1 - bit, 1), pick(other, 1 - bit, 1)).astype(LOW)
    return added(pick(keep, bit, 1), pick(other, bit, 1)).astype(LOW), send


def scatter_columns(keep, other):
    keep, send = column_parts(keep, other)
    return keep, flip(send, 2)


def scatter_lines(keep, other):
    line = lax.axis_index("clip") // 4
    total = added(keep, other).astype(LOW)
    parts = [flip(pick(total, line ^ step, 0), 4 * step) for step in range(1, 4)]
    return (pick(total, line, 0), *parts)


def scatter_frames(*parts):
    total = added(*parts).astype(LOW)
    total = total.reshape(2, total.shape[0] // 2, total.shape[1])
    place = lax.axis_index("frame")
    return pick(total, place, 0), swap_axis(pick(total, 1 - place, 0), "frame")


def flat_rows(values):
    return values.reshape(-1, values.shape[-1])


def clip_local(
    tokens,
    cotangent,
    space_gain,
    time_gain,
    feed_gain,
    space_proj,
    space_out,
    time_proj,
    time_out,
    up_proj,
    down_proj,
):
    axes = ("clip", "frame")
    place = lax.axis_index("frame")
    owners = lax.axis_size(axes)
    share, width = space_out.shape
    blocks = down_proj.shape[0] // share
    core = bit_of(1).reshape(1)
    spot = place.reshape(1)

    gains = jnp.stack([space_gain, time_gain, feed_gain], axis=1)
    gains = jnp.pad(gains, ((0, 0), (0, LANES - 3)))
    first = collect_start(space_proj[:, : 2 * width])
    second = collect_start(
        jnp.concatenate([space_proj[:, 2 * width :], space_out, gains], axis=1)
    )
    up_order = up_proj.reshape(share, owners, blocks, share).transpose(0, 2, 1, 3)
    down_order = down_proj.reshape(blocks, share, width).transpose(1, 0, 2)
    packed = jnp.concatenate(
        [time_proj, time_out, up_order.reshape(share, -1), down_order.reshape(share, -1)], axis=1
    )
    first, second, by_place, g_place, tokens, packed = tie(
        first, second, tokens.transpose(0, 2, 1, 3), cotangent.transpose(0, 2, 1, 3), tokens, packed
    )
    packed = lax.all_gather(packed, axes, axis=0, tiled=True)
    half = by_place.shape[1] // 2
    send = pick(by_place, 1 - place, 0)
    rest_a = swap_axis(send[:half], "frame")
    first = collect_lines(first)
    own, g_own, g_send = (
        pick(tokens, place, 0), pick(g_place, place, 0), pick(g_place, 1 - place, 0)
    )
    second, first, rest_a, send, own, g_own, g_send = tie(
        second, first, rest_a, send, own, g_own, g_send
    )
    rest_b = swap_axis(send[half:], "frame")
    second = collect_lines(second)
    first = collect_half(first, 2, 1)
    first, second = tie(first, second)
    second = collect_half(second, 2, 1)
    second, rest_b, g_send = tie(second, rest_b, g_send)
    g_rest = swap_axis(g_send, "frame")
    first = merged(collect_half(first, 1, 2))
    second = merged(collect_half(second, 1, 2))
    rest = jnp.concatenate([rest_a, rest_b], axis=0).transpose(1, 0, 2)
    table = second[:, 2 * width : 2 * width + 3].astype(WIDE).T
    sgain, tgain, fgain = (table[index : index + 1] for index in range(3))
    in_o, qkv_o, o_o, after_o = space_forward(own, sgain, first, second)
    rest, after_o = tie(rest, after_o)
    in_r, qkv_r, o_r, after_r = space_forward(rest, sgain, first, second)
    g_rest, after_r = tie(g_rest, after_r)
    qkv_t, time_in, feed_in, hidden, mixed, mixed_r, g_time, gain_f = middle(
        spot, after_o, after_r, g_own, g_rest, tgain, fgain, packed
    )
    mixed_other = swap_axis(mixed_r, "frame")
    scatter = lambda item: lax.psum_scatter(item, axes, scatter_dimension=0, tiled=True)
    d_feed = feed_gradient(feed_in, hidden, width)
    d_feed, g_time = tie(d_feed, g_time)
    d_feed = scatter(d_feed)
    grads_t, gs_o, gs_r, gain_t = time_backward(
        qkv_t, g_time, after_o, after_r, tgain, packed
    )
    d_time = time_gradient(core, owners, time_in, grads_t, width)
    d_time, gs_r, mixed_other = tie(d_time, gs_r, mixed_other)
    d_time = scatter_columns(*scatter_core(*d_time))
    gq_r, sb_r, gx_r, gain_sr = space_backward(spot, rest, gs_r, qkv_r, sgain, first, second, LOW)
    grad_a = swap_axis(gx_r[:half], "frame")
    grad_b = swap_axis(gx_r[half:], "frame")
    d_time, gs_o, sb_r = tie(d_time, gs_o, sb_r)
    d_time = scatter_lines(*d_time)
    gq_o, sb_o, grad_tokens, gain_so = space_backward(spot, own, gs_o, qkv_o, sgain, first, second, WIDE)
    d_time, gq_o, sb_o, grad_a = tie(d_time, gq_o, sb_o, grad_a)
    gain_grads = jnp.stack(
        [jnp.sum(item, axis=0) for item in (gain_so + gain_sr, gain_t, gain_f)], axis=1
    )
    gain_grads = jnp.pad(gain_grads, ((0, 0), (0, LANES - 3))).astype(LOW)
    gain_grads = gain_grads.reshape(owners // 4, 2, 2 * share, LANES)
    gain_grads = [pick(gain_grads, side, 1) for side in (core[0], 1 - core[0])]
    inputs = [(flat_rows(in_o), flat_rows(gq_o)), (flat_rows(in_r), flat_rows(gq_r))]
    d_first = scatter_core(*split_gradient(core, owners, (inputs, 0, 3, 1, 0)))
    first_keep, first_send = column_parts(*d_first)
    first_keep, first_send, o_o = tie(first_keep, first_send, o_o)
    d_first = first_keep, flip(first_send, 2)
    outputs = [(flat_rows(o_o), flat_rows(sb_o)), (flat_rows(o_r), flat_rows(sb_r))]
    d_second = split_gradient(core, owners, (outputs, 0, 1, 1, 0))
    d_second = [
        jnp.concatenate([item, gain], axis=2) for item, gain in zip(d_second, gain_grads)
    ]
    d_second = scatter_core(*d_second)
    d_first, d_second, d_time, mixed_other, grad_a, grad_b, d_feed = tie(
        d_first, d_second, d_time, mixed_other, grad_a, grad_b, d_feed
    )
    d_first = scatter_lines(*d_first)
    d_second = scatter_columns(*d_second)
    d_time = scatter_frames(*d_time)
    d_feed = d_feed.astype(WIDE)
    d_up, d_down = d_feed[:, : blocks * width], d_feed[:, blocks * width :]
    d_up = d_up.reshape(share, blocks, owners, share).transpose(0, 2, 1, 3)
    d_up = d_up.reshape(up_proj.shape)
    d_down = d_down.reshape(share, blocks, width).transpose(1, 0, 2).reshape(down_proj.shape)
    mixed = lax.dynamic_update_index_in_dim(mixed, mixed_other, 1 - place, 0)
    for start, item in ((0, grad_a), (half, grad_b)):
        grad_tokens = lax.dynamic_update_slice(
            grad_tokens, item.astype(WIDE)[None], (1 - place, start, 0, 0)
        )
    d_first, mixed, grad_tokens, d_up, d_down = tie(d_first, mixed, grad_tokens, d_up, d_down)
    d_first = scatter_frames(*d_first)
    d_second = scatter_frames(*scatter_lines(*d_second))
    d_first, d_second, d_time = (added(*item) for item in (d_first, d_second, d_time))
    mixed, grad_tokens = mixed.transpose(0, 2, 1, 3), grad_tokens.transpose(0, 2, 1, 3)
    return (
        mixed,
        grad_tokens,
        d_second[:, width],
        d_second[:, width + 1],
        d_second[:, width + 2],
        d_first,
        d_second[:, :width],
        d_time[:, : 3 * width],
        d_time[:, 3 * width :],
        d_up,
        d_down,
    )


def shards(tokens, *others):
    frames = lax.axis_size("frame")
    local = frames == 2 and tokens.shape[0] == 2 and tokens.shape[1] == GROUP
    return (clip_local if local else general)(tokens, *others)


def solution(mesh):
    in_specs = (
        P("clip", "frame", None, None),
        P("clip", "frame", None, None),
        P(("clip", "frame")),
        P(("clip", "frame")),
        P(("clip", "frame")),
        P(("clip", "frame"), None),
        P(("clip", "frame"), None),
        P(("clip", "frame"), None),
        P(("clip", "frame"), None),
        P(("clip", "frame"), None),
        P(("clip", "frame"), None),
    )
    out_specs = (
        P("clip", "frame", None, None),
        P("clip", "frame", None, None),
        P(("clip", "frame")),
        P(("clip", "frame")),
        P(("clip", "frame")),
        P(("clip", "frame"), None),
        P(("clip", "frame"), None),
        P(("clip", "frame"), None),
        P(("clip", "frame"), None),
        P(("clip", "frame"), None),
        P(("clip", "frame"), None),
    )
    return jax.shard_map(shards, mesh=mesh, in_specs=in_specs, out_specs=out_specs, check_vma=False)
```

```python
import functools
import math

import jax
import jax.numpy as jnp
from jax import lax
from jax.experimental import pallas as pl
from jax.experimental.pallas import tpu as pltpu
from jax.sharding import PartitionSpec as P

HEADS = 12
HEAD = 64
PAIRS = HEADS // 2
LANES = 2 * HEAD
epsilon = 1e-06
LOW = jnp.bfloat16
WIDE = jnp.float32
NN = (((1,), (0,)), ((), ()))
NT = (((1,), (1,)), ((), ()))
TN = (((0,), (0,)), ((), ()))
SCALE = HEAD ** (-0.5)
POWER = SCALE * math.log2(math.e)
NEVER = -1e30
GROUP = 8
STEP = 2 * GROUP
LIMIT = 60 << 20
SHRINK = 6
TIME_BATCH = 12
SPACE_BATCH = 6


def dot(first, second, numbers=NN):
    return lax.dot_general(first, second, numbers, preferred_element_type=WIDE)


def norm_rows(values, gain):
    centred = values - jnp.mean(values, axis=-1, keepdims=True)
    inverse = lax.rsqrt(jnp.mean(centred * centred, axis=-1, keepdims=True) + epsilon)
    normed = centred * inverse
    return normed * gain, normed, inverse


def norm_back(gradient, normed, inverse, gain):
    scaled = gradient * gain
    return inverse * (
        scaled
        - jnp.mean(scaled, axis=-1, keepdims=True)
        - normed * jnp.mean(scaled * normed, axis=-1, keepdims=True)
    )


def fold_rows(values):
    rows, width = values.shape
    return jnp.sum(values.reshape(rows // 8, 8, width), axis=0)


def split_heads(values):
    first = lax.broadcasted_iota(jnp.int32, values.shape, 1) < HEAD
    zero = jnp.zeros_like(values)
    return jnp.where(first, values, zero), jnp.where(first, zero, values)


def join_heads(first, second):
    keep = lax.broadcasted_iota(jnp.int32, first.shape, 1) < HEAD
    return jnp.where(keep, first, second)


def stack_heads(values):
    return jnp.concatenate(split_heads(values), axis=0)


def halves(ref):
    middle_column = ref.shape[1] // 2
    return ref.at[:, :middle_column], ref.at[:, middle_column:]


def pair(ref, rows, part, index):
    start = (part * PAIRS + index) * LANES
    return ref[rows, start : start + LANES]


def batches(count, size):
    return [range(start, min(start + size, count)) for start in range(0, count, size)]


def time_batches(block):
    spots = [
        (slice(group * block, (group + 1) * block), index)
        for group in range(2)
        for index in range(PAIRS)
    ]
    return [spots[start : start + TIME_BATCH] for start in range(0, len(spots), TIME_BATCH)]


def shares(scores, axis):
    highest = [jnp.max(item, axis=axis, keepdims=True) for item in scores]
    powers = [jnp.exp2((item - top) * POWER) for item, top in zip(scores, highest)]
    totals = [jnp.sum(item, axis=axis, keepdims=True) for item in powers]
    return [item * (1.0 / total) for item, total in zip(powers, totals)]


def score_grads(chances, grads, axis):
    means = [jnp.sum(p * g, axis=axis, keepdims=True) for p, g in zip(chances, grads)]
    return [(p * (g - mean)).astype(LOW) for p, g, mean in zip(chances, grads, means)]


def load_padded(x_ref, pad_ref):
    frames, places, width = x_ref.shape

    @pl.when(pl.program_id(0) == 0)
    def _():
        pad_ref[...] = jnp.zeros_like(pad_ref)

    for frame in range(frames):
        pad_ref[frame, 0:places] = x_ref[frame].astype(WIDE)
    return pad_ref[...].reshape(frames * pad_ref.shape[1], width)


def space_forward_kernel(
    places, x_ref, gain_ref, qk_ref, v_ref, out_ref, in_ref, qkv_ref, o_ref, after_ref, pad_ref
):
    frames, padded, width = pad_ref.shape
    values = load_padded(x_ref, pad_ref)
    normed = norm_rows(values, gain_ref[...])[0].astype(LOW)
    in_ref[...] = normed.reshape(frames, padded, width)
    for start, ref in ((0, qk_ref), (2 * width, v_ref)):
        part = dot(normed, ref[...]).astype(LOW)
        qkv_ref[:, :, start : start + part.shape[1]] = part.reshape(frames, padded, -1)
    real = lax.broadcasted_iota(jnp.int32, (padded, padded), 1) < places

    def one_frame(frame):
        for batch in batches(PAIRS, SPACE_BATCH):
            part = lambda number, index: qkv_ref[
                frame, :, number * width + index * LANES : number * width + (index + 1) * LANES
            ]
            keys = [split_heads(part(1, index)) for index in batch]
            scores = [
                jnp.where(real, dot(part(0, index), key, NT), NEVER)
                for index, both in zip(batch, keys)
                for key in both
            ]
            chances = [item.astype(LOW) for item in shares(scores, 1)]
            outs = [
                dot(chances[2 * slot + head], part(2, index))
                for slot, index in enumerate(batch)
                for head in range(2)
            ]
            for slot, index in enumerate(batch):
                o_ref[frame, :, index * LANES : (index + 1) * LANES] = join_heads(
                    *outs[2 * slot : 2 * slot + 2]
                ).astype(LOW)

    for frame in range(frames):
        one_frame(frame)
    after = values + dot(o_ref[...].reshape(frames * padded, width), out_ref[...])
    after = after.reshape(frames, padded // GROUP, GROUP, width)
    for frame in range(frames):
        after_ref[:, frame] = after[frame].astype(after_ref.dtype)


def middle_kernel(
    places,
    place_ref,
    ao_ref,
    ar_ref,
    go_ref,
    gr_ref,
    tgain_ref,
    fgain_ref,
    tproj_ref,
    tout_ref,
    up_ref,
    down_ref,
    qkv_ref,
    time_ref,
    feed_ref,
    hidden_ref,
    mo_ref,
    mr_ref,
    gt_ref,
    gain_ref,
):
    half = ao_ref.shape[1]
    frames = half + ar_ref.shape[1]
    width = ao_ref.shape[3]
    int_ref, ot_ref = halves(time_ref)
    inf_ref, gb_ref = halves(feed_ref)
    gh_ref, act_ref = halves(hidden_ref)
    rows = 2 * frames * GROUP
    block = frames * GROUP
    values = jnp.concatenate([ao_ref[...].astype(WIDE), ar_ref[...].astype(WIDE)], axis=1).reshape(rows, width)
    in_time = norm_rows(values, tgain_ref[...])[0].astype(LOW)
    int_ref[...] = in_time
    qkv_ref[...] = dot(in_time, tproj_ref[...]).astype(LOW)
    across = lax.broadcasted_iota(jnp.int32, (block, block), 0)
    down = lax.broadcasted_iota(jnp.int32, (block, block), 1)
    bias = jnp.where(((across ^ down) & (GROUP - 1)) == 0, 0.0, NEVER)
    for batch in time_batches(block):
        both = [
            dot(pair(qkv_ref, own, 0, index), stack_heads(pair(qkv_ref, own, 1, index)), NT)
            for own, index in batch
        ]
        scores = [
            item[:, head * block : (head + 1) * block] + bias for item in both for head in range(2)
        ]
        chances = [item.astype(LOW) for item in shares(scores, 1)]
        results = [
            dot(
                jnp.concatenate(chances[2 * slot : 2 * slot + 2], axis=1),
                stack_heads(pair(qkv_ref, own, 2, index)),
            )
            for slot, (own, index) in enumerate(batch)
        ]
        for result, (own, index) in zip(results, batch):
            ot_ref[own, index * LANES : (index + 1) * LANES] = result.astype(LOW)
    values = values + dot(ot_ref[...], tout_ref[...])
    feed_gain = fgain_ref[...]
    in_feed, normed, inverse = norm_rows(values, feed_gain)
    in_feed = in_feed.astype(LOW)
    inf_ref[...] = in_feed
    place = pl.program_id(0) * STEP + lax.broadcasted_iota(jnp.int32, (STEP, half, width), 0)
    sides = [jnp.where(place < places, ref[...].astype(WIDE), 0.0) for ref in (go_ref, gr_ref)]
    gradient = jnp.concatenate(
        [
            jnp.swapaxes(side[start : start + GROUP], 0, 1).reshape(half * GROUP, width)
            for start in (0, GROUP)
            for side in sides
        ],
        axis=0,
    )
    grad_low = gradient.astype(LOW)
    gb_ref[...] = grad_low
    hidden_width = up_ref.shape[1]
    root = math.sqrt(2.0 / math.pi)
    cuts = [slice(start, start + width) for start in range(0, hidden_width, width)]

    def products(cut):
        return dot(in_feed, up_ref[:, cut]), dot(grad_low, down_ref[:, cut], NT)

    mixed = values
    ready = products(cuts[0])
    for number, cut in enumerate(cuts):
        hidden, grad_active = ready
        if number + 1 < len(cuts):
            ready = products(cuts[number + 1])
        square = hidden * hidden
        plus = 0.5 * jnp.tanh(hidden * (root + (root * 0.044715) * square)) + 0.5
        active = hidden * plus
        act_ref[:, cut] = active.astype(LOW)
        inner = 2.0 * root + (6.0 * root * 0.044715) * square
        gh_ref[:, cut] = (grad_active * (plus + active * (1.0 - plus) * inner)).astype(LOW)
    for cut in cuts:
        mixed = mixed + dot(act_ref[:, cut], down_ref[:, cut])
    back = dot(gh_ref[...], up_ref[...], NT)
    mixed = mixed.reshape(2, frames, GROUP, width)
    for group in range(2):
        cut = slice(group * GROUP, (group + 1) * GROUP)
        mo_ref[0, cut] = jnp.swapaxes(mixed[group, :half], 0, 1).astype(LOW)
        mr_ref[cut] = jnp.swapaxes(mixed[group, half:], 0, 1).astype(LOW)
    g_time = gradient + norm_back(back, normed, inverse, feed_gain)
    gt_ref[...] = g_time.astype(gt_ref.dtype)

    @pl.when(pl.program_id(0) == 0)
    def _():
        gain_ref[...] = jnp.zeros_like(gain_ref)

    gain_ref[...] += fold_rows(back * normed)


def time_backward_kernel(
    qkv_ref,
    gt_ref,
    ao_ref,
    ar_ref,
    tgain_ref,
    tout_ref,
    tproj_ref,
    grad_ref,
    gso_ref,
    gsr_ref,
    gain_ref,
    d_ref,
):
    half = ao_ref.shape[1]
    frames = half + ar_ref.shape[1]
    width = ao_ref.shape[3]
    rows = 2 * frames * GROUP
    block = frames * GROUP
    gq_ref, tb_ref = grad_ref.at[:, : 3 * width], grad_ref.at[:, 3 * width :]
    tb = gt_ref[...].astype(LOW)
    tb_ref[...] = tb
    d_ref[...] = dot(tb, tout_ref[...], NT).astype(LOW)
    across = lax.broadcasted_iota(jnp.int32, (block, block), 0)
    down = lax.broadcasted_iota(jnp.int32, (block, block), 1)
    bias = jnp.where(((across ^ down) & (GROUP - 1)) == 0, 0.0, NEVER)
    for batch in time_batches(block):
        keys = [stack_heads(pair(qkv_ref, own, 1, index)) for own, index in batch]
        both = [dot(key, pair(qkv_ref, own, 0, index), NT) for key, (own, index) in zip(keys, batch)]
        grad_both = [
            dot(stack_heads(pair(qkv_ref, own, 2, index)), pair(d_ref, own, 0, index), NT)
            for own, index in batch
        ]
        cuts = [slice(0, block), slice(block, 2 * block)]
        chances = shares([item[cut] + bias for item in both for cut in cuts], 0)
        grads = score_grads(chances, [item[cut] for item in grad_both for cut in cuts], 0)
        chances = [item.astype(LOW) for item in chances]
        results = []
        for slot, (own, index) in enumerate(batch):
            two = slice(2 * slot, 2 * slot + 2)
            grad = stack_heads(pair(d_ref, own, 0, index))
            queries = stack_heads(pair(qkv_ref, own, 0, index))
            results.append(
                (
                    dot(jnp.concatenate(grads[two], axis=0), keys[slot], TN) * SCALE,
                    dot(jnp.concatenate(grads[two], axis=1), queries) * SCALE,
                    dot(jnp.concatenate(chances[two], axis=1), grad),
                )
            )
        for items, (own, index) in zip(results, batch):
            for part, item in enumerate(items):
                start = (part * PAIRS + index) * LANES
                gq_ref[own, start : start + LANES] = item.astype(LOW)
    values = jnp.concatenate([ao_ref[...].astype(WIDE), ar_ref[...].astype(WIDE)], axis=1).reshape(rows, width)
    gain = tgain_ref[...]
    _, normed, inverse = norm_rows(values, gain)
    back = dot(gq_ref[...], tproj_ref[...], NT)
    result = gt_ref[...].astype(WIDE) + norm_back(back, normed, inverse, gain)
    for frame in range(frames):
        low = result[frame * GROUP : (frame + 1) * GROUP]
        high = result[block + frame * GROUP : block + (frame + 1) * GROUP]
        tile = jnp.concatenate([low, high], axis=0).astype(gso_ref.dtype)
        if frame < half:
            gso_ref[frame] = tile
        else:
            gsr_ref[frame - half] = tile

    @pl.when(pl.program_id(0) == 0)
    def _():
        gain_ref[...] = jnp.zeros_like(gain_ref)

    gain_ref[...] += fold_rows(back * normed)


def space_backward_kernel(
    places,
    place_ref,
    x_ref,
    gs_ref,
    qkv_ref,
    gain_row_ref,
    out_ref,
    qk_ref,
    v_ref,
    gq_ref,
    sb_ref,
    gx_ref,
    gain_ref,
    pad_ref,
    d_ref,
    order_ref,
):
    frames, padded, width = pad_ref.shape
    stride = order_ref.shape[1] // padded
    values = load_padded(x_ref, pad_ref)
    grad_space = gs_ref[...].astype(WIDE).reshape(frames * padded, width)
    sb = grad_space.astype(LOW)
    sb_ref[...] = sb.reshape(frames, padded, width)
    d_ref[...] = dot(sb, out_ref[...], NT).astype(LOW).reshape(frames, padded, width)
    real = lax.broadcasted_iota(jnp.int32, (padded, padded), 0) < places

    def one_frame(frame):
        for batch in batches(PAIRS, SPACE_BATCH):
            part = lambda number, index: qkv_ref[
                frame, :, number * width + index * LANES : number * width + (index + 1) * LANES
            ]
            grad = lambda index: d_ref[frame, :, index * LANES : (index + 1) * LANES]
            heads = [(index, head) for index in batch for head in range(2)]
            scores = [
                jnp.where(real, dot(split_heads(part(1, index))[head], part(0, index), NT), NEVER)
                for index, head in heads
            ]
            grad_shares = [
                dot(split_heads(part(2, index))[head], grad(index), NT) for index, head in heads
            ]
            chances = shares(scores, 0)
            grads = score_grads(chances, grad_shares, 0)
            chances = [item.astype(LOW) for item in chances]
            dq = [dot(ds, part(1, index), TN) * SCALE for ds, (index, _) in zip(grads, heads)]
            dk = [dot(ds, part(0, index)) * SCALE for ds, (index, _) in zip(grads, heads)]
            dv = [dot(p, grad(index)) for p, (index, _) in zip(chances, heads)]
            for number, items in enumerate((dq, dk, dv)):
                for slot, index in enumerate(batch):
                    start = number * width + index * LANES
                    gq_ref[frame, :, start : start + LANES] = join_heads(
                        items[2 * slot], items[2 * slot + 1]
                    ).astype(LOW)

    for frame in range(frames):
        one_frame(frame)
    gain = gain_row_ref[...]
    _, normed, inverse = norm_rows(values, gain)
    back = dot(gq_ref[:, :, : 2 * width].reshape(frames * padded, 2 * width), qk_ref[...], NT)
    back = back + dot(gq_ref[:, :, 2 * width :].reshape(frames * padded, width), v_ref[...], NT)
    result = grad_space + norm_back(back, normed, inverse, gain)
    result = result.reshape(frames, padded, width)
    for frame in range(frames):
        rows = pl.ds(pl.program_id(0) * frames + frame, padded, stride=stride)
        for lane in range(width // LANES):
            order_ref[lane, rows, :] = result[frame, :, lane * LANES : (lane + 1) * LANES]

    @pl.when(pl.program_id(0) == pl.num_programs(0) - 1)
    def _():
        for lane in range(width // LANES):
            tile = order_ref[lane, 0 : places * stride].astype(gx_ref.dtype)
            tile = tile.reshape(places, stride, LANES)
            if len(gx_ref.shape) == 4:
                gx_ref[0, :, :, lane * LANES : (lane + 1) * LANES] = tile
            else:
                gx_ref[:, :, lane * LANES : (lane + 1) * LANES] = tile

    @pl.when(pl.program_id(0) == 0)
    def _():
        gain_ref[...] = jnp.zeros_like(gain_ref)

    gain_ref[...] += fold_rows(back * normed)


def whole(shape):
    return pl.BlockSpec(
        shape, lambda *_: (0,) * len(shape), pipeline_mode=pl.Buffered(buffer_count=1)
    )


def columns(array, width, index):
    return pl.BlockSpec(
        (array.shape[0], width),
        lambda *_: (0, index),
        pipeline_mode=pl.Buffered(buffer_count=1),
    )


def params():
    return pltpu.CompilerParams(vmem_limit_bytes=LIMIT)


def cost(flops, *arrays):
    size = sum(math.prod(item.shape) * jnp.dtype(item.dtype).itemsize for item in arrays)
    return pl.CostEstimate(
        flops=int(flops) // SHRINK, bytes_accessed=int(size) // SHRINK, transcendentals=0
    )


def padded_places(places):
    return -(-places // STEP) * STEP


def by_frame(count, *tail):
    return pl.BlockSpec((count,) + tail, lambda step, *_: (step,) + (0,) * len(tail))


def space_forward(x, gain, first, second):
    frames, places, width = x.shape
    padded = padded_places(places)
    groups = padded // GROUP
    rows = frames * padded
    outs = (
        jax.ShapeDtypeStruct((frames, padded, width), LOW),
        jax.ShapeDtypeStruct((frames, padded, 3 * width), LOW),
        jax.ShapeDtypeStruct((frames, padded, width), LOW),
        jax.ShapeDtypeStruct((groups, frames, GROUP, width), WIDE),
    )
    flops = 2 * rows * width * 4 * width + 8 * rows * padded * width
    return pl.pallas_call(
        functools.partial(space_forward_kernel, places),
        grid=(frames // 2,),
        in_specs=[
            by_frame(2, places, width),
            whole(gain.shape),
            whole(first.shape),
            columns(second, width, 0),
            columns(second, width, 1),
        ],
        out_specs=[
            by_frame(2, padded, width),
            by_frame(2, padded, 3 * width),
            by_frame(2, padded, width),
            pl.BlockSpec((groups, 2, GROUP, width), lambda step: (0, step, 0, 0)),
        ],
        out_shape=outs,
        scratch_shapes=[pltpu.VMEM((2, padded, width), WIDE)],
        compiler_params=params(),
        cost_estimate=cost(flops, x, first, second, *outs),
        name="space_forward",
    )(x, gain, first, second, second)


def middle(place, after_own, after_rest, g_own, g_rest, tgain, fgain, packed):
    groups, half, _, width = after_own.shape
    places = g_own.shape[0]
    frames = 2 * half
    rows = groups * frames * GROUP
    block = 2 * frames * GROUP
    hidden = (packed.shape[1] - 4 * width) // 2
    padded = groups * GROUP
    outs = (
        jax.ShapeDtypeStruct((rows, 3 * width), LOW),
        jax.ShapeDtypeStruct((rows, 2 * width), LOW),
        jax.ShapeDtypeStruct((rows, 2 * width), LOW),
        jax.ShapeDtypeStruct((rows, 2 * hidden), LOW),
        jax.ShapeDtypeStruct((2, places, half, width), LOW),
        jax.ShapeDtypeStruct((places, half, width), LOW),
        jax.ShapeDtypeStruct((rows, width), WIDE),
        jax.ShapeDtypeStruct((8, width), WIDE),
    )
    by_row = lambda size: pl.BlockSpec((block, size), lambda step, place: (step, 0))
    by_group = pl.BlockSpec((2, half, GROUP, width), lambda step, place: (step, 0, 0, 0))
    by_place = pl.BlockSpec((STEP, half, width), lambda step, place: (step, 0, 0))
    flops = 2 * rows * width * (4 * width + 4 * hidden) + 8 * rows * frames * GROUP * width
    return pl.pallas_call(
        functools.partial(middle_kernel, places),
        grid_spec=pltpu.PrefetchScalarGridSpec(
            num_scalar_prefetch=1,
            grid=(groups // 2,),
            in_specs=[by_group, by_group, by_place, by_place]
            + [
                whole(tgain.shape),
                whole(fgain.shape),
                columns(packed, 3 * width, 0),
                columns(packed, width, 3),
                columns(packed, hidden, 1),
                columns(packed, hidden, 2),
            ],
            out_specs=[
                by_row(3 * width),
                by_row(2 * width),
                by_row(2 * width),
                by_row(2 * hidden),
                pl.BlockSpec((1, STEP, half, width), lambda step, place: (place[0], step, 0, 0)),
                by_place,
                by_row(width),
                pl.BlockSpec((8, width), lambda step, place: (0, 0)),
            ],
        ),
        out_shape=outs,
        compiler_params=params(),
        cost_estimate=cost(flops, after_own, after_rest, g_own, g_rest, *outs),
        name="middle",
    )(place, after_own, after_rest, g_own, g_rest, tgain, fgain, packed, packed, packed, packed)


def time_backward(qkv, g_time, after_own, after_rest, tgain, packed):
    groups, half, _, width = after_own.shape
    frames = 2 * half
    rows = groups * frames * GROUP
    block = 2 * frames * GROUP
    padded = groups * GROUP
    outs = (
        jax.ShapeDtypeStruct((rows, 4 * width), LOW),
        jax.ShapeDtypeStruct((half, padded, width), WIDE),
        jax.ShapeDtypeStruct((half, padded, width), WIDE),
        jax.ShapeDtypeStruct((8, width), WIDE),
    )
    by_row = lambda size: pl.BlockSpec((block, size), lambda step: (step, 0))
    by_group = pl.BlockSpec((2, half, GROUP, width), lambda step: (step, 0, 0, 0))
    by_place = pl.BlockSpec((half, STEP, width), lambda step: (0, step, 0))
    flops = 2 * rows * width * 4 * width + 20 * rows * frames * GROUP * width
    return pl.pallas_call(
        time_backward_kernel,
        grid=(groups // 2,),
        in_specs=[by_row(3 * width), by_row(width), by_group, by_group]
        + [whole(tgain.shape), columns(packed, width, 3), columns(packed, 3 * width, 0)],
        out_specs=[
            by_row(4 * width),
            by_place,
            by_place,
            pl.BlockSpec((8, width), lambda step: (0, 0)),
        ],
        out_shape=outs,
        scratch_shapes=[pltpu.VMEM((block, width), LOW)],
        compiler_params=params(),
        cost_estimate=cost(flops, qkv, g_time, after_own, after_rest, *outs),
        name="time_backward",
    )(qkv, g_time, after_own, after_rest, tgain, packed, packed)


def space_backward(place, x, g_space, qkv, gain, first, second, kind):
    frames, places, width = x.shape
    padded = padded_places(places)
    rows = frames * padded
    own = kind == WIDE
    shape = (2, places, frames, width) if own else (places, frames, width)
    outs = (
        jax.ShapeDtypeStruct((frames, padded, 3 * width), LOW),
        jax.ShapeDtypeStruct((frames, padded, width), LOW),
        jax.ShapeDtypeStruct(shape, kind),
        jax.ShapeDtypeStruct((8, width), WIDE),
    )
    flops = 2 * rows * width * 4 * width + 20 * rows * padded * width
    return pl.pallas_call(
        functools.partial(space_backward_kernel, places),
        grid_spec=pltpu.PrefetchScalarGridSpec(
            num_scalar_prefetch=1,
            grid=(frames // 2,),
            in_specs=[
                by_frame(2, places, width),
                by_frame(2, padded, width),
                by_frame(2, padded, 3 * width),
                whole(gain.shape),
                columns(second, width, 1),
                whole(first.shape),
                columns(second, width, 0),
            ],
            out_specs=[
                by_frame(2, padded, 3 * width),
                by_frame(2, padded, width),
                pl.BlockSpec((1,) + shape[1:], lambda step, place: (place[0], 0, 0, 0))
                if own
                else pl.BlockSpec(shape, lambda step, place: (0, 0, 0)),
                pl.BlockSpec((8, width), lambda step, place: (0, 0)),
            ],
            scratch_shapes=[
                pltpu.VMEM((2, padded, width), WIDE),
                pltpu.VMEM((2, padded, width), LOW),
                pltpu.VMEM((width // LANES, padded * frames, LANES), WIDE),
            ],
        ),
        out_shape=outs,
        compiler_params=params(),
        cost_estimate=cost(flops, x, g_space, qkv, *outs),
        name="space_backward",
    )(place, x, g_space, qkv, gain, second, first, second)


def gradient_kernel(parts, tiles, core_ref, *refs):
    step = pl.program_id(0)

    def emit(pairs):
        total = dot(pairs[0][0][...], pairs[0][1][...], TN)
        for first, second in pairs[1:]:
            total = total + dot(first[...], second[...], TN)
        split_owners(core_ref, total, *refs[-2:])

    start = 0
    for (first, last), count in zip(tiles, parts):
        group = refs[start : start + 2 * count]
        start += 2 * count
        pairs = [(group[2 * index], group[2 * index + 1]) for index in range(count)]
        pl.when((step >= first) & (step < last))(functools.partial(emit, pairs))


def plan_gradient(groups):
    width = groups[0][0][0][0].shape[1] if groups[0][3] == 1 else groups[0][0][0][1].shape[1]
    count = groups[-1][2]
    specs, arrays, parts, tiles = [], [], [], []
    flops = 0
    for pairs, first, last, side, offset in groups:
        parts.append(len(pairs))
        tiles.append((first, last))
        for pair_arrays in pairs:
            for index, item in enumerate(pair_arrays):
                rows = item.shape[0]
                if index == side and last - first > 1:
                    spec = pl.BlockSpec(
                        (rows, width),
                        lambda step, *_, first=first, last=last, offset=offset: (
                            0,
                            jnp.clip(step - first, 0, last - first - 1) + offset,
                        ),
                    )
                else:
                    fixed = offset if index == side else 0
                    spec = pl.BlockSpec(
                        (rows, width),
                        lambda step, *_, fixed=fixed: (0, fixed),
                        pipeline_mode=pl.Buffered(buffer_count=1),
                    )
                specs.append(spec)
                arrays.append(item)
            flops += 2 * rows * width * width * (last - first)
    return width, count, specs, arrays, parts, tiles, flops


def paired_specs(narrow, wide, width, turns):
    count = wide.shape[1] // width
    return count, [
        pl.BlockSpec((narrow.shape[0], width), lambda step, *_: (0, step // turns)),
        pl.BlockSpec((wide.shape[0], width), lambda step, *_: (0, step)),
    ]


def feed_gradient_kernel(turns, narrow_ref, wide_ref, out_ref):
    @pl.when(pl.program_id(0) < turns)
    def _():
        out_ref[...] = dot(narrow_ref[...], wide_ref[...], TN).astype(LOW)

    @pl.when(pl.program_id(0) >= turns)
    def _():
        out_ref[...] = dot(wide_ref[...], narrow_ref[...], TN).astype(LOW)


def feed_gradient(feed, hidden, width):
    turns = hidden.shape[1] // width // 2
    count, specs = paired_specs(feed, hidden, width, turns)
    out = jax.ShapeDtypeStruct((width, count * width), LOW)
    return pl.pallas_call(
        functools.partial(feed_gradient_kernel, turns),
        grid=(count,),
        in_specs=specs,
        out_specs=pl.BlockSpec((width, width), lambda step: (0, step)),
        out_shape=out,
        compiler_params=params(),
        cost_estimate=cost(2 * feed.shape[0] * width * width * count, feed, hidden, out),
        name="feed_gradient",
    )(feed, hidden)


def split_owners(core_ref, total, keep_ref, send_ref):
    total = total.reshape(keep_ref.shape[0], 2, keep_ref.shape[1], keep_ref.shape[2])
    total = total.astype(LOW)
    keep = core_ref[0] == 0
    keep_ref[...] = jnp.where(keep, total[:, 0], total[:, 1])
    send_ref[...] = jnp.where(keep, total[:, 1], total[:, 0])


def time_gradient_kernel(core_ref, narrow_ref, wide_ref, keep_ref, send_ref):
    split_owners(core_ref, dot(narrow_ref[...], wide_ref[...], TN), keep_ref, send_ref)


def time_gradient(core, owners, inputs, grads, width):
    count, specs = paired_specs(inputs, grads, width, 3)
    blocks, rows = owners // 4, 2 * (width // owners)
    out = jax.ShapeDtypeStruct((blocks, rows, count * width), LOW)
    out_spec = pl.BlockSpec((blocks, rows, width), lambda step, core: (0, 0, step))
    return pl.pallas_call(
        time_gradient_kernel,
        grid_spec=pltpu.PrefetchScalarGridSpec(
            num_scalar_prefetch=1, grid=(count,), in_specs=specs, out_specs=[out_spec, out_spec]
        ),
        out_shape=[out, out],
        compiler_params=params(),
        cost_estimate=cost(2 * inputs.shape[0] * width * width * count, inputs, grads, out, out),
        name="time_gradient",
    )(core, inputs, grads)


def split_gradient(core, owners, *groups):
    width, count, specs, arrays, parts, tiles, flops = plan_gradient(groups)
    blocks, rows = owners // 4, 2 * (width // owners)
    out = jax.ShapeDtypeStruct((blocks, rows, count * width), LOW)
    out_spec = pl.BlockSpec((blocks, rows, width), lambda step, core: (0, 0, step))
    return pl.pallas_call(
        functools.partial(gradient_kernel, parts, tiles),
        grid_spec=pltpu.PrefetchScalarGridSpec(
            num_scalar_prefetch=1,
            grid=(count,),
            in_specs=specs,
            out_specs=[out_spec, out_spec],
        ),
        out_shape=[out, out],
        compiler_params=params(),
        cost_estimate=cost(flops, *arrays, out, out),
        name="split_gradient",
    )(core, *arrays)


MICRO = 2


def norm_forward(values, gain):
    centred = values - jnp.mean(values, axis=-1, keepdims=True)
    inverse = lax.rsqrt(jnp.mean(centred * centred, axis=-1, keepdims=True) + epsilon)
    normed = centred * inverse
    return (normed * gain, normed, inverse)


def norm_backward(gradient, normed, inverse, gain):
    gain_grad = jnp.sum(gradient * normed, axis=(0, 1, 2))
    scaled = gradient * gain
    centred_grad = (
        scaled
        - jnp.mean(scaled, axis=-1, keepdims=True)
        - normed * jnp.mean(scaled * normed, axis=-1, keepdims=True)
    )
    return (inverse * centred_grad, gain_grad)


def to_places(blocks):
    clip_count, frames, places, model_width = blocks.shape
    return blocks.transpose(0, 2, 1, 3).reshape(clip_count * places, frames, HEADS, HEAD)


def from_places(attended, clip_count, places):
    frames = attended.shape[1]
    return attended.reshape(clip_count, places, frames, HEADS * HEAD).transpose(0, 2, 1, 3)


def attend_forward(queries, key_block, value_block):
    factor = HEAD ** (-0.5)
    scores = (
        jnp.einsum("blhe,bmhe->bhlm", queries, key_block, preferred_element_type=jnp.float32)
        * factor
    )
    highest = jnp.max(scores, axis=-1, keepdims=True)
    powers = jnp.exp(scores - highest)
    row_total = jnp.sum(powers, axis=-1, keepdims=True)
    chances = (powers / row_total).astype(jnp.bfloat16)
    result = jnp.einsum("bhlm,bmhe->blhe", chances, value_block, preferred_element_type=jnp.float32)
    return (result, highest + jnp.log(row_total))


def attend_backward(queries, key_block, value_block, logsum, grad_out):
    factor = HEAD ** (-0.5)
    scores = (
        jnp.einsum("blhe,bmhe->bhlm", queries, key_block, preferred_element_type=jnp.float32)
        * factor
    )
    chances = jnp.exp(scores - logsum)
    grad_chances = jnp.einsum(
        "blhe,bmhe->bhlm", grad_out, value_block, preferred_element_type=jnp.float32
    )
    grad_scores = (
        chances * (grad_chances - jnp.sum(chances * grad_chances, axis=-1, keepdims=True))
    ).astype(jnp.bfloat16)
    grad_queries = (
        jnp.einsum("bhlm,bmhe->blhe", grad_scores, key_block, preferred_element_type=jnp.float32)
        * factor
    )
    grad_keys = (
        jnp.einsum("bhlm,blhe->bmhe", grad_scores, queries, preferred_element_type=jnp.float32)
        * factor
    )
    grad_values = jnp.einsum(
        "bhlm,blhe->bmhe",
        chances.astype(jnp.bfloat16),
        grad_out,
        preferred_element_type=jnp.float32,
    )
    return (grad_queries, grad_keys, grad_values)


def project(values, matrix):
    return jnp.einsum("cfpd,de->cfpe", values, matrix, preferred_element_type=jnp.float32)


def project_back(gradient, matrix):
    return jnp.einsum("cfpe,de->cfpd", gradient, matrix, preferred_element_type=jnp.float32)


def outer_sum(values, gradient):
    return jnp.einsum("cfpd,cfpe->de", values, gradient, preferred_element_type=jnp.float32)


def forward(sample, gathered):
    (
        space_gain,
        time_gain,
        feed_gain,
        space_proj,
        space_out,
        time_proj,
        time_out,
        up_proj,
        down_proj,
    ) = gathered
    clip_count, frames, places, model_width = sample.shape
    normed_space = norm_forward(sample, space_gain.astype(jnp.float32))
    in_space = normed_space[0].astype(jnp.bfloat16)
    qkv_space = project(in_space, space_proj).astype(jnp.bfloat16)
    parted = qkv_space.reshape(clip_count * frames, places, 3, HEADS, HEAD)
    attended, logsum_space = attend_forward(parted[:, :, 0], parted[:, :, 1], parted[:, :, 2])
    out_space = attended.reshape(clip_count, frames, places, model_width).astype(jnp.bfloat16)
    after_space = sample + project(out_space, space_out)
    normed_time = norm_forward(after_space, time_gain.astype(jnp.float32))
    in_time = normed_time[0].astype(jnp.bfloat16)
    qkv_time = project(in_time, time_proj).astype(jnp.bfloat16)
    kv_whole = lax.all_gather(qkv_time[..., model_width:], "frame", axis=1, tiled=True)
    attended, logsum_time = attend_forward(
        to_places(qkv_time[..., :model_width]),
        to_places(kv_whole[..., :model_width]),
        to_places(kv_whole[..., model_width:]),
    )
    out_time = from_places(attended, clip_count, places).astype(jnp.bfloat16)
    after_time = after_space + project(out_time, time_out)
    normed_feed = norm_forward(after_time, feed_gain.astype(jnp.float32))
    in_feed = normed_feed[0].astype(jnp.bfloat16)
    hidden = project(in_feed, up_proj)
    active = jax.nn.gelu(hidden).astype(jnp.bfloat16)
    result = after_time + project(active, down_proj)
    saved = (
        normed_space,
        in_space,
        qkv_space,
        logsum_space,
        out_space,
        normed_time,
        in_time,
        qkv_time,
        kv_whole,
        logsum_time,
        out_time,
        normed_feed,
        in_feed,
        hidden,
        active,
    )
    return (result, saved)


def backward(gradient, saved, gathered):
    (
        space_gain,
        time_gain,
        feed_gain,
        space_proj,
        space_out,
        time_proj,
        time_out,
        up_proj,
        down_proj,
    ) = gathered
    (
        normed_space,
        in_space,
        qkv_space,
        logsum_space,
        out_space,
        normed_time,
        in_time,
        qkv_time,
        time_side,
        logsum_time,
        out_time,
        normed_feed,
        in_feed,
        hidden,
        active,
    ) = saved
    clip_count, frames, places, model_width = gradient.shape
    grad_low = gradient.astype(jnp.bfloat16)
    grad_down = outer_sum(active, grad_low)
    grad_active = project_back(grad_low, down_proj)
    gelu_value, gelu_pull = jax.vjp(jax.nn.gelu, hidden)
    grad_hidden = gelu_pull(grad_active)[0].astype(jnp.bfloat16)
    grad_up = outer_sum(in_feed, grad_hidden)
    back_feed, grad_feed_gain = norm_backward(
        project_back(grad_hidden, up_proj),
        normed_feed[1],
        normed_feed[2],
        feed_gain.astype(jnp.float32),
    )
    grad_time = gradient + back_feed
    time_low = grad_time.astype(jnp.bfloat16)
    grad_tout = outer_sum(out_time, time_low)
    grad_out_time = project_back(time_low, time_out).astype(jnp.bfloat16)
    grad_queries, grad_keys, grad_values = attend_backward(
        to_places(qkv_time[..., :model_width]),
        to_places(time_side[..., :model_width]),
        to_places(time_side[..., model_width:]),
        logsum_time,
        to_places(grad_out_time),
    )
    grad_kv = jnp.concatenate(
        (from_places(grad_keys, clip_count, places), from_places(grad_values, clip_count, places)),
        axis=-1,
    )
    grad_kv_own = lax.psum_scatter(
        grad_kv.astype(jnp.bfloat16), "frame", scatter_dimension=1, tiled=True
    ).astype(jnp.float32)
    grad_qkv_time = jnp.concatenate(
        (from_places(grad_queries, clip_count, places), grad_kv_own), axis=-1
    ).astype(jnp.bfloat16)
    grad_tproj = outer_sum(in_time, grad_qkv_time)
    back_time, grad_time_gain = norm_backward(
        project_back(grad_qkv_time, time_proj),
        normed_time[1],
        normed_time[2],
        time_gain.astype(jnp.float32),
    )
    grad_space = grad_time + back_time
    space_low = grad_space.astype(jnp.bfloat16)
    grad_sout = outer_sum(out_space, space_low)
    grad_out_space = project_back(space_low, space_out).astype(jnp.bfloat16)
    parted = qkv_space.reshape(clip_count * frames, places, 3, HEADS, HEAD)
    grad_queries, grad_keys, grad_values = attend_backward(
        parted[:, :, 0],
        parted[:, :, 1],
        parted[:, :, 2],
        logsum_space,
        grad_out_space.reshape(clip_count * frames, places, HEADS, HEAD),
    )
    grad_qkv_space = (
        jnp.stack((grad_queries, grad_keys, grad_values), axis=2)
        .reshape(clip_count, frames, places, 3 * model_width)
        .astype(jnp.bfloat16)
    )
    grad_sproj = outer_sum(in_space, grad_qkv_space)
    back_space, grad_space_gain = norm_backward(
        project_back(grad_qkv_space, space_proj),
        normed_space[1],
        normed_space[2],
        space_gain.astype(jnp.float32),
    )
    grad_input = grad_space + back_space
    return (
        grad_input,
        (
            grad_space_gain,
            grad_time_gain,
            grad_feed_gain,
            grad_sproj,
            grad_sout,
            grad_tproj,
            grad_tout,
            grad_up,
            grad_down,
        ),
    )


def general(
    tokens,
    cotangent,
    space_gain,
    time_gain,
    feed_gain,
    space_proj,
    space_out,
    time_proj,
    time_out,
    up_proj,
    down_proj,
):
    owned = (
        space_gain,
        time_gain,
        feed_gain,
        space_proj,
        space_out,
        time_proj,
        time_out,
        up_proj,
        down_proj,
    )
    devices_all = lax.axis_size(("clip", "frame"))
    per_micro = tokens.shape[0] // MICRO
    totals = tuple(
        (
            jnp.zeros((piece.shape[0] * devices_all,) + piece.shape[1:], jnp.float32)
            for piece in owned
        )
    )
    gathered = (
        lax.all_gather(space_gain, ("clip", "frame"), axis=0, tiled=True),
        lax.all_gather(time_gain, ("clip", "frame"), axis=0, tiled=True),
        lax.all_gather(feed_gain, ("clip", "frame"), axis=0, tiled=True),
        lax.all_gather(space_proj, ("clip", "frame"), axis=0, tiled=True),
        lax.all_gather(space_out, ("clip", "frame"), axis=0, tiled=True),
        lax.all_gather(time_proj, ("clip", "frame"), axis=0, tiled=True),
        lax.all_gather(time_out, ("clip", "frame"), axis=0, tiled=True),
        lax.all_gather(up_proj, ("clip", "frame"), axis=0, tiled=True),
        lax.all_gather(down_proj, ("clip", "frame"), axis=0, tiled=True),
    )
    mixed_parts = []
    grad_parts = []
    for micro_index in range(MICRO):
        sample = tokens[micro_index * per_micro : (micro_index + 1) * per_micro].astype(jnp.float32)
        result, saved = forward(sample, gathered)
        mixed_parts.append(result.astype(jnp.bfloat16))
        gradient = cotangent[micro_index * per_micro : (micro_index + 1) * per_micro].astype(
            jnp.float32
        )
        grad_input, grads = backward(gradient, saved, gathered)
        grad_parts.append(grad_input)
        totals = tuple((first + second for first, second in zip(totals, grads)))
    flat = tuple((item.reshape(-1) for item in totals))
    owners = (
        lax.psum_scatter(flat[0], ("clip", "frame"), scatter_dimension=0, tiled=True),
        lax.psum_scatter(flat[1], ("clip", "frame"), scatter_dimension=0, tiled=True),
        lax.psum_scatter(flat[2], ("clip", "frame"), scatter_dimension=0, tiled=True),
        lax.psum_scatter(flat[3], ("clip", "frame"), scatter_dimension=0, tiled=True),
        lax.psum_scatter(flat[4], ("clip", "frame"), scatter_dimension=0, tiled=True),
        lax.psum_scatter(flat[5], ("clip", "frame"), scatter_dimension=0, tiled=True),
        lax.psum_scatter(flat[6], ("clip", "frame"), scatter_dimension=0, tiled=True),
        lax.psum_scatter(flat[7], ("clip", "frame"), scatter_dimension=0, tiled=True),
        lax.psum_scatter(flat[8], ("clip", "frame"), scatter_dimension=0, tiled=True),
    )
    shaped = tuple((piece.reshape(mine.shape) for piece, mine in zip(owners, owned)))
    mixed = jnp.concatenate(mixed_parts, axis=0)
    grad_tokens = jnp.concatenate(grad_parts, axis=0)
    return (
        mixed,
        grad_tokens,
        shaped[0],
        shaped[1],
        shaped[2],
        shaped[3],
        shaped[4],
        shaped[5],
        shaped[6],
        shaped[7],
        shaped[8],
    )


def swap_axis(values, axis):
    size = lax.axis_size(axis)
    return lax.ppermute(values, axis, [(index, size - 1 - index) for index in range(size)])


def flip(values, mask):
    size = lax.axis_size("clip")
    return lax.ppermute(values, "clip", [(index, index ^ mask) for index in range(size)])


def tie(*items):
    return lax.optimization_barrier(items)


def bit_of(mask):
    return (lax.axis_index("clip") // mask) % 2


def in_order(bit, mine, other, axis):
    return jnp.where(
        bit == 0, jnp.stack([mine, other], axis=axis), jnp.stack([other, mine], axis=axis)
    )


def pick(values, index, axis):
    return lax.dynamic_index_in_dim(values, index, axis, keepdims=False)


def added(*items):
    return sum(item.astype(WIDE) for item in items)


def collect_start(shard):
    return in_order(lax.axis_index("frame"), shard, swap_axis(shard, "frame"), 0)


def collect_lines(item):
    line = lax.axis_index("clip") // 4
    parts = [item] + [flip(item, 4 * step) for step in range(1, 4)]
    odd, far = line % 2, line // 2
    parts = [jnp.where(odd == 0, parts[index], parts[index ^ 1]) for index in range(4)]
    parts = [jnp.where(far == 0, parts[index], parts[index ^ 2]) for index in range(4)]
    return jnp.stack(parts, axis=0)


def collect_half(item, mask, axis):
    return in_order(bit_of(mask), item, flip(item, mask), axis)


def merged(item):
    return item.reshape(-1, item.shape[-1])


def scatter_core(keep, send):
    return keep, flip(send, 1)


def column_parts(keep, other):
    shape = (4, 2) + keep.shape[1:]
    keep, other = keep.reshape(shape), other.reshape(shape)
    bit = bit_of(2)
    send = added(pick(keep, 1 - bit, 1), pick(other, 1 - bit, 1)).astype(LOW)
    return added(pick(keep, bit, 1), pick(other, bit, 1)).astype(LOW), send


def scatter_columns(keep, other):
    keep, send = column_parts(keep, other)
    return keep, flip(send, 2)


def scatter_lines(keep, other):
    line = lax.axis_index("clip") // 4
    total = added(keep, other).astype(LOW)
    parts = [flip(pick(total, line ^ step, 0), 4 * step) for step in range(1, 4)]
    return (pick(total, line, 0), *parts)


def scatter_frames(*parts):
    total = added(*parts).astype(LOW)
    total = total.reshape(2, total.shape[0] // 2, total.shape[1])
    place = lax.axis_index("frame")
    return pick(total, place, 0), swap_axis(pick(total, 1 - place, 0), "frame")


def flat_rows(values):
    return values.reshape(-1, values.shape[-1])


def clip_local(
    tokens,
    cotangent,
    space_gain,
    time_gain,
    feed_gain,
    space_proj,
    space_out,
    time_proj,
    time_out,
    up_proj,
    down_proj,
):
    axes = ("clip", "frame")
    place = lax.axis_index("frame")
    owners = lax.axis_size(axes)
    share, width = space_out.shape
    blocks = down_proj.shape[0] // share
    core = bit_of(1).reshape(1)
    spot = place.reshape(1)

    gains = jnp.stack([space_gain, time_gain, feed_gain], axis=1)
    gains = jnp.pad(gains, ((0, 0), (0, LANES - 3)))
    first = collect_start(space_proj[:, : 2 * width])
    second = collect_start(
        jnp.concatenate([space_proj[:, 2 * width :], space_out, gains], axis=1)
    )
    up_order = up_proj.reshape(share, owners, blocks, share).transpose(0, 2, 1, 3)
    down_order = down_proj.reshape(blocks, share, width).transpose(1, 0, 2)
    packed = jnp.concatenate(
        [time_proj, time_out, up_order.reshape(share, -1), down_order.reshape(share, -1)], axis=1
    )
    first, second, by_place, g_place, tokens, packed = tie(
        first, second, tokens.transpose(0, 2, 1, 3), cotangent.transpose(0, 2, 1, 3), tokens, packed
    )
    packed = lax.all_gather(packed, axes, axis=0, tiled=True)
    half = by_place.shape[1] * 2 // 5
    send = pick(by_place, 1 - place, 0)
    rest_a = swap_axis(send[:half], "frame")
    first = collect_lines(first)
    own, g_own, g_send = (
        pick(tokens, place, 0), pick(g_place, place, 0), pick(g_place, 1 - place, 0)
    )
    second, first, rest_a, send, own, g_own, g_send = tie(
        second, first, rest_a, send, own, g_own, g_send
    )
    rest_b = swap_axis(send[half:], "frame")
    second = collect_lines(second)
    first = collect_half(first, 2, 1)
    first, second = tie(first, second)
    second = collect_half(second, 2, 1)
    second, rest_b, g_send = tie(second, rest_b, g_send)
    g_rest = swap_axis(g_send, "frame")
    first = merged(collect_half(first, 1, 2))
    second = merged(collect_half(second, 1, 2))
    rest = jnp.concatenate([rest_a, rest_b], axis=0).transpose(1, 0, 2)
    table = second[:, 2 * width : 2 * width + 3].astype(WIDE).T
    sgain, tgain, fgain = (table[index : index + 1] for index in range(3))
    in_o, qkv_o, o_o, after_o = space_forward(own, sgain, first, second)
    rest, after_o = tie(rest, after_o)
    in_r, qkv_r, o_r, after_r = space_forward(rest, sgain, first, second)
    g_rest, after_r = tie(g_rest, after_r)
    qkv_t, time_in, feed_in, hidden, mixed, mixed_r, g_time, gain_f = middle(
        spot, after_o, after_r, g_own, g_rest, tgain, fgain, packed
    )
    mixed_other = swap_axis(mixed_r, "frame")
    scatter = lambda item: lax.psum_scatter(item, axes, scatter_dimension=0, tiled=True)
    d_feed = feed_gradient(feed_in, hidden, width)
    d_feed, g_time = tie(d_feed, g_time)
    d_feed = scatter(d_feed)
    grads_t, gs_o, gs_r, gain_t = time_backward(
        qkv_t, g_time, after_o, after_r, tgain, packed
    )
    d_time = time_gradient(core, owners, time_in, grads_t, width)
    d_time, gs_r, mixed_other = tie(d_time, gs_r, mixed_other)
    d_time = scatter_columns(*scatter_core(*d_time))
    gq_r, sb_r, gx_r, gain_sr = space_backward(spot, rest, gs_r, qkv_r, sgain, first, second, LOW)
    grad_a = swap_axis(gx_r[:half], "frame")
    grad_b = swap_axis(gx_r[half:], "frame")
    d_time, gs_o, sb_r = tie(d_time, gs_o, sb_r)
    d_time = scatter_lines(*d_time)
    gq_o, sb_o, grad_tokens, gain_so = space_backward(spot, own, gs_o, qkv_o, sgain, first, second, WIDE)
    d_time, gq_o, sb_o, grad_a = tie(d_time, gq_o, sb_o, grad_a)
    gain_grads = jnp.stack(
        [jnp.sum(item, axis=0) for item in (gain_so + gain_sr, gain_t, gain_f)], axis=1
    )
    gain_grads = jnp.pad(gain_grads, ((0, 0), (0, LANES - 3))).astype(LOW)
    gain_grads = gain_grads.reshape(owners // 4, 2, 2 * share, LANES)
    gain_grads = [pick(gain_grads, side, 1) for side in (core[0], 1 - core[0])]
    inputs = [(flat_rows(in_o), flat_rows(gq_o)), (flat_rows(in_r), flat_rows(gq_r))]
    d_first = scatter_core(*split_gradient(core, owners, (inputs, 0, 3, 1, 0)))
    first_keep, first_send = column_parts(*d_first)
    first_keep, first_send, o_o = tie(first_keep, first_send, o_o)
    d_first = first_keep, flip(first_send, 2)
    outputs = [(flat_rows(o_o), flat_rows(sb_o)), (flat_rows(o_r), flat_rows(sb_r))]
    d_second = split_gradient(core, owners, (outputs, 0, 1, 1, 0))
    d_second = [
        jnp.concatenate([item, gain], axis=2) for item, gain in zip(d_second, gain_grads)
    ]
    d_second = scatter_core(*d_second)
    d_first, d_second, d_time, mixed_other, grad_a, grad_b, d_feed = tie(
        d_first, d_second, d_time, mixed_other, grad_a, grad_b, d_feed
    )
    d_first = scatter_lines(*d_first)
    d_second = scatter_columns(*d_second)
    d_time = scatter_frames(*d_time)
    d_feed = d_feed.astype(WIDE)
    d_up, d_down = d_feed[:, : blocks * width], d_feed[:, blocks * width :]
    d_up = d_up.reshape(share, blocks, owners, share).transpose(0, 2, 1, 3)
    d_up = d_up.reshape(up_proj.shape)
    d_down = d_down.reshape(share, blocks, width).transpose(1, 0, 2).reshape(down_proj.shape)
    mixed = lax.dynamic_update_index_in_dim(mixed, mixed_other, 1 - place, 0)
    for start, item in ((0, grad_a), (half, grad_b)):
        grad_tokens = lax.dynamic_update_slice(
            grad_tokens, item.astype(WIDE)[None], (1 - place, start, 0, 0)
        )
    d_first, mixed, grad_tokens, d_up, d_down = tie(d_first, mixed, grad_tokens, d_up, d_down)
    d_first = scatter_frames(*d_first)
    d_second = scatter_frames(*scatter_lines(*d_second))
    d_first, d_second, d_time = (added(*item) for item in (d_first, d_second, d_time))
    mixed, grad_tokens = mixed.transpose(0, 2, 1, 3), grad_tokens.transpose(0, 2, 1, 3)
    return (
        mixed,
        grad_tokens,
        d_second[:, width],
        d_second[:, width + 1],
        d_second[:, width + 2],
        d_first,
        d_second[:, :width],
        d_time[:, : 3 * width],
        d_time[:, 3 * width :],
        d_up,
        d_down,
    )


def shards(tokens, *others):
    frames = lax.axis_size("frame")
    local = frames == 2 and tokens.shape[0] == 2 and tokens.shape[1] == GROUP
    return (clip_local if local else general)(tokens, *others)


def solution(mesh):
    in_specs = (
        P("clip", "frame", None, None),
        P("clip", "frame", None, None),
        P(("clip", "frame")),
        P(("clip", "frame")),
        P(("clip", "frame")),
        P(("clip", "frame"), None),
        P(("clip", "frame"), None),
        P(("clip", "frame"), None),
        P(("clip", "frame"), None),
        P(("clip", "frame"), None),
        P(("clip", "frame"), None),
    )
    out_specs = (
        P("clip", "frame", None, None),
        P("clip", "frame", None, None),
        P(("clip", "frame")),
        P(("clip", "frame")),
        P(("clip", "frame")),
        P(("clip", "frame"), None),
        P(("clip", "frame"), None),
        P(("clip", "frame"), None),
        P(("clip", "frame"), None),
        P(("clip", "frame"), None),
        P(("clip", "frame"), None),
    )
    return jax.shard_map(shards, mesh=mesh, in_specs=in_specs, out_specs=out_specs, check_vma=False)
```
